32 devices in a mesh: dp: 8 (over z, y), fsdp: 4 (over x, core).
Axes of the slice: x: 2, y: 2, z: 4, core: 2. Of those that a mesh axis runs over, the one named last changes fastest.
Arguments:
- tokens: bfloat16 [4096, 2048], P(('dp', 'fsdp')), may hold values from -6 to 6
- lengths: int32 [8], replicated, may hold values from 64 to 512, as said below
- gain_attn: bfloat16 [2048], P(('dp', 'fsdp')), may hold values from 0.099609375 to 1.8984375
- w_qkv: bfloat16 [2048, 2304], P(('dp', 'fsdp')), may hold values from -0.125 to 0.125
- w_out: bfloat16 [2048, 2048], P(('dp', 'fsdp')), may hold values from -2 to 2
- gain_ffn: bfloat16 [2048], P(('dp', 'fsdp')), may hold values from 0.099609375 to 1.8984375
- w_gateup: bfloat16 [2048, 11264], P(('dp', 'fsdp')), may hold values from -0.125 to 0.125
- w_down: bfloat16 [2048, 5632], P(('dp', 'fsdp')), may hold values from -0.21875 to 0.21875
- out_grad: bfloat16 [4096, 2048], P(('dp', 'fsdp')), may hold values from -6 to 6
- kv_grad: bfloat16 [4096, 256], P(('dp', 'fsdp')), may hold values from -6 to 6
Outputs:
- mixed: bfloat16 [4096, 2048], P(('dp', 'fsdp'))
- shared_kv: bfloat16 [4096, 256], P(('dp', 'fsdp'))
- input_grad: bfloat16 [4096, 2048], P(('dp', 'fsdp'))
- grad_gain_attn: float32 [2048], P(('dp', 'fsdp'))
- grad_qkv: float32 [2048, 2304], P(('dp', 'fsdp'))
- grad_out: float32 [2048, 2048], P(('dp', 'fsdp'))
- grad_gain_ffn: float32 [2048], P(('dp', 'fsdp'))
- grad_gateup: float32 [2048, 11264], P(('dp', 'fsdp'))
- grad_down: float32 [2048, 5632], P(('dp', 'fsdp'))
The draws below stay inside these ranges and needn't reach their ends.
Inputs may be any that keep to these rules, and one draw needn't show every extreme that they name: lengths[g] is the number of valid tokens of sequence g; its other slots of 512 are padding; some sequence has exactly 512.
All inputs are finite; a program needn't handle non-finite values.
Results may differ from the reference program's by a relative error of at most 0.025.
Values may be sent and summed in bfloat16 or wider, within the bound.
A program may use at most 576 MiB of HBM per device.

```python
import jax
import jax.numpy as jnp
from jax import lax

D = 2048
HEADS = 16
HEAD_DIM = 128
FF = 5632
TOK_DEV = 128
MIN_LEN = 64
HQ = 2048
SLOT = 512
GROUPS = 8
TOKENS = 4096
N_DP = 8
N_FSDP = 4


def draw_lengths(key, part):
    key = jax.random.fold_in(key, 11)
    spread_key, full_key = jax.random.split(key)
    ranking = jax.random.randint(spread_key, (GROUPS,), 0, 64)
    lengths = MIN_LEN + (SLOT - MIN_LEN) * (ranking * ranking + 63 * ranking) // 7938
    chosen = jax.random.randint(full_key, (), 0, GROUPS)
    return jnp.where(jnp.arange(GROUPS) == chosen, SLOT, lengths).astype(jnp.int32)


def steps_of(rng, shape, pieces, least, largest):
    loudness = 1.0
    for position, blocks in pieces:
        steps = jax.random.uniform(jax.random.fold_in(jax.random.fold_in(rng, 6), position), (blocks,), jnp.float32, least / len(pieces), largest / len(pieces))
        loudness = loudness * jnp.repeat(jnp.exp(steps), shape[position] // blocks).reshape((-1,) + (1,) * (len(shape) - 1 - position))
    return loudness


def bell_draw(rng, dims, width, reach, cuts=(), kind=jnp.bfloat16):
    array = width * jax.random.normal(rng, dims, jnp.float32)
    if cuts:
        array = array * steps_of(rng, dims, cuts, -0.22, 0.18)
    return jnp.clip(array, -reach, reach).astype(kind)


def setup_inputs(seed: int = 0) -> dict:
    keys = jax.random.split(jax.random.key(seed), 11)
    return {
        "tokens": bell_draw(keys[0], (TOKENS, D), 1.0, 6.0, ((0, 32),)),
        "lengths": draw_lengths(jax.random.fold_in(keys[10], 71), 0),
        "gain_attn": jnp.clip(1.0 + 0.18 * jax.random.normal(keys[2], (D,), jnp.float32), 0.099609375, 1.8984375).astype(jnp.bfloat16),
        "w_qkv": bell_draw(keys[3], (D, HQ + 2 * HEAD_DIM), D ** -0.5, 0.125, ((0, 32),)),
        "w_out": bell_draw(keys[4], (D, HQ), (max(HQ // 256, 1)) ** -0.5, 2.0, ((0, 32),)),
        "gain_ffn": jnp.clip(1.0 + 0.18 * jax.random.normal(keys[5], (D,), jnp.float32), 0.099609375, 1.8984375).astype(jnp.bfloat16),
        "w_gateup": bell_draw(keys[6], (D, 2 * FF), D ** -0.5, 0.125, ((0, 32),)),
        "w_down": bell_draw(keys[7], (D, FF), (max(FF // 8, 1)) ** -0.5, 0.21875, ((0, 32),)),
        "out_grad": bell_draw(keys[8], (TOKENS, D), 1.0, 6.0, ((0, 32),)),
        "kv_grad": bell_draw(keys[9], (TOKENS, 2 * HEAD_DIM), 1.0, 6.0, ((0, 32),)),
    }


@jax.custom_vjp
def low(v):
    return lax.optimization_barrier(v.astype(jnp.bfloat16)).astype(jnp.float32)

@jax.custom_vjp
def low_back(v):
    return v

def low_keep(v):
    return (low(v), None)

def low_pass(kept, grad):
    return (grad,)

def back_keep(v):
    return (v, None)

def back_low(kept, grad):
    return (low(grad),)
low.defvjp(low_keep, low_pass)
low_back.defvjp(back_keep, back_low)
EPSILON = 1e-05
THETA = 10000.0
MASKED = -1e+30

def product(left, right):
    return jnp.dot(left, right, precision=lax.Precision.HIGHEST, preferred_element_type=jnp.float32)

def rms_scaled(values):
    return values * lax.rsqrt(lax.optimization_barrier(jnp.mean(values * values, axis=-1, keepdims=True)) + EPSILON)

def rotate(values, cosine, sine_part):
    half_dim = values.shape[-1] // 2
    first_half = values[..., :half_dim]
    second_half = values[..., half_dim:]
    return jnp.concatenate([first_half * cosine - second_half * sine_part, second_half * cosine + first_half * sine_part], axis=-1)

def slot_positions():
    indices = jnp.arange(SLOT, dtype=jnp.int32)
    return indices % TOK_DEV * N_FSDP + indices // TOK_DEV

@jax.checkpoint
def attend_group(queries, key_rows, values, length):
    positions = slot_positions()
    allowed = (positions[None, :] <= positions[:, None]) & (positions[None, :] < length)
    head_rows = queries.reshape(SLOT, HEADS, HEAD_DIM)
    scores = jnp.einsum('qhd,kd->hqk', head_rows, key_rows, precision=lax.Precision.HIGHEST) * HEAD_DIM ** (-0.5)
    scores = low_back(scores)
    scores = jnp.where(allowed[None], scores, MASKED)
    weights = jax.nn.softmax(scores, axis=-1)
    mixture = jnp.einsum('hqk,kd->qhd', low(weights), values, precision=lax.Precision.HIGHEST)
    return mixture.reshape(SLOT, HQ)

def layer_forward(tokens, gain_attn, w_qkv, w_out, gain_ffn, w_gateup, w_down, lengths):
    normed = low(rms_scaled(tokens) * gain_attn)
    projected = low_back(product(normed, w_qkv))
    grouped = projected.reshape(N_DP, SLOT, HQ + 2 * HEAD_DIM)
    frequency = THETA ** (-jnp.arange(HEAD_DIM // 2, dtype=jnp.float32) * (2.0 / HEAD_DIM))
    angles = slot_positions().astype(jnp.float32)[:, None] * frequency[None, :]
    cosine = jnp.cos(angles)
    sine_part = jnp.sin(angles)
    queries = grouped[..., :HQ].reshape(N_DP, SLOT, HEADS, HEAD_DIM)
    queries = low(rotate(queries, cosine[:, None, :], sine_part[:, None, :])).reshape(N_DP, SLOT, HQ)
    key_rows = low(rotate(grouped[..., HQ:HQ + HEAD_DIM], cosine, sine_part))
    values = low(grouped[..., HQ + HEAD_DIM:])
    attended = lax.map(lambda member: attend_group(*member), (queries, key_rows, values, lengths))
    attended = low(low_back(attended.reshape(N_DP * SLOT, HQ)))
    middle = tokens + low_back(product(attended, w_out.T))
    normed_ffn = low(rms_scaled(middle) * gain_ffn)
    gateup = low_back(product(normed_ffn, w_gateup))
    hidden = low(jax.nn.silu(gateup[:, :FF]) * gateup[:, FF:])
    result = middle + low_back(product(hidden, w_down.T))
    shared = jnp.concatenate([key_rows, values], axis=-1).reshape(N_DP * SLOT, 2 * HEAD_DIM)
    return (result, shared)

def reference(tokens, lengths, gain_attn, w_qkv, w_out, gain_ffn, w_gateup, w_down, out_grad, kv_grad):
    params = tuple((argument.astype(jnp.float32) for argument in (tokens, gain_attn, w_qkv, w_out, gain_ffn, w_gateup, w_down)))

    def forward(*inputs):
        return layer_forward(*inputs, lengths)
    (result, shared), pullback = jax.vjp(forward, *params)
    gradients = pullback((out_grad.astype(jnp.float32), kv_grad.astype(jnp.float32)))
    return (result.astype(jnp.bfloat16), shared.astype(jnp.bfloat16), gradients[0].astype(jnp.bfloat16), gradients[1], gradients[2], gradients[3], gradients[4], gradients[5], gradients[6])
```

```python
import functools

import jax
import jax.numpy as jnp
from jax import lax
from jax.experimental import pallas as pl
from jax.experimental.pallas import tpu as pltpu
from jax.sharding import PartitionSpec as P

HEADS = 16
HEAD_DIM = 128
FF = 5632
HQ = 2048
MODEL = 2048
KV = 2 * HEAD_DIM
LANES = 128

EPSILON = 1e-05
THETA = 10000.0
MASKED = -1e30
MESH = pl.DeviceIdType.MESH
ANY = pl.ANY


class Place:
    def __init__(self, dp_count, fsdp_count):
        self.fsdp = fsdp_count
        self.xs = fsdp_count // 2
        self.ys = self.xs
        self.zs = dp_count // self.ys
        self.rows = MODEL // (dp_count * fsdp_count)
        self.heads = HQ // fsdp_count
        self.attn_width = 2 * self.heads + KV
        self.zone = FF // self.zs
        self.block = LANES * -(-(self.zone // LANES) // 2)
        self.ffn_width = 3 * self.block


class Here:
    def __init__(self, place):
        self.place = place
        self.dp = lax.axis_index("dp")
        self.fs = lax.axis_index("fsdp")
        self.z = self.dp // place.ys
        self.y = lax.rem(self.dp, place.ys)
        self.x = self.fs // 2
        self.c = lax.rem(self.fs, 2)

    def device(self, z=None, y=None, x=None, c=None):
        z = self.z if z is None else z
        y = self.y if y is None else y
        x = self.x if x is None else x
        c = self.c if c is None else c
        return (z * self.place.ys + y, x * 2 + c)

    def sibling(self):
        return self.device(c=1 - self.c)


def shifted(value, step, count):
    return lax.rem(value + (step + count), count)


def rows_at(start, count):
    return pl.ds(pl.multiple_of(start, count), count)


def cols_at(start, count):
    return pl.ds(pl.multiple_of(start, LANES), count)


class Wires:
    def __init__(self, send, recv):
        self.send = send
        self.recv = recv
        self.used = 0
        self.finish = []

    def slot(self):
        self.used += 1
        return self.used - 1

    def copy(self, slot, source, target, device):
        return pltpu.make_async_remote_copy(
            src_ref=source,
            dst_ref=target,
            send_sem=self.send.at[slot],
            recv_sem=self.recv.at[slot],
            device_id=device,
            device_id_type=MESH,
        )

    def start(self, slot, source, target, device, when=None):
        copy = self.copy(slot, source, target, device)
        if when is None:
            copy.start()
            self.finish.append(copy.wait_send)
        else:
            pl.when(when)(copy.start)
            self.finish.append(lambda: pl.when(when)(copy.wait_send))

    def arrive(self, slot, target, device, when=None):
        copy = self.copy(slot, target, target, device)
        if when is None:
            copy.wait_recv()
        else:
            pl.when(when)(copy.wait_recv)

    def drain(self):
        for wait in self.finish:
            wait()


def greet(devices):
    barrier = pltpu.get_barrier_semaphore()
    for device in devices:
        pl.semaphore_signal(barrier, inc=1, device_id=device, device_id_type=MESH)
    pl.semaphore_wait(barrier, len(devices))


def line_partners(here):
    place = here.place
    return [here.device(z=shifted(here.z, step, place.zs)) for step in range(1, place.zs)]


def plane_partners(here):
    place = here.place
    return [here.device(y=shifted(here.y, step, place.ys)) for step in range(1, place.ys)] + [
        here.device(x=shifted(here.x, step, place.xs)) for step in range(1, place.xs)
    ]


class Line:
    def __init__(self, wires, here, view):
        self.wires = wires
        self.here = here
        self.view = view
        count = here.place.zs
        self.count = count
        self.up = [wires.slot() for step in range(count - 1)]
        self.down = [wires.slot() for step in range(count - 1)]

    def send(self, step):
        here, count = self.here, self.count
        if step >= count - 1:
            return
        z = here.z
        low = lax.max(z - step, 0)
        high = lax.min(z + step, count - 1)
        self.wires.start(
            self.up[step],
            self.view(low),
            self.view(low),
            here.device(z=lax.min(z + 1, count - 1)),
            when=(z >= step) & (z < count - 1),
        )
        self.wires.start(
            self.down[step],
            self.view(high),
            self.view(high),
            here.device(z=lax.max(z - 1, 0)),
            when=(z + step < count) & (z > 0),
        )

    def arrive(self, step):
        here, count = self.here, self.count
        z = here.z
        low = lax.max(z - step, 0)
        high = lax.min(z + step, count - 1)
        self.wires.arrive(
            self.up[step - 1], self.view(low), here.device(z=lax.max(z - 1, 0)), when=z >= step
        )
        self.wires.arrive(
            self.down[step - 1],
            self.view(high),
            here.device(z=lax.min(z + 1, count - 1)),
            when=z + step < count,
        )

    def valid(self, step):
        z = self.here.z
        if step == 0:
            return [(z, None)]
        return [
            (lax.max(z - step, 0), z >= step),
            (lax.min(z + step, self.count - 1), z + step < self.count),
        ]


def gather_kernel(
    place, w_qkv, w_out, w_gateup, w_down, tokens, dy, wa, wf, tok_all, dy_all, local, send, recv
):
    here = Here(place)
    wires = Wires(send, recv)
    z, y, x, c = here.z, here.y, here.x, here.c
    rows, heads, block, zone = place.rows, place.heads, place.block, place.zone
    toks = tokens.shape[0]
    partners = line_partners(here) + plane_partners(here)
    partners += [
        here.device(x=shifted(x, step, place.xs), c=1 - c) for step in range(place.xs)
    ]
    partners += [
        here.device(z=shifted(z, step, place.zs), c=1 - c) for step in range(1, place.zs)
    ]
    greet(partners)

    def index(z=z, y=y, x=x, c=c):
        return (z * place.ys + y) * place.fsdp + x * 2 + c

    locals_ = []

    def keep(source, target):
        copy = pltpu.make_async_copy(source, target, local.at[len(locals_)])
        copy.start()
        locals_.append(copy)

    def attn_pieces(owner):
        return [
            (w_qkv, owner * heads, heads, 0),
            (w_qkv, HQ, KV, heads),
            (w_out, owner * heads, heads, heads + KV),
        ]

    def ffn_pieces(zone_z, core):
        start = zone_z * zone + core * (zone - block)
        return [(w_gateup, start, 0), (w_gateup, FF + start, block), (w_down, start, 2 * block)]

    own_rows = rows_at(index() * rows, rows)

    attn_slots = []
    for step in range(1, place.fsdp):
        other = shifted(here.fs, step, place.fsdp)
        for ref, start, width, place_at in attn_pieces(other):
            slot = wires.slot()
            attn_slots.append((slot, step, width, place_at))
            wires.start(
                slot,
                ref.at[:, cols_at(start, width)],
                wa.at[own_rows, pl.ds(place_at, width)],
                (here.dp, other),
            )
    for ref, start, width, place_at in attn_pieces(here.fs):
        keep(ref.at[:, cols_at(start, width)], wa.at[own_rows, pl.ds(place_at, width)])

    def tok_view(x_at, c_at):
        return tok_all.at[rows_at((x_at * 2 + c_at) * toks, toks)]

    keep(tokens, tok_view(x, c))
    tok_slots = []
    for step in range(1, place.xs):
        slot = wires.slot()
        tok_slots.append(slot)
        wires.start(slot, tokens, tok_view(x, c), here.device(x=shifted(x, step, place.xs)))
    tok_core = [wires.slot() for step in range(place.xs)]
    wires.start(tok_core[0], tokens, tok_view(x, c), here.sibling())

    ffn_slots = {}
    for step in range(place.zs):
        for core in range(2):
            if step == 0 and core == 0:
                continue
            to_z, to_c = shifted(z, step, place.zs), lax.rem(c + core, 2)
            for ref, start, place_at in ffn_pieces(to_z, to_c):
                slot = wires.slot()
                ffn_slots.setdefault(step, []).append((slot, core, place_at))
                wires.start(
                    slot,
                    ref.at[:, cols_at(start, block)],
                    wf.at[own_rows, pl.ds(place_at, block)],
                    here.device(z=to_z, c=to_c),
                )
    for ref, start, place_at in ffn_pieces(z, c):
        keep(ref.at[:, cols_at(start, block)], wf.at[own_rows, pl.ds(place_at, block)])

    def dy_view(z_at, c_at):
        return dy_all.at[rows_at((z_at * 2 + c_at) * toks, toks)]

    keep(dy, dy_view(z, c))
    for copy in locals_:
        copy.wait()

    for slot, step, width, place_at in attn_slots:
        other = shifted(here.fs, -step, place.fsdp)
        at_rows = rows_at((here.dp * place.fsdp + other) * rows, rows)
        wires.arrive(slot, wa.at[at_rows, pl.ds(place_at, width)], (here.dp, other))

    def wa_view(z_at, y_at):
        count = place.fsdp * rows
        return wa.at[rows_at((z_at * place.ys + y_at) * count, count)]

    attn_line = Line(wires, here, lambda z_at: wa_view(z_at, y))
    attn_line.send(0)
    attn_plane = {}

    def attn_across(step):
        for side, (z_at, exists) in enumerate(attn_line.valid(step)):
            for hop in range(1, place.ys):
                slot = wires.slot()
                attn_plane[step, side, hop] = slot
                view = wa_view(z_at, y)
                wires.start(
                    slot, view, view, here.device(y=shifted(y, hop, place.ys)), when=exists
                )

    def attn_crossed(step):
        for side, (z_at, exists) in enumerate(attn_line.valid(step)):
            for hop in range(1, place.ys):
                from_y = shifted(y, -hop, place.ys)
                wires.arrive(
                    attn_plane[step, side, hop],
                    wa_view(z_at, from_y),
                    here.device(y=from_y),
                    when=exists,
                )

    attn_across(0)

    dy_line = Line(wires, here, lambda z_at: dy_view(z_at, c))
    dy_core = {}

    def dy_across(step):
        for side, (z_at, exists) in enumerate(dy_line.valid(step)):
            slot = wires.slot()
            dy_core[step, side] = slot
            view = dy_view(z_at, c)
            wires.start(slot, view, view, here.sibling(), when=exists)

    def dy_crossed(step):
        for side, (z_at, exists) in enumerate(dy_line.valid(step)):
            wires.arrive(dy_core[step, side], dy_view(z_at, 1 - c), here.sibling(), when=exists)

    def wf_view(z_at, y_at, x_at):
        return wf.at[rows_at(index(z_at, y_at, x_at, 0) * rows, 2 * rows)]

    plane_y, plane_x = {}, {}

    def ffn_arrive(step):
        from_z = shifted(z, -step, place.zs)
        for slot, core, place_at in ffn_slots[step]:
            from_c = lax.rem(c + core, 2)
            at_rows = rows_at(index(z=from_z, c=from_c) * rows, rows)
            wires.arrive(
                slot, wf.at[at_rows, pl.ds(place_at, block)], here.device(z=from_z, c=from_c)
            )

    def ffn_send_y(step):
        z_at = shifted(z, -step, place.zs)
        for hop in range(1, place.ys):
            slot = wires.slot()
            plane_y[step, hop] = slot
            view = wf_view(z_at, y, x)
            wires.start(slot, view, view, here.device(y=shifted(y, hop, place.ys)))

    def ffn_send_x(step, hop_y):
        z_at = shifted(z, -step, place.zs)
        y_at = shifted(y, -hop_y, place.ys)
        if hop_y:
            wires.arrive(plane_y[step, hop_y], wf_view(z_at, y_at, x), here.device(y=y_at))
        for hop in range(1, place.xs):
            slot = wires.slot()
            plane_x[step, hop_y, hop] = slot
            view = wf_view(z_at, y_at, x)
            wires.start(slot, view, view, here.device(x=shifted(x, hop, place.xs)))

    def ffn_arrive_x(step, hop_y):
        z_at = shifted(z, -step, place.zs)
        y_at = shifted(y, -hop_y, place.ys)
        for hop in range(1, place.xs):
            from_x = shifted(x, -hop, place.xs)
            wires.arrive(
                plane_x[step, hop_y, hop], wf_view(z_at, y_at, from_x), here.device(x=from_x)
            )

    def tok_arrive():
        for step, slot in zip(range(1, place.xs), tok_slots):
            from_x = shifted(x, -step, place.xs)
            wires.arrive(slot, tok_view(from_x, c), here.device(x=from_x))
            view = tok_view(from_x, c)
            wires.start(tok_core[step], view, view, here.sibling())

    for step in range(place.zs):
        ffn_arrive(step)
        ffn_send_y(step)
        ffn_send_x(step, 0)
        if step == 0:
            tok_arrive()
            dy_line.send(0)
            dy_across(0)
        else:
            attn_line.arrive(step)
            attn_line.send(step)
            attn_across(step)
            for hop_y in range(1, place.ys):
                ffn_send_x(step - 1, hop_y)
    for hop_y in range(1, place.ys):
        ffn_send_x(place.zs - 1, hop_y)
    for step in range(1, place.zs):
        dy_line.arrive(step)
        dy_line.send(step)
        dy_across(step)
    for step in range(place.zs):
        attn_crossed(step)
        dy_crossed(step)
    for step in range(place.xs):
        from_x = shifted(x, -step, place.xs)
        wires.arrive(tok_core[step], tok_view(from_x, 1 - c), here.sibling())
    for step in range(place.zs):
        for hop_y in range(place.ys):
            ffn_arrive_x(step, hop_y)
    wires.drain()


def gather(place, w_qkv, w_out, w_gateup, w_down, tokens, dy):
    toks = tokens.shape[0]
    count = 512
    return pl.pallas_call(
        functools.partial(gather_kernel, place),
        out_shape=(
            jax.ShapeDtypeStruct((MODEL, place.attn_width), jnp.bfloat16),
            jax.ShapeDtypeStruct((MODEL, place.ffn_width), jnp.bfloat16),
            jax.ShapeDtypeStruct((place.fsdp * toks, MODEL), jnp.bfloat16),
            jax.ShapeDtypeStruct((place.zs * 2 * toks, MODEL), jnp.bfloat16),
        ),
        in_specs=[pl.BlockSpec(memory_space=ANY)] * 6,
        out_specs=(pl.BlockSpec(memory_space=ANY),) * 4,
        scratch_shapes=[
            pltpu.SemaphoreType.DMA((8,)),
            pltpu.SemaphoreType.DMA((count,)),
            pltpu.SemaphoreType.DMA((count,)),
        ],
        compiler_params=pltpu.CompilerParams(collective_id=0, has_side_effects=True),
        name="gather_weights",
    )(w_qkv, w_out, w_gateup, w_down, tokens, dy)


def each_rows(count, body, size=16):
    def step(index, carry):
        body(pl.ds(pl.multiple_of(index * size, size), size), index * size)
        return carry

    lax.fori_loop(0, count // size, step, 0)


def dot_nn(left, right):
    return lax.dot_general(
        left, right, (((1,), (0,)), ((), ())), preferred_element_type=jnp.float32
    )


def dot_nt(left, right):
    return lax.dot_general(
        left, right, (((1,), (1,)), ((), ())), preferred_element_type=jnp.float32
    )


def dot_tn(left, right):
    return lax.dot_general(
        left, right, (((0,), (0,)), ((), ())), preferred_element_type=jnp.float32
    )


def visit_order(count):
    orders = []
    for z in range(count):
        far = sorted(range(count), key=lambda other: (abs(other - z), other))
        orders.append(far)
    return orders


def chosen(z, turn, orders):
    total = 0
    for z_at, order in enumerate(orders):
        here = jnp.where(z == z_at, 1, 0)
        for turn_at, value in enumerate(order):
            if isinstance(turn, int):
                if turn == turn_at:
                    total = total + here * value
            else:
                total = total + here * jnp.where(turn == turn_at, 1, 0) * value
    return total


def ffn_kernel(
    place, part, tokens, dy, dy_all, wf,
    mixed, dmid, dbr_all, gf,
    w_v, s2_v, dy_v, hid_v, dgu_v, pr_v, ps_v, px_v, mid_v, inv_v,
    po_v, pd_v, so_v, sd_v, zo_v, zd_v, local, send, recv,
):
    here = Here(place)
    wires = Wires(send, recv)
    z, y, x, c = here.z, here.y, here.x, here.c
    toks = tokens.shape[0]
    pair = 2 * toks
    zs, xs, block = place.zs, place.xs, place.block
    width = 256
    sibling = here.sibling()
    greet(
        [sibling]
        + line_partners(here)
        + [here.device(x=shifted(x, step, xs)) for step in range(1, xs)]
    )

    loads = [
        pltpu.make_async_copy(wf, w_v, local.at[0]),
        pltpu.make_async_copy(dy_all, dy_v, local.at[1]),
        pltpu.make_async_copy(part, pr_v, local.at[2]),
    ]
    loads[2].start()
    loads[0].start()
    loads[1].start()
    loads[2].wait()

    def part_rows(x_at, c_at):
        return rows_at((x_at * 2 + c_at) * toks, toks)

    def x_rows(x_at):
        return rows_at(x_at * toks, toks)

    sib = [wires.slot() for step in range(xs)]
    for step in list(range(1, xs)) + [0]:
        x_at = shifted(x, step, xs)
        wires.start(sib[step], pr_v.at[part_rows(x_at, 1 - c)], ps_v.at[x_rows(x_at)], sibling)
    across = {}
    for step in list(range(1, xs)) + [0]:
        x_at = shifted(x, step, xs)
        wires.arrive(sib[step], ps_v.at[x_rows(x_at)], sibling)

        def add_pair(at, first, x_at=x_at):
            mine = pr_v[pl.ds(pl.multiple_of((x_at * 2 + c) * toks + first, 16), 16), :]
            at = pl.ds(pl.multiple_of(x_at * toks + first, 16), 16)
            ps_v[at, :] = (mine.astype(jnp.float32) + ps_v[at, :].astype(jnp.float32)).astype(
                jnp.bfloat16
            )

        each_rows(toks, add_pair)
        if step:
            across[step] = wires.slot()
            wires.start(
                across[step], ps_v.at[x_rows(x_at)], px_v.at[x_rows(x)], here.device(x=x_at)
            )
    for step in range(1, xs):
        from_x = shifted(x, -step, xs)
        wires.arrive(across[step], px_v.at[x_rows(from_x)], here.device(x=from_x))

    my_s2 = pl.multiple_of((z * 2 + c) * toks, toks)

    def middle_rows(at, first):
        total = ps_v[pl.ds(pl.multiple_of(x * toks + first, 16), 16), :].astype(jnp.float32)
        for step in range(1, xs):
            from_x = shifted(x, -step, xs)
            total = total + px_v[
                pl.ds(pl.multiple_of(from_x * toks + first, 16), 16), :
            ].astype(jnp.float32)
        middle = tokens[at, :].astype(jnp.float32) + total
        inverse = lax.rsqrt(jnp.mean(middle * middle, axis=1, keepdims=True) + EPSILON)
        mid_v[at, :] = middle
        inv_v[at, :] = jnp.broadcast_to(inverse, (16, LANES))
        s2_v[pl.ds(pl.multiple_of(my_s2 + first, 16), 16), :] = (middle * inverse).astype(
            jnp.bfloat16
        )

    each_rows(toks, middle_rows)

    def s2_view(z_at, c_at):
        return s2_v.at[rows_at((z_at * 2 + c_at) * toks, toks)]

    line = Line(wires, here, lambda z_at: s2_view(z_at, c))
    core_slots = {}

    def to_sibling(step):
        for side, (z_at, exists) in enumerate(line.valid(step)):
            core_slots[step, side] = wires.slot()
            view = s2_view(z_at, c)
            wires.start(core_slots[step, side], view, view, sibling, when=exists)

    def from_sibling(step):
        for side, (z_at, exists) in enumerate(line.valid(step)):
            wires.arrive(core_slots[step, side], s2_view(z_at, 1 - c), sibling, when=exists)

    line.send(0)
    to_sibling(0)

    orders = visit_order(zs)
    duplicate = 2 * block - place.zone

    def compute(b):
        at = rows_at(b * pair, pair)

        def hidden_tile(j, carry):
            def cols(base):
                return pl.ds(pl.multiple_of(base + j * width, width), width)

            gate = dot_nn(s2_v[at, :], w_v[:, cols(0)])
            up = dot_nn(s2_v[at, :], w_v[:, cols(block)])
            dhid = dot_nn(dy_v[at, :], w_v[:, cols(2 * block)])
            sg = 1.0 / (1.0 + jnp.exp(-gate))
            lane = lax.broadcasted_iota(jnp.int32, gate.shape, 1) + j * width
            keep = (lane >= duplicate) | (c == 0)
            act = gate * sg
            hid_v[at, cols(0)] = jnp.where(keep, act * up, 0.0).astype(jnp.bfloat16)
            dgate = dhid * up * sg * (1.0 + gate * (1.0 - sg))
            dgu_v[at, cols(0)] = jnp.where(keep, dgate, 0.0).astype(jnp.bfloat16)
            dgu_v[at, cols(block)] = jnp.where(keep, dhid * act, 0.0).astype(jnp.bfloat16)
            return carry

        lax.fori_loop(0, block // width, hidden_tile, 0)

        def back_tile(n, carry):
            cols = pl.ds(pl.multiple_of(n * width, width), width)
            pd_v[at, cols] = dot_nt(dgu_v[at, :], w_v[cols, pl.ds(0, 2 * block)]).astype(
                jnp.bfloat16
            )
            po_v[at, cols] = dot_nt(hid_v[at, :], w_v[cols, pl.ds(2 * block, block)]).astype(
                jnp.bfloat16
            )
            return carry

        lax.fori_loop(0, MODEL // width, back_tile, 0)

    sums = {}
    outs = {}

    def share(turn, b):
        for buffer, landing, kind in ((pd_v, sd_v, 0), (po_v, so_v, 1)):
            slot = wires.slot()
            sums[turn, kind] = slot
            wires.start(
                slot,
                buffer.at[rows_at((b * 2 + 1 - c) * toks, toks)],
                landing.at[rows_at(b * toks, toks)],
                sibling,
            )

    def add_up(turn, b):
        for buffer, landing, out, kind in ((pd_v, sd_v, zd_v, 0), (po_v, so_v, zo_v, 1)):
            view = landing.at[rows_at(b * toks, toks)]
            wires.arrive(sums[turn, kind], view, sibling)

            def add(at, first, buffer=buffer, landing=landing):
                mine = buffer[pl.ds(pl.multiple_of((b * 2 + c) * toks + first, 16), 16), :]
                at = pl.ds(pl.multiple_of(b * toks + first, 16), 16)
                landing[at, :] = (
                    mine.astype(jnp.float32) + landing[at, :].astype(jnp.float32)
                ).astype(jnp.bfloat16)

            each_rows(toks, add)
            if turn:
                outs[turn, kind] = True
                copy = pltpu.make_async_remote_copy(
                    src_ref=view,
                    dst_ref=out.at[rows_at(z * toks, toks)],
                    send_sem=send.at[z_send[kind] + turn],
                    recv_sem=recv.at[z_recv[kind] + z],
                    device_id=here.device(z=b),
                    device_id_type=MESH,
                )
                copy.start()
                wires.finish.append(copy.wait_send)

    z_send = [wires.used, wires.used + zs]
    z_recv = z_send
    wires.used += 2 * zs

    loads[0].wait()
    loads[1].wait()
    blocks = [chosen(z, turn, orders) for turn in range(zs)]
    from_sibling(0)
    for turn in range(zs):
        compute(blocks[turn])
        share(turn, blocks[turn])
        if turn + 1 < zs:
            line.arrive(turn + 1)
            line.send(turn + 1)
            to_sibling(turn + 1)
            from_sibling(turn + 1)
        if turn:
            add_up(turn - 1, blocks[turn - 1])
    add_up(zs - 1, blocks[zs - 1])

    def grad_tile(n, carry):
        cols = pl.ds(pl.multiple_of(n * width, width), width)
        w_v[cols, pl.ds(0, 2 * block)] = dot_tn(s2_v[:, cols], dgu_v[...]).astype(jnp.bfloat16)
        w_v[cols, pl.ds(2 * block, block)] = dot_tn(dy_v[:, cols], hid_v[...]).astype(
            jnp.bfloat16
        )
        return carry

    lax.fori_loop(0, MODEL // width, grad_tile, 0)
    store = pltpu.make_async_copy(w_v, gf, local.at[0])
    store.start()

    for kind, out in ((0, zd_v), (1, zo_v)):
        for step in range(1, zs):
            from_z = shifted(z, -step, zs)
            pltpu.make_async_remote_copy(
                src_ref=out.at[rows_at(from_z * toks, toks)],
                dst_ref=out.at[rows_at(from_z * toks, toks)],
                send_sem=send.at[z_send[kind]],
                recv_sem=recv.at[z_recv[kind] + from_z],
                device_id=here.device(z=from_z),
                device_id_type=MESH,
            ).wait_recv()

    def finish_rows(at, first):
        own = pl.ds(pl.multiple_of(z * toks + first, 16), 16)
        ds2 = sd_v[own, :].astype(jnp.float32)
        out = so_v[own, :].astype(jnp.float32)
        for step in range(1, zs):
            from_z = shifted(z, -step, zs)
            there = pl.ds(pl.multiple_of(from_z * toks + first, 16), 16)
            ds2 = ds2 + zd_v[there, :].astype(jnp.float32)
            out = out + zo_v[there, :].astype(jnp.float32)
        middle = mid_v[at, :]
        inverse = inv_v[at, :][:, :1]
        mixed[at, :] = (middle + out).astype(jnp.bfloat16)
        s2 = middle * inverse
        back = dy[at, :].astype(jnp.float32) + inverse * (
            ds2 - s2 * jnp.mean(ds2 * s2, axis=1, keepdims=True)
        )
        dmid[at, :] = back
        px_v[at, :] = back.astype(jnp.bfloat16)

    each_rows(toks, finish_rows)

    def dbr_view(x_at, c_at):
        return dbr_all.at[part_rows(x_at, c_at)]

    own = px_v.at[pl.ds(0, toks)]
    keep = pltpu.make_async_copy(own, dbr_view(x, c), local.at[1])
    keep.start()
    cross = [wires.slot() for step in range(xs)]
    core = [wires.slot() for step in range(xs)]
    wires.start(core[0], own, dbr_view(x, c), sibling)
    for step in range(1, xs):
        wires.start(cross[step], own, dbr_view(x, c), here.device(x=shifted(x, step, xs)))
    for step in range(1, xs):
        from_x = shifted(x, -step, xs)
        view = dbr_view(from_x, c)
        wires.arrive(cross[step], view, here.device(x=from_x))
        wires.start(core[step], view, view, sibling)
    for step in range(xs):
        wires.arrive(core[step], dbr_view(shifted(x, -step, xs), 1 - c), sibling)
    keep.wait()
    store.wait()
    wires.drain()


def feed_forward(place, part, tokens, dy, dy_all, wf):
    toks = tokens.shape[0]
    count = 128
    every = place.zs * 2 * toks
    seq = place.fsdp * toks
    low = jnp.bfloat16
    vmem = pl.BlockSpec(memory_space=pltpu.VMEM)
    hbm = pl.BlockSpec(memory_space=ANY)
    return pl.pallas_call(
        functools.partial(ffn_kernel, place),
        out_shape=(
            jax.ShapeDtypeStruct((toks, MODEL), low),
            jax.ShapeDtypeStruct((toks, MODEL), jnp.float32),
            jax.ShapeDtypeStruct((seq, MODEL), low),
            jax.ShapeDtypeStruct((MODEL, place.ffn_width), low),
        ),
        in_specs=[hbm, vmem, vmem, hbm, hbm],
        out_specs=(vmem, vmem, hbm, hbm),
        scratch_shapes=[
            pltpu.VMEM((MODEL, place.ffn_width), low),
            pltpu.VMEM((every, MODEL), low),
            pltpu.VMEM((every, MODEL), low),
            pltpu.VMEM((every, place.block), low),
            pltpu.VMEM((every, 2 * place.block), low),
            pltpu.VMEM((seq, MODEL), low),
            pltpu.VMEM((place.xs * toks, MODEL), low),
            pltpu.VMEM((place.xs * toks, MODEL), low),
            pltpu.VMEM((toks, MODEL), jnp.float32),
            pltpu.VMEM((toks, LANES), jnp.float32),
            pltpu.VMEM((every, MODEL), low),
            pltpu.VMEM((every, MODEL), low),
            pltpu.VMEM((place.zs * toks, MODEL), low),
            pltpu.VMEM((place.zs * toks, MODEL), low),
            pltpu.VMEM((place.zs * toks, MODEL), low),
            pltpu.VMEM((place.zs * toks, MODEL), low),
            pltpu.SemaphoreType.DMA((3,)),
            pltpu.SemaphoreType.DMA((count,)),
            pltpu.SemaphoreType.DMA((count,)),
        ],
        compiler_params=pltpu.CompilerParams(
            collective_id=1, has_side_effects=True, vmem_limit_bytes=60 * 2**20
        ),
        name="feed_forward",
    )(part, tokens, dy, dy_all, wf)


def reduce_kernel(
    place, gf, ga, dn1,
    out_f, out_a, ds1,
    own_f, x_f, y_f, own_a, y_a, z_a, own_d, s_d, x_d, local, send, recv,
):
    here = Here(place)
    wires = Wires(send, recv)
    z, y, x, c = here.z, here.y, here.x, here.c
    zs, ys, xs, rows, fsdp = place.zs, place.ys, place.xs, place.rows, place.fsdp
    toks = ds1.shape[0]
    sibling = here.sibling()
    low = jnp.bfloat16
    partners = line_partners(here) + plane_partners(here)
    partners += [here.device(x=shifted(x, step, xs), c=1 - c) for step in range(xs)]
    partners += [here.device(z=shifted(z, step, zs), c=1 - c) for step in range(1, zs)]
    greet(partners)

    pair = 2 * rows
    slab = fsdp * rows
    loads = []

    def load(source, target):
        copy = pltpu.make_async_copy(source, target, local.at[len(loads)])
        copy.start()
        loads.append(copy)

    def add(target, start, sources, count):
        def step(at, first):
            at = pl.ds(pl.multiple_of(start + first, 16), 16)
            total = target[at, :].astype(jnp.float32)
            for source, source_start in sources:
                there = pl.ds(pl.multiple_of(source_start + first, 16), 16)
                total = total + source[there, :].astype(jnp.float32)
            target[at, :] = total.astype(low)

        each_rows(count, step)

    def part_rows(x_at, c_at):
        return rows_at((x_at * 2 + c_at) * toks, toks)

    order = list(range(1, zs)) + [0]
    x_order = list(range(1, xs)) + [0]
    y_order = list(range(1, ys)) + [0]

    load(dn1, own_d)
    sib = [wires.slot() for step in range(xs)]
    for step in x_order:
        x_at = shifted(x, step, xs)
        wires.start(
            sib[step],
            dn1.at[part_rows(x_at, 1 - c)],
            s_d.at[rows_at(x_at * toks, toks)],
            sibling,
        )

    def f_block(z_at, y_at, x_at):
        return rows_at((((z_at * ys + y_at) * xs + x_at) * 2) * rows, pair)

    def f_own(z_at, y_at):
        return (z_at * ys + y_at) * pair

    send_x, send_y, attn_y = {}, {}, {}
    for step in order:
        z_at = shifted(z, step, zs)
        for hop in range(1, ys):
            y_at = shifted(y, hop, ys)
            attn_y[step, hop] = wires.slot()
            wires.start(
                attn_y[step, hop],
                ga.at[rows_at((z_at * ys + y_at) * slab, slab)],
                y_a.at[rows_at((z_at * ys + y) * slab, slab)],
                here.device(y=y_at),
            )
        load(
            ga.at[rows_at((z_at * ys + y) * slab, slab)], own_a.at[rows_at(z_at * slab, slab)]
        )
        for hop_y in y_order:
            y_at = shifted(y, hop_y, ys)
            for hop in range(1, xs):
                x_at = shifted(x, hop, xs)
                send_x[step, hop_y, hop] = wires.slot()
                wires.start(
                    send_x[step, hop_y, hop],
                    gf.at[f_block(z_at, y_at, x_at)],
                    x_f.at[f_block(z_at, y_at, x)],
                    here.device(x=x_at),
                )
            load(gf.at[f_block(z_at, y_at, x)], own_f.at[rows_at(f_own(z_at, y_at), pair)])
    for copy in loads:
        copy.wait()

    across = {}
    for step in x_order:
        x_at = shifted(x, step, xs)
        view = s_d.at[rows_at(x_at * toks, toks)]
        wires.arrive(sib[step], view, sibling)
        add(s_d, x_at * toks, [(own_d, (x_at * 2 + c) * toks)], toks)
        if step:
            across[step] = wires.slot()
            wires.start(
                across[step], view, x_d.at[rows_at(x * toks, toks)], here.device(x=x_at)
            )

    attn_z, ffn_z = {}, {}

    def f_across(step):
        z_at = shifted(z, step, zs)
        for hop_y in y_order:
            y_at = shifted(y, hop_y, ys)
            sources = []
            for hop in range(1, xs):
                from_x = shifted(x, -hop, xs)
                block = f_block(z_at, y_at, from_x)
                wires.arrive(send_x[step, hop_y, hop], x_f.at[block], here.device(x=from_x))
                sources.append((x_f, (((z_at * ys + y_at) * xs + from_x) * 2) * rows))
            add(own_f, f_own(z_at, y_at), sources, pair)
            if hop_y:
                send_y[step, hop_y] = wires.slot()
                wires.start(
                    send_y[step, hop_y],
                    own_f.at[rows_at(f_own(z_at, y_at), pair)],
                    y_f.at[rows_at(f_own(z_at, y), pair)],
                    here.device(y=y_at),
                )

    def a_across(step):
        z_at = shifted(z, step, zs)
        sources = []
        for hop in range(1, ys):
            from_y = shifted(y, -hop, ys)
            start = (z_at * ys + from_y) * slab
            wires.arrive(attn_y[step, hop], y_a.at[rows_at(start, slab)], here.device(y=from_y))
            sources.append((y_a, start))
        add(own_a, z_at * slab, sources, slab)
        if step:
            attn_z[step] = wires.slot()
            wires.start(
                attn_z[step],
                own_a.at[rows_at(z_at * slab, slab)],
                z_a.at[rows_at(z * slab, slab)],
                here.device(z=z_at),
            )

    def f_out(step):
        z_at = shifted(z, step, zs)
        sources = []
        for hop in range(1, ys):
            from_y = shifted(y, -hop, ys)
            start = f_own(z_at, from_y)
            wires.arrive(send_y[step, hop], y_f.at[rows_at(start, pair)], here.device(y=from_y))
            sources.append((y_f, start))
        add(own_f, f_own(z_at, y), sources, pair)
        for core in range(2):
            to_c = lax.rem(c + core, 2)
            source = own_f.at[rows_at(f_own(z_at, y) + to_c * rows, rows)]
            target = out_f.at[z * 2 + c]
            if step == 0 and core == 0:
                load(source, target)
            else:
                ffn_z[step, core] = wires.slot()
                wires.start(ffn_z[step, core], source, target, here.device(z=z_at, c=to_c))

    for turn, step in enumerate(order):
        a_across(step)
        f_across(step)
        if turn:
            f_out(order[turn - 1])
    sources = []
    for step in range(1, zs):
        from_z = shifted(z, -step, zs)
        start = from_z * slab
        wires.arrive(attn_z[step], z_a.at[rows_at(start, slab)], here.device(z=from_z))
        sources.append((z_a, start))
    add(own_a, z * slab, sources, slab)
    attn_f = {}
    for step in range(fsdp):
        other = shifted(here.fs, step, fsdp)
        source = own_a.at[rows_at(z * slab + other * rows, rows)]
        target = out_a.at[here.fs]
        if step:
            attn_f[step] = wires.slot()
            wires.start(attn_f[step], source, target, (here.dp, other))
        else:
            load(source, target)
    f_out(order[-1])

    def ds1_rows(at, first):
        total = s_d[pl.ds(pl.multiple_of(x * toks + first, 16), 16), :].astype(jnp.float32)
        for step in range(1, xs):
            from_x = shifted(x, -step, xs)
            there = pl.ds(pl.multiple_of(from_x * toks + first, 16), 16)
            total = total + x_d[there, :].astype(jnp.float32)
        ds1[at, :] = total

    for step in range(1, xs):
        from_x = shifted(x, -step, xs)
        wires.arrive(
            across[step], x_d.at[rows_at(from_x * toks, toks)], here.device(x=from_x)
        )
    each_rows(toks, ds1_rows)
    for step in range(1, fsdp):
        other = shifted(here.fs, -step, fsdp)
        wires.arrive(attn_f[step], out_a.at[other], (here.dp, other))
    for step in range(zs):
        from_z = shifted(z, -step, zs)
        for core in range(2):
            if step or core:
                from_c = lax.rem(c + core, 2)
                wires.arrive(
                    ffn_z[step, core],
                    out_f.at[from_z * 2 + from_c],
                    here.device(z=from_z, c=from_c),
                )
    for copy in loads[-2:]:
        copy.wait()
    wires.drain()


def reduce_gradients(place, gf, ga, dn1, toks):
    zs, ys, xs, rows, fsdp = place.zs, place.ys, place.xs, place.rows, place.fsdp
    slab = fsdp * rows
    low = jnp.bfloat16
    count = 256
    vmem = pl.BlockSpec(memory_space=pltpu.VMEM)
    hbm = pl.BlockSpec(memory_space=ANY)
    return pl.pallas_call(
        functools.partial(reduce_kernel, place),
        out_shape=(
            jax.ShapeDtypeStruct((2 * zs, rows, place.ffn_width), low),
            jax.ShapeDtypeStruct((fsdp, rows, place.attn_width), low),
            jax.ShapeDtypeStruct((toks, MODEL), jnp.float32),
        ),
        in_specs=[hbm] * 3,
        out_specs=(hbm, hbm, vmem),
        scratch_shapes=[
            pltpu.VMEM((zs * ys * 2 * rows, place.ffn_width), low),
            pltpu.VMEM((MODEL, place.ffn_width), low),
            pltpu.VMEM((zs * ys * 2 * rows, place.ffn_width), low),
            pltpu.VMEM((zs * slab, place.attn_width), low),
            pltpu.VMEM((MODEL, place.attn_width), low),
            pltpu.VMEM((zs * slab, place.attn_width), low),
            pltpu.VMEM((fsdp * toks, MODEL), low),
            pltpu.VMEM((xs * toks, MODEL), low),
            pltpu.VMEM((xs * toks, MODEL), low),
            pltpu.SemaphoreType.DMA((zs * ys + zs + 8,)),
            pltpu.SemaphoreType.DMA((count,)),
            pltpu.SemaphoreType.DMA((count,)),
        ],
        compiler_params=pltpu.CompilerParams(
            collective_id=2, has_side_effects=True, vmem_limit_bytes=60 * 2**20
        ),
        name="reduce_gradients",
    )(gf, ga, dn1)


def rotate(values, cosine, sine_part):
    half = values.shape[-1] // 2
    first, second = values[..., :half], values[..., half:]
    return jnp.concatenate(
        [first * cosine - second * sine_part, second * cosine + first * sine_part], axis=-1
    )


def on_device(
    place, tokens, lengths, gain_attn, w_qkv, w_out, gain_ffn, w_gateup, w_down, out_grad, kv_grad
):
    toks = tokens.shape[0]
    fsdp = place.fsdp
    seq = toks * fsdp
    own_heads = place.heads // HEAD_DIM
    scale = HEAD_DIM ** (-0.5)
    low = jnp.bfloat16
    f32 = jnp.float32
    group = lax.axis_index("dp")
    own = lax.axis_index("fsdp")
    length = jnp.sum(
        jnp.where(jnp.arange(lengths.shape[0], dtype=jnp.int32) == group, lengths, 0)
    )
    slots = jnp.arange(seq, dtype=jnp.int32)
    positions = slots % toks * fsdp + slots // toks
    frequency = THETA ** (-jnp.arange(HEAD_DIM // 2, dtype=f32) * (2.0 / HEAD_DIM))
    angles = positions.astype(f32)[:, None] * frequency[None, :]
    cosine, sine_part = jnp.cos(angles), jnp.sin(angles)
    allowed = (positions[None, :] <= positions[:, None]) & (positions[None, :] < length)

    gain_a = gain_attn.astype(f32)[:, None]
    gain_f = gain_ffn.astype(f32)[:, None]
    folded_qkv = (w_qkv.astype(f32) * gain_a).astype(low)
    folded_gateup = (w_gateup.astype(f32) * gain_f).astype(low)
    wa, wf, tok_all, dy_all = gather(
        place, folded_qkv, w_out, folded_gateup, w_down, tokens, out_grad
    )
    w_proj = wa[:, : place.heads + KV]
    w_branch = wa[:, place.heads + KV :]

    seq_values = tok_all.astype(f32)
    seq_inverse = lax.rsqrt(jnp.mean(seq_values * seq_values, axis=1, keepdims=True) + EPSILON)
    s1_all = (seq_values * seq_inverse).astype(low)
    projected = dot_nn(s1_all, w_proj)
    queries = rotate(
        projected[:, : place.heads].reshape(seq, own_heads, HEAD_DIM),
        cosine[:, None, :],
        sine_part[:, None, :],
    ).astype(low)
    queries = queries.transpose(1, 0, 2)
    keys = rotate(
        projected[:, place.heads : place.heads + HEAD_DIM], cosine, sine_part
    ).astype(low)
    values = projected[:, place.heads + HEAD_DIM :].astype(low)
    shared_kv = lax.dynamic_slice_in_dim(
        jnp.concatenate([keys, values], axis=1), own * toks, toks, 0
    )
    scores = jnp.einsum("hqd,kd->hqk", queries, keys, preferred_element_type=f32) * scale
    scores = jnp.where(allowed[None], scores, MASKED)
    row_max = jnp.max(scores, axis=-1, keepdims=True)
    exponent = jnp.exp(scores - row_max)
    row_total = jnp.sum(exponent, axis=-1, keepdims=True)
    attended_f = (
        jnp.einsum("hqk,kd->hqd", exponent.astype(low), values, preferred_element_type=f32)
        / row_total
    )
    log_total = row_max + jnp.log(row_total)
    attended = attended_f.transpose(1, 0, 2).reshape(seq, place.heads).astype(low)
    part = dot_nt(attended, w_branch).astype(low)

    mixed, dmid, dbr_all, gf = feed_forward(place, part, tokens, out_grad, dy_all, wf)

    dattended = dot_nn(dbr_all, w_branch).astype(low)
    grads = dattended.reshape(seq, own_heads, HEAD_DIM).transpose(1, 0, 2)
    delta = jnp.sum(grads.astype(f32) * attended_f, axis=-1, keepdims=True)
    probability = jnp.exp(scores - log_total)
    dprob = jnp.einsum("hqd,kd->hqk", grads, values, preferred_element_type=f32)
    dscore = (probability * (dprob - delta)).astype(low)
    dquery = jnp.einsum("hqk,kd->hqd", dscore, keys, preferred_element_type=f32) * scale
    dkey = jnp.einsum("hqk,hqd->kd", dscore, queries, preferred_element_type=f32) * scale
    dvalue = jnp.einsum(
        "hqk,hqd->kd", probability.astype(low), grads, preferred_element_type=f32
    )
    dkv = jnp.concatenate([dkey, dvalue], axis=1)
    own_kv = lax.dynamic_slice_in_dim(dkv, own * toks, toks, 0) + kv_grad.astype(f32)
    dkv = lax.dynamic_update_slice_in_dim(dkv, own_kv, own * toks, 0)
    dq_raw = rotate(
        dquery.transpose(1, 0, 2), cosine[:, None, :], -sine_part[:, None, :]
    ).reshape(seq, place.heads)
    dk_raw = rotate(dkv[:, :HEAD_DIM], cosine, -sine_part)
    dprojected = jnp.concatenate([dq_raw, dk_raw, dkv[:, HEAD_DIM:]], axis=1).astype(low)
    dn1 = dot_nt(dprojected, w_proj).astype(low)
    ga = jnp.concatenate(
        [dot_tn(s1_all, dprojected).astype(low), dot_tn(dbr_all, attended).astype(low)], axis=1
    )

    out_f, out_a, ds1 = reduce_gradients(place, gf, ga, dn1, toks)

    own_values = tokens.astype(f32)
    inverse = lax.rsqrt(jnp.mean(own_values * own_values, axis=1, keepdims=True) + EPSILON)
    s1 = own_values * inverse
    input_grad = (
        dmid + inverse * (ds1 - s1 * jnp.mean(ds1 * s1, axis=1, keepdims=True))
    ).astype(low)

    heads, block = place.heads, place.block
    duplicate = 2 * block - place.zone
    out_f = out_f.astype(f32)
    out_a = out_a.astype(f32)

    def columns(start):
        pieces = []
        for z_at in range(place.zs):
            pieces.append(out_f[2 * z_at, :, start : start + block])
            pieces.append(out_f[2 * z_at + 1, :, start + duplicate : start + block])
        return pieces

    plain_gateup = jnp.concatenate(columns(0) + columns(block), axis=1)
    grad_down = jnp.concatenate(columns(2 * block), axis=1)
    plain_qkv = jnp.concatenate(
        [out_a[at, :, :heads] for at in range(fsdp)]
        + [jnp.sum(out_a[:, :, heads : heads + KV], axis=0)],
        axis=1,
    )
    grad_out = jnp.concatenate([out_a[at, :, heads + KV :] for at in range(fsdp)], axis=1)
    grad_gain_attn = jnp.sum(w_qkv.astype(f32) * plain_qkv, axis=1)
    grad_gain_ffn = jnp.sum(w_gateup.astype(f32) * plain_gateup, axis=1)
    return (
        mixed,
        shared_kv,
        input_grad,
        grad_gain_attn,
        plain_qkv * gain_a,
        grad_out,
        grad_gain_ffn,
        plain_gateup * gain_f,
        grad_down,
    )


def solution(mesh):
    place = Place(mesh.shape["dp"], mesh.shape["fsdp"])
    row = P(("dp", "fsdp"), None)
    line = P(("dp", "fsdp"))
    return jax.shard_map(
        functools.partial(on_device, place),
        mesh=mesh,
        in_specs=(row, P(), line, row, row, line, row, row, row, row),
        out_specs=(row, row, row, line, row, row, line, row, row),
        check_vma=False,
    )
```

```python
import functools

import jax
import jax.numpy as jnp
import numpy as np
from jax import lax
from jax.experimental import pallas as pl
from jax.experimental.pallas import tpu as pltpu
from jax.sharding import PartitionSpec as P

HEADS = 16
HEAD_DIM = 128
FF = 5632
HQ = 2048
MODEL = 2048
KV = 2 * HEAD_DIM
LANES = 128

EPSILON = 1e-05
THETA = 10000.0
MASKED = -1e30
MESH = pl.DeviceIdType.MESH
ANY = pl.ANY


class Place:
    def __init__(self, dp_count, fsdp_count):
        self.fsdp = fsdp_count
        self.xs = fsdp_count // 2
        self.ys = self.xs
        self.zs = dp_count // self.ys
        self.rows = MODEL // (dp_count * fsdp_count)
        self.heads = HQ // fsdp_count
        self.attn_width = 2 * self.heads + KV
        self.zone = FF // self.zs
        self.block = LANES * -(-(self.zone // LANES) // 2)
        self.ffn_width = 3 * self.block
        zs, ys, xs, fsdp = self.zs, self.ys, self.xs, self.fsdp
        across = (ys - 1) + (xs - 1)
        line = 2 * (zs - 1)
        self.copies = (
            3 * (fsdp - 1) + 3 * (2 * zs - 1) + 2 * (line + (2 * zs - 1) * (ys - 1))
            + 2 * (line + 2 * zs - 1) + 2 * xs + 2 * (2 * xs - 1) + 4 * zs
            + 2 * zs * max(across + xs * (ys - 1), across + ys * (xs - 1))
            + 2 * zs * (ys - 1) + zs - 1 + 2 * zs - 1 + fsdp - 1 + 2 * xs
        )


class Here:
    def __init__(self, place):
        self.place = place
        self.dp = lax.axis_index("dp")
        self.fs = lax.axis_index("fsdp")
        self.z = self.dp // place.ys
        self.y = lax.rem(self.dp, place.ys)
        self.x = self.fs // 2
        self.c = lax.rem(self.fs, 2)

    def device(self, z=None, y=None, x=None, c=None):
        z = self.z if z is None else z
        y = self.y if y is None else y
        x = self.x if x is None else x
        c = self.c if c is None else c
        return (z * self.place.ys + y, x * 2 + c)

    def sibling(self):
        return self.device(c=1 - self.c)


def shifted(value, step, count):
    return lax.rem(value + (step + count), count)


def rows_at(start, count):
    return pl.ds(pl.multiple_of(start, count), count)


def cols_at(start, count):
    return pl.ds(pl.multiple_of(start, LANES), count)


class Wires:
    def __init__(self, send, recv):
        self.send = send
        self.recv = recv
        self.used = 0
        self.finish = []

    def slot(self):
        self.used += 1
        return self.used - 1

    def copy(self, slot, source, target, device):
        return pltpu.make_async_remote_copy(
            src_ref=source,
            dst_ref=target,
            send_sem=self.send.at[slot],
            recv_sem=self.recv.at[slot],
            device_id=device,
            device_id_type=MESH,
        )

    def start(self, slot, source, target, device, when=None):
        copy = self.copy(slot, source, target, device)
        if when is None:
            copy.start()
            wait = copy.wait_send
        else:
            pl.when(when)(copy.start)

            def wait():
                pl.when(when)(copy.wait_send)

        self.finish.append(wait)

        def done():
            self.finish.remove(wait)
            wait()

        return done

    def arrive(self, slot, target, device, when=None):
        copy = self.copy(slot, target, target, device)
        if when is None:
            copy.wait_recv()
        else:
            pl.when(when)(copy.wait_recv)

    def drain(self):
        for wait in self.finish:
            wait()
        self.finish = []


def greet(devices):
    barrier = pltpu.get_barrier_semaphore()
    for device in devices:
        pl.semaphore_signal(barrier, inc=1, device_id=device, device_id_type=MESH)
    pl.semaphore_wait(barrier, len(devices))


def line_partners(here):
    place = here.place
    return [here.device(z=shifted(here.z, step, place.zs)) for step in range(1, place.zs)]


def plane_partners(here):
    place = here.place
    return [here.device(y=shifted(here.y, step, place.ys)) for step in range(1, place.ys)] + [
        here.device(x=shifted(here.x, step, place.xs)) for step in range(1, place.xs)
    ]


class Line:
    def __init__(self, wires, here, view):
        self.wires = wires
        self.here = here
        self.view = view
        count = here.place.zs
        self.count = count
        self.up = [wires.slot() for step in range(count - 1)]
        self.down = [wires.slot() for step in range(count - 1)]

    def send(self, step):
        here, count = self.here, self.count
        if step >= count - 1:
            return []
        z = here.z
        low = lax.max(z - step, 0)
        high = lax.min(z + step, count - 1)
        up = self.wires.start(
            self.up[step],
            self.view(low),
            self.view(low),
            here.device(z=lax.min(z + 1, count - 1)),
            when=(z >= step) & (z < count - 1),
        )
        down = self.wires.start(
            self.down[step],
            self.view(high),
            self.view(high),
            here.device(z=lax.max(z - 1, 0)),
            when=(z + step < count) & (z > 0),
        )
        return [up, down]

    def arrive(self, step):
        here, count = self.here, self.count
        z = here.z
        low = lax.max(z - step, 0)
        high = lax.min(z + step, count - 1)
        self.wires.arrive(
            self.up[step - 1], self.view(low), here.device(z=lax.max(z - 1, 0)), when=z >= step
        )
        self.wires.arrive(
            self.down[step - 1],
            self.view(high),
            here.device(z=lax.min(z + 1, count - 1)),
            when=z + step < count,
        )

    def valid(self, step):
        z = self.here.z
        if step == 0:
            return [(z, None)]
        return [
            (lax.max(z - step, 0), z >= step),
            (lax.min(z + step, self.count - 1), z + step < self.count),
        ]


def each_rows(count, body, size=16):
    def step(index, carry):
        body(pl.ds(pl.multiple_of(index * size, size), size), index * size)
        return carry

    lax.fori_loop(0, count // size, step, 0)


def dot_nn(left, right):
    return lax.dot_general(
        left, right, (((1,), (0,)), ((), ())), preferred_element_type=jnp.float32
    )


def dot_nt(left, right):
    return lax.dot_general(
        left, right, (((1,), (1,)), ((), ())), preferred_element_type=jnp.float32
    )


def dot_tn(left, right):
    return lax.dot_general(
        left, right, (((0,), (0,)), ((), ())), preferred_element_type=jnp.float32
    )


def visit_order(count):
    orders = []
    for z in range(count):
        far = sorted(range(count), key=lambda other: (abs(other - z), other))
        orders.append(far)
    return orders


def chosen(z, turn, orders):
    total = 0
    for z_at, order in enumerate(orders):
        here = jnp.where(z == z_at, 1, 0)
        for turn_at, value in enumerate(order):
            if isinstance(turn, int):
                if turn == turn_at:
                    total = total + here * value
            else:
                total = total + here * jnp.where(turn == turn_at, 1, 0) * value
    return total


def block_kernel(
    place, w_qkv, w_out, w_gateup, w_down, tokens, dy, kv_grad, cos_t, sin_t, key_at,
    mixed, shared_kv, input_grad, out_f, out_a,
    wa, w_v, tok_v, dy_v, s2_v, hid_v, dgu_v, pr_v, ps_v, px_v, mid_v, inv_v,
    so_v, sd_v, zo_v, zd_v, q_v, kv_v, att_v, dkv_v,
    x_f, y_f, y_a, z_a, local, send, recv,
):
    here = Here(place)
    wires = Wires(send, recv)
    z, y, x, c = here.z, here.y, here.x, here.c
    zs, ys, xs, fsdp, rows = place.zs, place.ys, place.xs, place.fsdp, place.rows
    heads, block, zone = place.heads, place.block, place.zone
    proj = heads + KV
    toks = tokens.shape[0]
    seq = toks * fsdp
    pair = 2 * toks
    slab = fsdp * rows
    width = 256
    low = jnp.bfloat16
    f32 = jnp.float32
    scale = HEAD_DIM ** (-0.5)
    sibling = here.sibling()
    partners = line_partners(here) + plane_partners(here)
    partners += [here.device(x=shifted(x, step, xs), c=1 - c) for step in range(xs)]
    partners += [here.device(z=shifted(z, step, zs), c=1 - c) for step in range(1, zs)]
    greet(partners)

    def index(z=z, y=y, x=x, c=c):
        return (z * ys + y) * fsdp + x * 2 + c

    locals_ = []

    def keep(source, target):
        copy = pltpu.make_async_copy(source, target, local.at[len(locals_)])
        copy.start()
        locals_.append(copy)
        return copy

    def at16(start):
        return pl.ds(pl.multiple_of(start, 16), 16)

    def add(target, start, sources, count):
        def step(at, first):
            at = at16(start + first)
            total = target[at, :].astype(f32)
            for source, source_start in sources:
                total = total + source[at16(source_start + first), :].astype(f32)
            target[at, :] = total.astype(low)

        each_rows(count, step)

    own_rows = rows_at(index() * rows, rows)
    qkv_cols, out_cols = pl.ds(0, proj), pl.ds(proj, heads)

    def qkv_pieces(owner):
        return [(w_qkv, owner * heads, heads, 0), (w_qkv, HQ, KV, heads)]

    def out_pieces(owner):
        return [(w_out, owner * heads, heads, proj)]

    def attn_spread(pieces):
        slots = []
        for step in range(1, fsdp):
            other = shifted(here.fs, step, fsdp)
            for ref, start, count, place_at in pieces(other):
                slot = wires.slot()
                slots.append((slot, step, count, place_at))
                wires.start(
                    slot,
                    ref.at[:, cols_at(start, count)],
                    wa.at[own_rows, pl.ds(place_at, count)],
                    (here.dp, other),
                )
        for ref, start, count, place_at in pieces(here.fs):
            keep(ref.at[:, cols_at(start, count)], wa.at[own_rows, pl.ds(place_at, count)])
        return slots

    def attn_collect(slots):
        for slot, step, count, place_at in slots:
            other = shifted(here.fs, -step, fsdp)
            at = rows_at((here.dp * fsdp + other) * rows, rows)
            wires.arrive(slot, wa.at[at, pl.ds(place_at, count)], (here.dp, other))

    def ffn_pieces(zone_z, core):
        start = zone_z * zone + core * (zone - block)
        return [(w_gateup, start, 0), (w_gateup, FF + start, block), (w_down, start, 2 * block)]

    ffn_slots = {}

    def ffn_spread(step):
        for core in range(2):
            to_z, to_c = shifted(z, step, zs), lax.rem(c + core, 2)
            for ref, start, place_at in ffn_pieces(to_z, to_c):
                source = ref.at[:, cols_at(start, block)]
                target = w_v.at[own_rows, pl.ds(place_at, block)]
                if step == 0 and core == 0:
                    keep(source, target)
                    continue
                slot = wires.slot()
                ffn_slots.setdefault(step, []).append((slot, core, place_at))
                wires.start(slot, source, target, here.device(z=to_z, c=to_c))

    def ffn_collect(step):
        from_z = shifted(z, -step, zs)
        for slot, core, place_at in ffn_slots[step]:
            from_c = lax.rem(c + core, 2)
            at = rows_at(index(z=from_z, c=from_c) * rows, rows)
            wires.arrive(slot, w_v.at[at, pl.ds(place_at, block)], here.device(z=from_z, c=from_c))

    def w_view(z_at, y_at, x_at):
        return w_v.at[rows_at(index(z_at, y_at, x_at, 0) * rows, 2 * rows)]

    near, far = {}, {}
    w_sent = []

    def axes(step):
        ways = [("y", y, ys), ("x", x, xs)]
        return ways if step != 2 else ways[::-1]

    def at_plane(name, value, other):
        return {"y_at": value, "x_at": other} if name == "y" else {"y_at": other, "x_at": value}

    def to_plane(name, value):
        return here.device(y=value) if name == "y" else here.device(x=value)

    def ffn_send(slots, key, name, me, count, view):
        for hop in range(1, count):
            slot = slots[key + (hop,)] = wires.slot()
            w_sent.append(wires.start(slot, view, view, to_plane(name, shifted(me, hop, count))))

    def ffn_forward(step):
        ffn_collect(step)
        z_at = shifted(z, -step, zs)
        (first, me, count), (second, me2, count2) = axes(step)
        ffn_send(near, (step,), first, me, count, w_view(z_at, y, x))
        ffn_send(far, (step, 0), second, me2, count2, w_view(z_at, y, x))

    def ffn_across(step):
        z_at = shifted(z, -step, zs)
        (first, me, count), (second, me2, count2) = axes(step)
        for hop in range(1, count):
            origin = shifted(me, -hop, count)
            view = w_view(z_at, **at_plane(first, origin, me2))
            wires.arrive(near[step, hop], view, to_plane(first, origin))
            ffn_send(far, (step, hop), second, me2, count2, view)

    def ffn_arrive(step):
        z_at = shifted(z, -step, zs)
        (first, me, count), (second, me2, count2) = axes(step)
        for hop in range(count):
            for hop2 in range(1, count2):
                origin, origin2 = shifted(me, -hop, count), shifted(me2, -hop2, count2)
                view = w_view(z_at, **at_plane(first, origin, origin2))
                wires.arrive(far[step, hop, hop2], view, to_plane(second, origin2))

    class Spread:
        def __init__(self, cols):
            self.cols = cols
            self.line = Line(wires, here, lambda z_at: self.view(z_at, y))
            self.plane = {}
            self.sent = []

        def view(self, z_at, y_at):
            return wa.at[rows_at((z_at * ys + y_at) * slab, slab), self.cols]

        def step(self, step):
            if step:
                self.line.arrive(step)
            self.sent += self.line.send(step)
            for side, (z_at, exists) in enumerate(self.line.valid(step)):
                for hop in range(1, ys):
                    slot = self.plane[step, side, hop] = wires.slot()
                    view = self.view(z_at, y)
                    there = here.device(y=shifted(y, hop, ys))
                    self.sent.append(wires.start(slot, view, view, there, when=exists))

        def crossed(self):
            for step in range(zs):
                for side, (z_at, exists) in enumerate(self.line.valid(step)):
                    for hop in range(1, ys):
                        from_y = shifted(y, -hop, ys)
                        wires.arrive(
                            self.plane[step, side, hop],
                            self.view(z_at, from_y),
                            here.device(y=from_y),
                            when=exists,
                        )

    class Acts:
        def __init__(self, ref):
            self.ref = ref
            self.line = Line(wires, here, lambda z_at: self.view(z_at, c))
            self.core = {}
            self.sent = []

        def view(self, z_at, c_at):
            return self.ref.at[rows_at((z_at * 2 + c_at) * toks, toks)]

        def step(self, step):
            if step:
                self.line.arrive(step)
            self.sent += self.line.send(step)
            for side, (z_at, exists) in enumerate(self.line.valid(step)):
                slot = self.core[step, side] = wires.slot()
                view = self.view(z_at, c)
                self.sent.append(wires.start(slot, view, view, sibling, when=exists))

        def crossed(self, step):
            for side, (z_at, exists) in enumerate(self.line.valid(step)):
                wires.arrive(self.core[step, side], self.view(z_at, 1 - c), sibling, when=exists)

    def tok_view(x_at, c_at):
        return tok_v.at[rows_at((x_at * 2 + c_at) * toks, toks)]

    qkv_slots = attn_spread(qkv_pieces)
    ffn_spread(0)
    ffn_spread(1)
    keep(tokens, tok_view(x, c))
    tok_cross = [wires.slot() for step in range(xs)]
    tok_core = [wires.slot() for step in range(xs)]
    wires.start(tok_core[0], tokens, tok_view(x, c), sibling)
    for step in range(1, xs):
        wires.start(
            tok_cross[step], tokens, tok_view(x, c), here.device(x=shifted(x, step, xs))
        )
    out_slots = attn_spread(out_pieces)
    dys = Acts(dy_v)
    keep(dy, dys.view(z, c))
    for copy in locals_:
        copy.wait()
    first_local = len(locals_)
    ffn_forward(0)
    attn_collect(qkv_slots)
    qkv = Spread(qkv_cols)
    qkv.step(0)
    attn_collect(out_slots)
    outw = Spread(out_cols)
    outw.step(0)
    ffn_forward(1)
    tok_sent = []
    for step in range(1, xs):
        from_x = shifted(x, -step, xs)
        view = tok_view(from_x, c)
        wires.arrive(tok_cross[step], view, here.device(x=from_x))
        tok_sent.append(wires.start(tok_core[step], view, view, sibling))
    ffn_across(0)
    qkv.step(1)
    outw.step(1)
    for step in range(xs):
        from_x = shifted(x, -step, xs)
        wires.arrive(tok_core[step], tok_view(from_x, 1 - c), sibling)
    for done in tok_sent:
        done()

    def norm_rows(at, first):
        values = tok_v[at, :].astype(f32)
        inverse = lax.rsqrt(jnp.mean(values * values, axis=1, keepdims=True) + EPSILON)
        tok_v[at, :] = (values * inverse).astype(low)

    each_rows(seq, norm_rows)
    qkv.step(2)
    outw.step(2)
    ffn_across(1)
    late = [zs - 1] + list(range(2, zs - 1))
    for step in late:
        ffn_spread(step)
    dys.step(0)
    for step in range(3, zs):
        qkv.step(step)
        outw.step(step)
    qkv.crossed()

    half = HEAD_DIM // 2

    def turned(values, at, sign):
        return values * cos_t[at, :] + pltpu.roll(values, half, 1) * (sign * sin_t[at, :])

    row_blocks = seq // width

    def project(step, carry):
        at = rows_at(step * width, width)

        def query_tile(j, carry):
            cols = pl.ds(pl.multiple_of(j * HEAD_DIM, HEAD_DIM), HEAD_DIM)
            q_v[at, cols] = turned(dot_nn(tok_v[at, :], wa[:, cols]), at, 1.0).astype(low)
            return carry

        lax.fori_loop(0, heads // HEAD_DIM, query_tile, 0)
        both = dot_nn(tok_v[at, :], wa[:, pl.ds(heads, KV)])
        kv_v[at, :HEAD_DIM] = turned(both[:, :HEAD_DIM], at, 1.0).astype(low)
        kv_v[at, HEAD_DIM:] = both[:, HEAD_DIM:].astype(low)
        return carry

    lax.fori_loop(0, row_blocks, project, 0)
    shared_kv[...] = kv_v[rows_at(here.fs * toks, toks), :]

    def weights_of(at, cols, first):
        scores = dot_nt(q_v[at, cols], kv_v[:, :HEAD_DIM]) * scale
        row = lax.broadcasted_iota(jnp.int32, (width, LANES), 0) + first
        query_at = lax.rem(row, toks) * fsdp + row // toks
        allowed = key_at[0:1, :] <= query_at[:, :1]
        scores = jnp.where(allowed, scores, MASKED)
        exponent = jnp.exp(scores - jnp.max(scores, axis=1, keepdims=True))
        return exponent, jnp.sum(exponent, axis=1, keepdims=True)

    def attend(step, carry):
        at = rows_at(lax.rem(step, row_blocks) * width, width)
        cols = pl.ds(pl.multiple_of(step // row_blocks * HEAD_DIM, HEAD_DIM), HEAD_DIM)
        exponent, total = weights_of(at, cols, lax.rem(step, row_blocks) * width)
        att_v[at, cols] = (dot_nn(exponent.astype(low), kv_v[:, HEAD_DIM:]) / total).astype(low)
        return carry

    lax.fori_loop(0, row_blocks * (heads // HEAD_DIM), attend, 0)
    outw.crossed()

    def branch_tile(n, carry):
        cols = pl.ds(pl.multiple_of(n * width, width), width)
        pr_v[:, cols] = dot_nt(att_v[...], wa[cols, out_cols]).astype(low)
        return carry

    lax.fori_loop(0, MODEL // width, branch_tile, 0)

    def part_rows(x_at, c_at):
        return rows_at((x_at * 2 + c_at) * toks, toks)

    def x_rows(x_at):
        return rows_at(x_at * toks, toks)

    x_order = list(range(1, xs)) + [0]

    def reduce_sequence(source):
        sib = [wires.slot() for step in range(xs)]
        across = {}
        sent = []
        for step in x_order:
            x_at = shifted(x, step, xs)
            sent.append(
                wires.start(
                    sib[step], source.at[part_rows(x_at, 1 - c)], ps_v.at[x_rows(x_at)], sibling
                )
            )
        for step in x_order:
            x_at = shifted(x, step, xs)
            wires.arrive(sib[step], ps_v.at[x_rows(x_at)], sibling)
            add(ps_v, x_at * toks, [(source, (x_at * 2 + c) * toks)], toks)
            if step == x_order[0]:
                for done in sent:
                    done()
            if step:
                across[step] = wires.slot()
                sent.append(
                    wires.start(
                        across[step], ps_v.at[x_rows(x_at)], px_v.at[x_rows(x)], here.device(x=x_at)
                    )
                )
        return across, sent[xs:]

    def sequence_arrive(across):
        for step in range(1, xs):
            from_x = shifted(x, -step, xs)
            wires.arrive(across[step], px_v.at[x_rows(from_x)], here.device(x=from_x))

    def sequence_total(first):
        total = ps_v[at16(x * toks + first), :].astype(f32)
        for step in range(1, xs):
            total = total + px_v[at16(shifted(x, -step, xs) * toks + first), :].astype(f32)
        return total

    across, across_sent = reduce_sequence(pr_v)
    ffn_forward(late[0])
    sequence_arrive(across)
    s2s = Acts(s2_v)
    my_s2 = (z * 2 + c) * toks

    def middle_rows(at, first):
        middle = tokens[at, :].astype(f32) + sequence_total(first)
        inverse = lax.rsqrt(jnp.mean(middle * middle, axis=1, keepdims=True) + EPSILON)
        mid_v[at, :] = middle
        inv_v[at, :] = jnp.broadcast_to(inverse, (16, LANES))
        s2_v[at16(my_s2 + first), :] = (middle * inverse).astype(low)

    each_rows(toks, middle_rows)
    s2s.step(0)
    ffn_across(late[0])
    for step in late[1:]:
        ffn_forward(step)
    dys.step(1)
    for step in late[1:]:
        ffn_across(step)
    s2s.step(1)
    for done in across_sent:
        done()
    for step in range(zs):
        ffn_arrive(step)
    orders = visit_order(zs)
    blocks = [chosen(z, turn, orders) for turn in range(zs)]
    duplicate = 2 * block - zone

    def hidden(b):
        at = rows_at(b * pair, pair)

        def hidden_tile(j, carry):
            def cols(base):
                return pl.ds(pl.multiple_of(base + j * width, width), width)

            gate = dot_nn(s2_v[at, :], w_v[:, cols(0)])
            up = dot_nn(s2_v[at, :], w_v[:, cols(block)])
            dhid = dot_nn(dy_v[at, :], w_v[:, cols(2 * block)])
            sg = 1.0 / (1.0 + jnp.exp(-gate))
            lane = lax.broadcasted_iota(jnp.int32, gate.shape, 1) + j * width
            mine = (lane >= duplicate) | (c == 0)
            act = gate * sg
            hid_v[at, cols(0)] = jnp.where(mine, act * up, 0.0).astype(low)
            dgate = dhid * up * sg * (1.0 + gate * (1.0 - sg))
            dgu_v[at, cols(0)] = jnp.where(mine, dgate, 0.0).astype(low)
            dgu_v[at, cols(block)] = jnp.where(mine, dhid * act, 0.0).astype(low)
            return carry

        lax.fori_loop(0, block // width, hidden_tile, 0)

    pd_v, po_v = px_v, ps_v

    def back(b):
        at = rows_at(b * pair, pair)

        def back_tile(n, carry):
            cols = pl.ds(pl.multiple_of(n * width, width), width)
            pd_v[pl.ds(0, pair), cols] = dot_nt(
                dgu_v[at, :], w_v[cols, pl.ds(0, 2 * block)]
            ).astype(low)
            po_v[pl.ds(0, pair), cols] = dot_nt(hid_v[at, :], w_v[cols, pl.ds(2 * block, block)]).astype(low)
            return carry

        lax.fori_loop(0, MODEL // width, back_tile, 0)

    kinds = ((pd_v, sd_v, zd_v), (po_v, so_v, zo_v))
    z_slots = [wires.used, wires.used + zs]
    wires.used += 2 * zs
    shares = {}

    def share(turn, b):
        for kind, (buffer, landing, out) in enumerate(kinds):
            slot = wires.slot()
            done = wires.start(
                slot,
                buffer.at[rows_at((1 - c) * toks, toks)],
                landing.at[rows_at(b * toks, toks)],
                sibling,
            )
            shares[turn, kind] = (slot, done)

    def add_up(turn, b):
        for kind, (buffer, landing, out) in enumerate(kinds):
            slot, done = shares[turn, kind]
            view = landing.at[rows_at(b * toks, toks)]
            wires.arrive(slot, view, sibling)
            add(landing, b * toks, [(buffer, c * toks)], toks)
            done()
        if turn:
            send_line(0, turn)

    def send_line(kind, turn):
        buffer, landing, out = kinds[kind]
        b = blocks[turn]
        copy = pltpu.make_async_remote_copy(
            src_ref=landing.at[rows_at(b * toks, toks)],
            dst_ref=out.at[line_slot(z, b)],
            send_sem=send.at[z_slots[kind] + turn],
            recv_sem=recv.at[z_slots[kind] + z],
            device_id=here.device(z=b),
            device_id_type=MESH,
        )
        copy.start()
        wires.finish.append(copy.wait_send)

    def line_slot(source, owner):
        return rows_at(lax.rem(owner - source + zs, zs) * toks - toks, toks)

    def collect_line(kind):
        out = kinds[kind][2]
        for step in range(1, zs):
            from_z = shifted(z, -step, zs)
            view = out.at[pl.ds((step - 1) * toks, toks)]
            pltpu.make_async_remote_copy(
                src_ref=view,
                dst_ref=view,
                send_sem=send.at[z_slots[kind]],
                recv_sem=recv.at[z_slots[kind] + from_z],
                device_id=here.device(z=from_z),
                device_id_type=MESH,
            ).wait_recv()

    def line_total(kind, first):
        buffer, landing, out = kinds[kind]
        total = landing[at16(z * toks + first), :].astype(f32)
        for step in range(1, zs):
            total = total + out[at16((step - 1) * toks + first), :].astype(f32)
        return total

    s2s.crossed(0)
    dys.crossed(0)
    for turn in range(zs):
        if turn:
            s2s.crossed(turn)
            dys.crossed(turn)
        hidden(blocks[turn])
        if turn:
            add_up(turn - 1, blocks[turn - 1])
        back(blocks[turn])
        share(turn, blocks[turn])
        if turn + 2 < zs:
            dys.step(turn + 2)
            s2s.step(turn + 2)
    add_up(zs - 1, blocks[zs - 1])
    for turn in range(1, zs):
        send_line(1, turn)
    for done in w_sent:
        done()

    f_order = [step for step in range(1, zs)] + [0]
    y_order = list(range(1, ys)) + [0]
    send_x, send_y, attn_y, attn_z, ffn_z = {}, {}, {}, {}, {}

    def f_rows(z_at, y_at, x_at):
        return index(z_at, y_at, x_at, 0) * rows

    def grad_ffn(step, hop_y):
        z_at, y_at = shifted(z, step, zs), shifted(y, hop_y, ys)

        def tile(n, carry):
            cols = pl.ds(pl.multiple_of((z_at * ys + y_at) * slab + n * LANES, LANES), LANES)
            w_v[cols, pl.ds(0, 2 * block)] = dot_tn(s2_v[:, cols], dgu_v[...]).astype(low)
            w_v[cols, pl.ds(2 * block, block)] = dot_tn(dy_v[:, cols], hid_v[...]).astype(low)
            return carry

        lax.fori_loop(0, slab // LANES, tile, 0)

    def x_slot(hop, z_at, y_at):
        return (((hop - 1) * zs + z_at) * ys + y_at) * 2 * rows

    def grad_send_x(step, hop_y):
        z_at, y_at = shifted(z, step, zs), shifted(y, hop_y, ys)
        for hop in range(1, xs):
            x_at = shifted(x, hop, xs)
            slot = send_x[step, hop_y, hop] = wires.slot()
            wires.start(
                slot,
                w_v.at[rows_at(f_rows(z_at, y_at, x_at), 2 * rows)],
                x_f.at[rows_at(x_slot(hop, z_at, y_at), 2 * rows)],
                here.device(x=x_at),
            )

    def f_across(step):
        z_at = shifted(z, step, zs)
        for hop_y in y_order:
            y_at = shifted(y, hop_y, ys)
            sources = []
            for hop in range(1, xs):
                start = x_slot(hop, z_at, y_at)
                wires.arrive(
                    send_x[step, hop_y, hop],
                    x_f.at[rows_at(start, 2 * rows)],
                    here.device(x=shifted(x, -hop, xs)),
                )
                sources.append((x_f, start))
            add(w_v, f_rows(z_at, y_at, x), sources, 2 * rows)
            if hop_y:
                slot = send_y[step, hop_y] = wires.slot()
                wires.start(
                    slot,
                    w_v.at[rows_at(f_rows(z_at, y_at, x), 2 * rows)],
                    y_f.at[rows_at(((hop_y - 1) * zs + z_at) * 2 * rows, 2 * rows)],
                    here.device(y=y_at),
                )

    def f_out(step):
        z_at = shifted(z, step, zs)
        sources = []
        for hop in range(1, ys):
            start = ((hop - 1) * zs + z_at) * 2 * rows
            wires.arrive(
                send_y[step, hop],
                y_f.at[rows_at(start, 2 * rows)],
                here.device(y=shifted(y, -hop, ys)),
            )
            sources.append((y_f, start))
        add(w_v, f_rows(z_at, y, x), sources, 2 * rows)
        for core in range(2):
            to_c = lax.rem(c + core, 2)
            source = w_v.at[rows_at(f_rows(z_at, y, x) + to_c * rows, rows)]
            target = out_f.at[z * 2 + c]
            if step == 0 and core == 0:
                keep(source, target)
            else:
                slot = ffn_z[step, core] = wires.slot()
                wires.start(slot, source, target, here.device(z=z_at, c=to_c))

    early = 2
    all_blocks = [(step, hop_y) for step in f_order for hop_y in y_order]
    for step, hop_y in all_blocks[:early]:
        grad_ffn(step, hop_y)
        grad_send_x(step, hop_y)
    for step, hop_y in all_blocks[early:]:
        grad_ffn(step, hop_y)

    collect_line(0)

    def dmiddle_rows(at, first):
        ds2 = line_total(0, first)
        middle = mid_v[at, :]
        inverse = inv_v[at, :][:, :1]
        s2 = middle * inverse
        grad = dy_v[at16(my_s2 + first), :].astype(f32) + inverse * (
            ds2 - s2 * jnp.mean(ds2 * s2, axis=1, keepdims=True)
        )
        input_grad[at, :] = grad.astype(low)

    each_rows(toks, dmiddle_rows)

    dbr_v = pr_v

    def dbr_view(x_at, c_at):
        return dbr_v.at[part_rows(x_at, c_at)]

    own_copy = keep(input_grad, dbr_view(x, c))
    dbr_cross = [wires.slot() for step in range(xs)]
    dbr_core = [wires.slot() for step in range(xs)]
    dbr_sent = [wires.start(dbr_core[0], input_grad, dbr_view(x, c), sibling)]
    for step in range(1, xs):
        there = here.device(x=shifted(x, step, xs))
        dbr_sent.append(wires.start(dbr_cross[step], input_grad, dbr_view(x, c), there))
    for step, hop_y in all_blocks[early:]:
        grad_send_x(step, hop_y)
    for step in range(1, xs):
        from_x = shifted(x, -step, xs)
        view = dbr_view(from_x, c)
        wires.arrive(dbr_cross[step], view, here.device(x=from_x))
        wires.start(dbr_core[step], view, view, sibling)
    f_across(f_order[0])
    own_copy.wait()
    for step in range(xs):
        wires.arrive(dbr_core[step], dbr_view(shifted(x, -step, xs), 1 - c), sibling)

    da_v, dpr_v = hid_v, dgu_v
    qkv_rows = pl.ds(0, seq)

    def dattended_tile(n, carry):
        at = rows_at(lax.rem(n, row_blocks) * width, width)
        start = n // row_blocks * width
        cols = pl.ds(pl.multiple_of(start, width), width)
        w_cols = pl.ds(pl.multiple_of(proj + start, width), width)
        da_v[at, cols] = dot_nn(dbr_v[at, :], wa[:, w_cols]).astype(low)
        return carry

    lax.fori_loop(0, row_blocks * (heads // width), dattended_tile, 0)

    def grad_out_tile(n, carry):
        cols = pl.ds(pl.multiple_of(n * width, width), width)
        wa[cols, out_cols] = dot_tn(dbr_v[:, cols], att_v[...]).astype(low)
        return carry

    for done in qkv.sent + outw.sent:
        done()
    lax.fori_loop(0, MODEL // width, grad_out_tile, 0)

    def y_slot(hop, z_at):
        return ((hop - 1) * zs + z_at) * slab

    def attn_send_y(part, cols):
        for step in f_order:
            z_at = shifted(z, step, zs)
            for hop in range(1, ys):
                y_at = shifted(y, hop, ys)
                slot = attn_y[part, step, hop] = wires.slot()
                wires.start(
                    slot,
                    wa.at[rows_at((z_at * ys + y_at) * slab, slab), cols],
                    y_a.at[rows_at(y_slot(hop, z_at), slab), cols],
                    here.device(y=y_at),
                )

    attn_send_y(0, out_cols)

    dkv_v[...] = jnp.zeros_like(dkv_v)

    def attend_back(step, carry):
        at = rows_at(lax.rem(step, row_blocks) * width, width)
        cols = pl.ds(pl.multiple_of(step // row_blocks * HEAD_DIM, HEAD_DIM), HEAD_DIM)
        exponent, total = weights_of(at, cols, lax.rem(step, row_blocks) * width)
        prob = exponent / total
        dout = da_v[at, cols]
        delta = jnp.sum(dout.astype(f32) * att_v[at, cols].astype(f32), axis=1, keepdims=True)
        dprob = dot_nt(dout, kv_v[:, HEAD_DIM:])
        dscore = (prob * (dprob - delta)).astype(low)
        dquery = dot_nn(dscore, kv_v[:, :HEAD_DIM]) * scale
        dpr_v[at, cols] = turned(dquery, at, -1.0).astype(low)
        dkv_v[:, :HEAD_DIM] += dot_tn(dscore, q_v[at, cols]) * scale
        dkv_v[:, HEAD_DIM:] += dot_tn(prob.astype(low), dout)
        return carry

    lax.fori_loop(0, row_blocks * (heads // HEAD_DIM), attend_back, 0)
    mine = rows_at(here.fs * toks, toks)
    dkv_v[mine, :] += kv_grad[...].astype(f32)

    def dkv_rows(step, carry):
        at = rows_at(step * width, width)
        dpr_v[at, pl.ds(heads, HEAD_DIM)] = turned(dkv_v[at, :HEAD_DIM], at, -1.0).astype(low)
        dpr_v[at, pl.ds(heads + HEAD_DIM, HEAD_DIM)] = dkv_v[at, HEAD_DIM:].astype(low)
        return carry

    lax.fori_loop(0, row_blocks, dkv_rows, 0)
    dn1_v = s2_v

    def dn1_tile(n, carry):
        cols = pl.ds(pl.multiple_of(n * width, width), width)
        dn1_v[pl.ds(0, seq), cols] = dot_nt(dpr_v[qkv_rows, qkv_cols], wa[cols, qkv_cols]).astype(low)
        return carry

    for done in s2s.sent:
        done()
    lax.fori_loop(0, MODEL // width, dn1_tile, 0)

    def grad_qkv_tile(n, carry):
        cols = pl.ds(pl.multiple_of(n * width, width), width)
        wa[cols, qkv_cols] = dot_tn(tok_v[:, cols], dpr_v[qkv_rows, qkv_cols]).astype(low)
        return carry

    lax.fori_loop(0, MODEL // width, grad_qkv_tile, 0)
    attn_send_y(1, qkv_cols)
    across, across_sent = reduce_sequence(dn1_v)

    def a_across(step):
        z_at = shifted(z, step, zs)
        sources = []
        for hop in range(1, ys):
            start = y_slot(hop, z_at)
            for part, cols in enumerate((out_cols, qkv_cols)):
                wires.arrive(
                    attn_y[part, step, hop],
                    y_a.at[rows_at(start, slab), cols],
                    here.device(y=shifted(y, -hop, ys)),
                )
            sources.append((y_a, start))
        add(wa, (z_at * ys + y) * slab, sources, slab)
        if step:
            slot = attn_z[step] = wires.slot()
            wires.start(
                slot,
                wa.at[rows_at((z_at * ys + y) * slab, slab)],
                z_a.at[rows_at((step - 1) * slab, slab)],
                here.device(z=z_at),
            )

    for turn, step in enumerate(f_order):
        if turn:
            f_across(step)
            f_out(f_order[turn - 1])
        a_across(step)
    sources = []
    for step in range(1, zs):
        start = (step - 1) * slab
        wires.arrive(
            attn_z[step], z_a.at[rows_at(start, slab)], here.device(z=shifted(z, -step, zs))
        )
        sources.append((z_a, start))
    add(wa, (z * ys + y) * slab, sources, slab)
    attn_f = {}
    for step in range(fsdp):
        other = shifted(here.fs, step, fsdp)
        source = wa.at[rows_at((here.dp * fsdp + other) * rows, rows)]
        target = out_a.at[here.fs]
        if step:
            slot = attn_f[step] = wires.slot()
            wires.start(slot, source, target, (here.dp, other))
        else:
            keep(source, target)
    f_out(f_order[-1])

    collect_line(1)

    def mixed_rows(at, first):
        mixed[at, :] = (mid_v[at, :] + line_total(1, first)).astype(low)

    each_rows(toks, mixed_rows)
    sequence_arrive(across)

    def input_rows(at, first):
        ds1 = sequence_total(first)
        values = tokens[at, :].astype(f32)
        inverse = lax.rsqrt(jnp.mean(values * values, axis=1, keepdims=True) + EPSILON)
        s1 = values * inverse
        back = inverse * (ds1 - s1 * jnp.mean(ds1 * s1, axis=1, keepdims=True))
        input_grad[at, :] = (input_grad[at, :].astype(f32) + back).astype(low)

    for done in dbr_sent:
        done()
    each_rows(toks, input_rows)
    for step in range(1, fsdp):
        other = shifted(here.fs, -step, fsdp)
        wires.arrive(attn_f[step], out_a.at[other], (here.dp, other))
    for step in range(zs):
        from_z = shifted(z, -step, zs)
        for core in range(2):
            if step or core:
                from_c = lax.rem(c + core, 2)
                wires.arrive(
                    ffn_z[step, core],
                    out_f.at[from_z * 2 + from_c],
                    here.device(z=from_z, c=from_c),
                )
    for copy in locals_[first_local + 1 :]:
        copy.wait()
    wires.drain()


def whole_block(place, w_qkv, w_out, w_gateup, w_down, tokens, dy, kv_grad, cos_t, sin_t, key_at):
    toks = tokens.shape[0]
    zs, ys, xs, fsdp, rows = place.zs, place.ys, place.xs, place.fsdp, place.rows
    heads = place.heads
    seq = toks * fsdp
    every = zs * 2 * toks
    slab = fsdp * rows
    low, f32 = jnp.bfloat16, jnp.float32
    count = place.copies
    vmem = pl.BlockSpec(memory_space=pltpu.VMEM)
    hbm = pl.BlockSpec(memory_space=ANY)
    return pl.pallas_call(
        functools.partial(block_kernel, place),
        out_shape=(
            jax.ShapeDtypeStruct((toks, MODEL), low),
            jax.ShapeDtypeStruct((toks, KV), low),
            jax.ShapeDtypeStruct((toks, MODEL), low),
            jax.ShapeDtypeStruct((2 * zs, rows, place.ffn_width), low),
            jax.ShapeDtypeStruct((fsdp, rows, place.attn_width), low),
        ),
        in_specs=[hbm] * 4 + [vmem, hbm] + [vmem] * 4,
        out_specs=(vmem, vmem, vmem, hbm, hbm),
        scratch_shapes=[
            pltpu.VMEM((MODEL, place.attn_width), low),
            pltpu.VMEM((MODEL, place.ffn_width), low),
            pltpu.VMEM((seq, MODEL), low),
            pltpu.VMEM((every, MODEL), low),
            pltpu.VMEM((every, MODEL), low),
            pltpu.VMEM((every, place.block), low),
            pltpu.VMEM((every, 2 * place.block), low),
            pltpu.VMEM((seq, MODEL), low),
            pltpu.VMEM((xs * toks, MODEL), low),
            pltpu.VMEM((xs * toks, MODEL), low),
            pltpu.VMEM((toks, MODEL), f32),
            pltpu.VMEM((toks, LANES), f32),
            pltpu.VMEM((zs * toks, MODEL), low),
            pltpu.VMEM((zs * toks, MODEL), low),
            pltpu.VMEM(((zs - 1) * toks, MODEL), low),
            pltpu.VMEM(((zs - 1) * toks, MODEL), low),
            pltpu.VMEM((seq, heads), low),
            pltpu.VMEM((seq, KV), low),
            pltpu.VMEM((seq, heads), low),
            pltpu.VMEM((seq, KV), f32),
            pltpu.VMEM(((xs - 1) * zs * ys * 2 * rows, place.ffn_width), low),
            pltpu.VMEM(((ys - 1) * zs * 2 * rows, place.ffn_width), low),
            pltpu.VMEM(((ys - 1) * zs * slab, place.attn_width), low),
            pltpu.VMEM(((zs - 1) * slab, place.attn_width), low),
            pltpu.SemaphoreType.DMA((16,)),
            pltpu.SemaphoreType.DMA((count,)),
            pltpu.SemaphoreType.DMA((count,)),
        ],
        compiler_params=pltpu.CompilerParams(
            collective_id=0, has_side_effects=True, vmem_limit_bytes=63 * 2**20 + 2**19
        ),
        name="whole_block",
    )(w_qkv, w_out, w_gateup, w_down, tokens, dy, kv_grad, cos_t, sin_t, key_at)


def on_device(
    place, tokens, lengths, gain_attn, w_qkv, w_out, gain_ffn, w_gateup, w_down, out_grad, kv_grad
):
    toks = tokens.shape[0]
    fsdp = place.fsdp
    seq = toks * fsdp
    low = jnp.bfloat16
    f32 = jnp.float32
    group = lax.axis_index("dp")
    length = jnp.sum(
        jnp.where(jnp.arange(lengths.shape[0], dtype=jnp.int32) == group, lengths, 0)
    )
    slots = np.arange(seq)
    at = slots % toks * fsdp + slots // toks
    frequency = THETA ** (-np.arange(HEAD_DIM // 2, dtype=np.float64) * (2.0 / HEAD_DIM))
    angles = at[:, None] * frequency[None, :]
    cos_t = jnp.asarray(np.tile(np.cos(angles), (1, 2)), f32)
    sin_t = jnp.asarray(np.concatenate([-np.sin(angles), np.sin(angles)], axis=1), f32)
    positions = jnp.asarray(at, jnp.int32)
    key_at = jnp.where(positions < length, positions, seq)
    key_at = jnp.broadcast_to(key_at[None, :], (8, seq))

    gain_a = gain_attn.astype(f32)[:, None]
    gain_f = gain_ffn.astype(f32)[:, None]
    folded_qkv = (w_qkv.astype(f32) * gain_a).astype(low)
    folded_gateup = (w_gateup.astype(f32) * gain_f).astype(low)
    mixed, shared_kv, input_grad, out_f, out_a = whole_block(
        place, folded_qkv, w_out, folded_gateup, w_down, tokens, out_grad, kv_grad,
        cos_t, sin_t, key_at,
    )

    heads, block = place.heads, place.block
    duplicate = 2 * block - place.zone
    out_f = out_f.astype(f32)
    out_a = out_a.astype(f32)

    def columns(start):
        pieces = []
        for z_at in range(place.zs):
            pieces.append(out_f[2 * z_at, :, start : start + block])
            pieces.append(out_f[2 * z_at + 1, :, start + duplicate : start + block])
        return pieces

    plain_gateup = jnp.concatenate(columns(0) + columns(block), axis=1)
    grad_down = jnp.concatenate(columns(2 * block), axis=1)
    plain_qkv = jnp.concatenate(
        [out_a[at, :, :heads] for at in range(fsdp)]
        + [jnp.sum(out_a[:, :, heads : heads + KV], axis=0)],
        axis=1,
    )
    grad_out = jnp.concatenate([out_a[at, :, heads + KV :] for at in range(fsdp)], axis=1)
    grad_gain_attn = jnp.sum(w_qkv.astype(f32) * plain_qkv, axis=1)
    grad_gain_ffn = jnp.sum(w_gateup.astype(f32) * plain_gateup, axis=1)
    return (
        mixed,
        shared_kv,
        input_grad,
        grad_gain_attn,
        plain_qkv * gain_a,
        grad_out,
        grad_gain_ffn,
        plain_gateup * gain_f,
        grad_down,
    )


def solution(mesh):
    place = Place(mesh.shape["dp"], mesh.shape["fsdp"])
    row = P(("dp", "fsdp"), None)
    line = P(("dp", "fsdp"))
    return jax.shard_map(
        functools.partial(on_device, place),
        mesh=mesh,
        in_specs=(row, P(), line, row, row, line, row, row, row, row),
        out_specs=(row, row, row, line, row, row, line, row, row),
        check_vma=False,
    )
```

```python
import functools

import jax
import jax.numpy as jnp
import numpy as np
from jax import lax
from jax.experimental import pallas as pl
from jax.experimental.pallas import tpu as pltpu
from jax.sharding import PartitionSpec as P

HEADS = 16
HEAD_DIM = 128
FF = 5632
HQ = 2048
MODEL = 2048
KV = 2 * HEAD_DIM
LANES = 128

EPSILON = 1e-05
THETA = 10000.0
MASKED = -1e30
MESH = pl.DeviceIdType.MESH
ANY = pl.ANY


class Place:
    def __init__(self, dp_count, fsdp_count):
        self.fsdp = fsdp_count
        self.xs = fsdp_count // 2
        self.ys = self.xs
        self.zs = dp_count // self.ys
        self.rows = MODEL // (dp_count * fsdp_count)
        self.heads = HQ // fsdp_count
        self.attn_width = 2 * self.heads + KV
        self.zone = FF // self.zs
        self.block = LANES * -(-(self.zone // LANES) // 2)
        self.ffn_width = 3 * self.block
        zs, ys, xs, fsdp = self.zs, self.ys, self.xs, self.fsdp
        across = (ys - 1) + (xs - 1)
        line = 2 * (zs - 1)
        self.copies = (
            3 * (fsdp - 1) + 3 * (2 * zs - 1) + 2 * (line + (2 * zs - 1) * (ys - 1))
            + 2 * (line + 2 * zs - 1) + 2 * xs + 2 * (2 * xs - 1) + 2 * zs + 9 * line
            + 2 * zs * max(across + xs * (ys - 1), across + ys * (xs - 1))
            + 2 * zs * (ys - 1) + 2 * zs - 1 + fsdp - 1 + 2 * xs
        )


class Here:
    def __init__(self, place):
        self.place = place
        self.dp = lax.axis_index("dp")
        self.fs = lax.axis_index("fsdp")
        self.z = self.dp // place.ys
        self.y = lax.rem(self.dp, place.ys)
        self.x = self.fs // 2
        self.c = lax.rem(self.fs, 2)

    def device(self, z=None, y=None, x=None, c=None):
        z = self.z if z is None else z
        y = self.y if y is None else y
        x = self.x if x is None else x
        c = self.c if c is None else c
        return (z * self.place.ys + y, x * 2 + c)

    def sibling(self):
        return self.device(c=1 - self.c)


def shifted(value, step, count):
    return lax.rem(value + (step + count), count)


def rows_at(start, count):
    return pl.ds(pl.multiple_of(start, count), count)


def cols_at(start, count):
    return pl.ds(pl.multiple_of(start, LANES), count)


class Wires:
    def __init__(self, send, recv):
        self.send = send
        self.recv = recv
        self.used = 0
        self.finish = []

    def slot(self):
        self.used += 1
        return self.used - 1

    def copy(self, slot, source, target, device):
        return pltpu.make_async_remote_copy(
            src_ref=source,
            dst_ref=target,
            send_sem=self.send.at[slot],
            recv_sem=self.recv.at[slot],
            device_id=device,
            device_id_type=MESH,
        )

    def start(self, slot, source, target, device, when=None):
        copy = self.copy(slot, source, target, device)
        if when is None:
            copy.start()
            wait = copy.wait_send
        else:
            pl.when(when)(copy.start)

            def wait():
                pl.when(when)(copy.wait_send)

        self.finish.append(wait)

        def done():
            self.finish.remove(wait)
            wait()

        return done

    def arrive(self, slot, target, device, when=None):
        copy = self.copy(slot, target, target, device)
        if when is None:
            copy.wait_recv()
        else:
            pl.when(when)(copy.wait_recv)

    def drain(self):
        for wait in self.finish:
            wait()
        self.finish = []


def greet(devices):
    barrier = pltpu.get_barrier_semaphore()
    for device in devices:
        pl.semaphore_signal(barrier, inc=1, device_id=device, device_id_type=MESH)
    pl.semaphore_wait(barrier, len(devices))


def line_partners(here):
    place = here.place
    return [here.device(z=shifted(here.z, step, place.zs)) for step in range(1, place.zs)]


def plane_partners(here):
    place = here.place
    return [here.device(y=shifted(here.y, step, place.ys)) for step in range(1, place.ys)] + [
        here.device(x=shifted(here.x, step, place.xs)) for step in range(1, place.xs)
    ]


class Line:
    def __init__(self, wires, here, view):
        self.wires = wires
        self.here = here
        self.view = view
        count = here.place.zs
        self.count = count
        self.up = [wires.slot() for step in range(count - 1)]
        self.down = [wires.slot() for step in range(count - 1)]

    def send(self, step):
        here, count = self.here, self.count
        if step >= count - 1:
            return []
        z = here.z
        low = lax.max(z - step, 0)
        high = lax.min(z + step, count - 1)
        up = self.wires.start(
            self.up[step],
            self.view(low),
            self.view(low),
            here.device(z=lax.min(z + 1, count - 1)),
            when=(z >= step) & (z < count - 1),
        )
        down = self.wires.start(
            self.down[step],
            self.view(high),
            self.view(high),
            here.device(z=lax.max(z - 1, 0)),
            when=(z + step < count) & (z > 0),
        )
        return [up, down]

    def arrive(self, step):
        here, count = self.here, self.count
        z = here.z
        low = lax.max(z - step, 0)
        high = lax.min(z + step, count - 1)
        self.wires.arrive(
            self.up[step - 1], self.view(low), here.device(z=lax.max(z - 1, 0)), when=z >= step
        )
        self.wires.arrive(
            self.down[step - 1],
            self.view(high),
            here.device(z=lax.min(z + 1, count - 1)),
            when=z + step < count,
        )

    def valid(self, step):
        z = self.here.z
        if step == 0:
            return [(z, None)]
        return [
            (lax.max(z - step, 0), z >= step),
            (lax.min(z + step, self.count - 1), z + step < self.count),
        ]


def each_rows(count, body, size=16):
    def step(index, carry):
        body(pl.ds(pl.multiple_of(index * size, size), size), index * size)
        return carry

    lax.fori_loop(0, count // size, step, 0)


def dot_nn(left, right):
    return lax.dot_general(
        left, right, (((1,), (0,)), ((), ())), preferred_element_type=jnp.float32
    )


def dot_nt(left, right):
    return lax.dot_general(
        left, right, (((1,), (1,)), ((), ())), preferred_element_type=jnp.float32
    )


def dot_tn(left, right):
    return lax.dot_general(
        left, right, (((0,), (0,)), ((), ())), preferred_element_type=jnp.float32
    )


def visit_order(count):
    orders = []
    for z in range(count):
        far = sorted(range(count), key=lambda other: (abs(other - z), other))
        orders.append(far)
    return orders


def chosen(z, turn, orders):
    total = 0
    for z_at, order in enumerate(orders):
        here = jnp.where(z == z_at, 1, 0)
        for turn_at, value in enumerate(order):
            if isinstance(turn, int):
                if turn == turn_at:
                    total = total + here * value
            else:
                total = total + here * jnp.where(turn == turn_at, 1, 0) * value
    return total


def block_kernel(
    place, w_qkv, w_out, w_gateup, w_down, tokens, dy, kv_grad, rope, key_at,
    mixed, shared_kv, input_grad, out_f, out_a,
    wa, w_v, tok_v, dy_v, s2_v, hid_v, dgu_v, pr_v, ps_v, px_v, mid_v, inv_v,
    so_v, sd_v, z_land, q_v, kv_v, att_v, dkv_v,
    x_f, y_f, y_a, z_a, local, send, recv, credit,
):
    here = Here(place)
    wires = Wires(send, recv)
    z, y, x, c = here.z, here.y, here.x, here.c
    zs, ys, xs, fsdp, rows = place.zs, place.ys, place.xs, place.fsdp, place.rows
    heads, block, zone = place.heads, place.block, place.zone
    proj = heads + KV
    toks = tokens.shape[0]
    seq = toks * fsdp
    pair = 2 * toks
    slab = fsdp * rows
    width = 256
    low = jnp.bfloat16
    f32 = jnp.float32
    scale = HEAD_DIM ** (-0.5)
    sibling = here.sibling()
    partners = line_partners(here) + plane_partners(here)
    partners += [here.device(x=shifted(x, step, xs), c=1 - c) for step in range(xs)]
    partners += [here.device(z=shifted(z, step, zs), c=1 - c) for step in range(1, zs)]
    greet(partners)

    def index(z=z, y=y, x=x, c=c):
        return (z * ys + y) * fsdp + x * 2 + c

    locals_ = []

    def keep(source, target):
        copy = pltpu.make_async_copy(source, target, local.at[len(locals_)])
        copy.start()
        locals_.append(copy)
        return copy

    def at16(start):
        return pl.ds(pl.multiple_of(start, 16), 16)

    def add(target, start, sources, count, cols=slice(None)):
        def step(at, first):
            at = at16(start + first)
            total = target[at, cols].astype(f32)
            for source, source_start in sources:
                total = total + source[at16(source_start + first), cols].astype(f32)
            target[at, cols] = total.astype(low)

        each_rows(count, step)

    own_rows = rows_at(index() * rows, rows)
    qkv_cols, out_cols = pl.ds(0, proj), pl.ds(proj, heads)

    def qkv_pieces(owner):
        return [(w_qkv, owner * heads, heads, 0), (w_qkv, HQ, KV, heads)]

    def out_pieces(owner):
        return [(w_out, owner * heads, heads, proj)]

    def attn_spread(pieces):
        slots = []
        for step in range(1, fsdp):
            other = shifted(here.fs, step, fsdp)
            for ref, start, count, place_at in pieces(other):
                slot = wires.slot()
                slots.append((slot, step, count, place_at))
                wires.start(
                    slot,
                    ref.at[:, cols_at(start, count)],
                    wa.at[own_rows, pl.ds(place_at, count)],
                    (here.dp, other),
                )
        for ref, start, count, place_at in pieces(here.fs):
            keep(ref.at[:, cols_at(start, count)], wa.at[own_rows, pl.ds(place_at, count)])
        return slots

    def attn_collect(slots):
        for slot, step, count, place_at in slots:
            other = shifted(here.fs, -step, fsdp)
            at = rows_at((here.dp * fsdp + other) * rows, rows)
            wires.arrive(slot, wa.at[at, pl.ds(place_at, count)], (here.dp, other))

    def ffn_pieces(zone_z, core):
        start = zone_z * zone + core * (zone - block)
        return [(w_gateup, start, 0), (w_gateup, FF + start, block), (w_down, start, 2 * block)]

    ffn_slots = {}

    def ffn_spread(step):
        for core in range(2):
            to_z, to_c = shifted(z, step, zs), lax.rem(c + core, 2)
            for ref, start, place_at in ffn_pieces(to_z, to_c):
                source = ref.at[:, cols_at(start, block)]
                target = w_v.at[own_rows, pl.ds(place_at, block)]
                if step == 0 and core == 0:
                    keep(source, target)
                    continue
                slot = wires.slot()
                ffn_slots.setdefault(step, []).append((slot, core, place_at))
                wires.start(slot, source, target, here.device(z=to_z, c=to_c))

    def ffn_collect(step):
        from_z = shifted(z, -step, zs)
        for slot, core, place_at in ffn_slots[step]:
            from_c = lax.rem(c + core, 2)
            at = rows_at(index(z=from_z, c=from_c) * rows, rows)
            wires.arrive(slot, w_v.at[at, pl.ds(place_at, block)], here.device(z=from_z, c=from_c))

    def w_view(z_at, y_at, x_at):
        return w_v.at[rows_at(index(z_at, y_at, x_at, 0) * rows, 2 * rows)]

    near, far = {}, {}
    w_sent = []

    def axes(step):
        ways = [("y", y, ys), ("x", x, xs)]
        return ways if step else ways[::-1]

    def at_plane(name, value, other):
        return {"y_at": value, "x_at": other} if name == "y" else {"y_at": other, "x_at": value}

    def to_plane(name, value):
        return here.device(y=value) if name == "y" else here.device(x=value)

    def ffn_send(slots, key, name, me, count, view):
        for hop in range(1, count):
            slot = slots[key + (hop,)] = wires.slot()
            w_sent.append(wires.start(slot, view, view, to_plane(name, shifted(me, hop, count))))

    def ffn_near(step):
        z_at = shifted(z, -step, zs)
        first, me, count = axes(step)[0]
        ffn_send(near, (step,), first, me, count, w_view(z_at, y, x))

    def ffn_far(step):
        z_at = shifted(z, -step, zs)
        second, me, count = axes(step)[1]
        ffn_send(far, (step, 0), second, me, count, w_view(z_at, y, x))

    def ffn_forward(step):
        ffn_collect(step)
        ffn_near(step)
        ffn_far(step)

    def ffn_across(step):
        z_at = shifted(z, -step, zs)
        (first, me, count), (second, me2, count2) = axes(step)
        for hop in range(1, count):
            origin = shifted(me, -hop, count)
            view = w_view(z_at, **at_plane(first, origin, me2))
            wires.arrive(near[step, hop], view, to_plane(first, origin))
            ffn_send(far, (step, hop), second, me2, count2, view)

    def ffn_arrive(step):
        z_at = shifted(z, -step, zs)
        (first, me, count), (second, me2, count2) = axes(step)
        for hop in range(count):
            for hop2 in range(1, count2):
                origin, origin2 = shifted(me, -hop, count), shifted(me2, -hop2, count2)
                view = w_view(z_at, **at_plane(first, origin, origin2))
                wires.arrive(far[step, hop, hop2], view, to_plane(second, origin2))

    class Spread:
        def __init__(self, cols):
            self.cols = cols
            self.line = Line(wires, here, lambda z_at: self.view(z_at, y))
            self.plane = {}
            self.sent = []

        def view(self, z_at, y_at):
            return wa.at[rows_at((z_at * ys + y_at) * slab, slab), self.cols]

        def step(self, step):
            if step:
                self.line.arrive(step)
            self.sent += self.line.send(step)
            for side, (z_at, exists) in enumerate(self.line.valid(step)):
                for hop in range(1, ys):
                    slot = self.plane[step, side, hop] = wires.slot()
                    view = self.view(z_at, y)
                    there = here.device(y=shifted(y, hop, ys))
                    self.sent.append(wires.start(slot, view, view, there, when=exists))

        def crossed(self):
            for step in range(zs):
                for side, (z_at, exists) in enumerate(self.line.valid(step)):
                    for hop in range(1, ys):
                        from_y = shifted(y, -hop, ys)
                        wires.arrive(
                            self.plane[step, side, hop],
                            self.view(z_at, from_y),
                            here.device(y=from_y),
                            when=exists,
                        )

    class Acts:
        def __init__(self, ref):
            self.ref = ref
            self.line = Line(wires, here, lambda z_at: self.view(z_at, c))
            self.core = {}
            self.sent = []

        def view(self, z_at, c_at):
            return self.ref.at[rows_at((z_at * 2 + c_at) * toks, toks)]

        def step(self, step):
            if step:
                self.line.arrive(step)
            self.sent += self.line.send(step)
            for side, (z_at, exists) in enumerate(self.line.valid(step)):
                slot = self.core[step, side] = wires.slot()
                view = self.view(z_at, c)
                self.sent.append(wires.start(slot, view, view, sibling, when=exists))

        def crossed(self, step):
            for side, (z_at, exists) in enumerate(self.line.valid(step)):
                wires.arrive(self.core[step, side], self.view(z_at, 1 - c), sibling, when=exists)

    def tok_view(x_at, c_at):
        return tok_v.at[rows_at((x_at * 2 + c_at) * toks, toks)]

    qkv_slots = attn_spread(qkv_pieces)
    ffn_spread(0)
    ffn_spread(1)
    keep(tokens, tok_view(x, c))
    tok_cross = [wires.slot() for step in range(xs)]
    tok_core = [wires.slot() for step in range(xs)]
    wires.start(tok_core[0], tokens, tok_view(x, c), sibling)
    for step in range(1, xs):
        wires.start(
            tok_cross[step], tokens, tok_view(x, c), here.device(x=shifted(x, step, xs))
        )
    out_slots = attn_spread(out_pieces)
    dys = Acts(dy_v)
    keep(dy, dys.view(z, c))
    for copy in locals_:
        copy.wait()
    first_local = len(locals_)
    ffn_collect(0)
    ffn_near(0)
    attn_collect(qkv_slots)
    qkv = Spread(qkv_cols)
    qkv.step(0)
    attn_collect(out_slots)
    outw = Spread(out_cols)
    outw.step(0)
    ffn_collect(1)
    ffn_far(1)
    tok_sent = []
    for step in range(1, xs):
        from_x = shifted(x, -step, xs)
        view = tok_view(from_x, c)
        wires.arrive(tok_cross[step], view, here.device(x=from_x))
        tok_sent.append(wires.start(tok_core[step], view, view, sibling))
    qkv.step(1)
    outw.step(1)
    for step in range(xs):
        from_x = shifted(x, -step, xs)
        wires.arrive(tok_core[step], tok_view(from_x, 1 - c), sibling)
    for done in tok_sent:
        done()

    def norm_rows(at, first):
        values = tok_v[at, :].astype(f32)
        inverse = lax.rsqrt(jnp.mean(values * values, axis=1, keepdims=True) + EPSILON)
        tok_v[at, :] = (values * inverse).astype(low)

    each_rows(seq, norm_rows)
    qkv.step(2)
    outw.step(2)
    late = [zs - 1] + list(range(2, zs - 1))
    for step in late:
        ffn_spread(step)
    dys.step(0)
    for step in range(3, zs):
        qkv.step(step)
        outw.step(step)
    ffn_far(0)
    ffn_across(0)
    ffn_near(1)
    qkv.crossed()

    half = HEAD_DIM // 2

    def turned(values, at, sign):
        table = rope[at, :]
        across = pltpu.roll(table, half, 1)
        low_half = lax.broadcasted_iota(jnp.int32, table.shape, 1) < half
        cosine = jnp.where(low_half, table, across)
        sine_part = jnp.where(low_half, -across, table)
        return values * cosine + pltpu.roll(values, half, 1) * (sign * sine_part)

    row_blocks = seq // width

    def project(step, carry):
        at = rows_at(step * width, width)

        def query_tile(j, carry):
            cols = pl.ds(pl.multiple_of(j * HEAD_DIM, HEAD_DIM), HEAD_DIM)
            q_v[at, cols] = turned(dot_nn(tok_v[at, :], wa[:, cols]), at, 1.0).astype(low)
            return carry

        lax.fori_loop(0, heads // HEAD_DIM, query_tile, 0)
        both = dot_nn(tok_v[at, :], wa[:, pl.ds(heads, KV)])
        kv_v[at, :HEAD_DIM] = turned(both[:, :HEAD_DIM], at, 1.0).astype(low)
        kv_v[at, HEAD_DIM:] = both[:, HEAD_DIM:].astype(low)
        return carry

    lax.fori_loop(0, row_blocks, project, 0)
    shared_kv[...] = kv_v[rows_at(here.fs * toks, toks), :]

    def weights_of(at, cols, first):
        scores = dot_nt(q_v[at, cols], kv_v[:, :HEAD_DIM]) * scale
        row = lax.broadcasted_iota(jnp.int32, (width, LANES), 0) + first
        query_at = lax.rem(row, toks) * fsdp + row // toks
        allowed = key_at[0:1, :] <= query_at[:, :1]
        scores = jnp.where(allowed, scores, MASKED)
        exponent = jnp.exp(scores - jnp.max(scores, axis=1, keepdims=True))
        return exponent, jnp.sum(exponent, axis=1, keepdims=True)

    def attend(step, carry):
        at = rows_at(lax.rem(step, row_blocks) * width, width)
        cols = pl.ds(pl.multiple_of(step // row_blocks * HEAD_DIM, HEAD_DIM), HEAD_DIM)
        exponent, total = weights_of(at, cols, lax.rem(step, row_blocks) * width)
        att_v[at, cols] = (dot_nn(exponent.astype(low), kv_v[:, HEAD_DIM:]) / total).astype(low)
        return carry

    ffn_forward(late[0])
    lax.fori_loop(0, row_blocks * (heads // HEAD_DIM), attend, 0)
    outw.crossed()

    def branch_tile(n, carry):
        cols = pl.ds(pl.multiple_of(n * width, width), width)
        pr_v[:, cols] = dot_nt(att_v[...], wa[cols, out_cols]).astype(low)
        return carry

    lax.fori_loop(0, MODEL // width, branch_tile, 0)

    def part_rows(x_at, c_at):
        return rows_at((x_at * 2 + c_at) * toks, toks)

    def x_rows(x_at):
        return rows_at(x_at * toks, toks)

    x_order = list(range(1, xs)) + [0]

    def reduce_sequence(source):
        sib = [wires.slot() for step in range(xs)]
        across = {}
        sent = []
        for step in x_order:
            x_at = shifted(x, step, xs)
            sent.append(
                wires.start(
                    sib[step], source.at[part_rows(x_at, 1 - c)], ps_v.at[x_rows(x_at)], sibling
                )
            )
        for step in x_order:
            x_at = shifted(x, step, xs)
            wires.arrive(sib[step], ps_v.at[x_rows(x_at)], sibling)
            add(ps_v, x_at * toks, [(source, (x_at * 2 + c) * toks)], toks)
            if step == x_order[0]:
                for done in sent:
                    done()
            if step:
                across[step] = wires.slot()
                sent.append(
                    wires.start(
                        across[step], ps_v.at[x_rows(x_at)], px_v.at[x_rows(x)], here.device(x=x_at)
                    )
                )
        return across, sent[xs:]

    def sequence_arrive(across):
        for step in range(1, xs):
            from_x = shifted(x, -step, xs)
            wires.arrive(across[step], px_v.at[x_rows(from_x)], here.device(x=from_x))

    def sequence_total(first):
        total = ps_v[at16(x * toks + first), :].astype(f32)
        for step in range(1, xs):
            total = total + px_v[at16(shifted(x, -step, xs) * toks + first), :].astype(f32)
        return total

    across, across_sent = reduce_sequence(pr_v)
    sequence_arrive(across)
    s2s = Acts(s2_v)
    my_s2 = (z * 2 + c) * toks

    def middle_rows(at, first):
        middle = tokens[at, :].astype(f32) + sequence_total(first)
        inverse = lax.rsqrt(jnp.mean(middle * middle, axis=1, keepdims=True) + EPSILON)
        mid_v[at, :] = middle
        inv_v[at, :] = jnp.broadcast_to(inverse, (16, LANES))
        s2_v[at16(my_s2 + first), :] = (middle * inverse).astype(low)

    each_rows(toks, middle_rows)
    s2s.step(0)
    for step in late[1:]:
        ffn_forward(step)
    ffn_across(1)
    dys.step(1)
    ffn_across(late[0])
    s2s.step(1)
    for step in late[1:]:
        ffn_across(step)
    for done in across_sent:
        done()
    for step in range(zs):
        ffn_arrive(step)
    orders = visit_order(zs)
    blocks = [chosen(z, turn, orders) for turn in range(zs)]
    duplicate = 2 * block - zone

    def hidden(b):
        at = rows_at(b * pair, pair)

        def hidden_tile(j, carry):
            def cols(base):
                return pl.ds(pl.multiple_of(base + j * width, width), width)

            gate = dot_nn(s2_v[at, :], w_v[:, cols(0)])
            up = dot_nn(s2_v[at, :], w_v[:, cols(block)])
            dhid = dot_nn(dy_v[at, :], w_v[:, cols(2 * block)])
            sg = 1.0 / (1.0 + jnp.exp(-gate))
            lane = lax.broadcasted_iota(jnp.int32, gate.shape, 1) + j * width
            mine = (lane >= duplicate) | (c == 0)
            act = gate * sg
            hid_v[at, cols(0)] = jnp.where(mine, act * up, 0.0).astype(low)
            dgate = dhid * up * sg * (1.0 + gate * (1.0 - sg))
            dgu_v[at, cols(0)] = jnp.where(mine, dgate, 0.0).astype(low)
            dgu_v[at, cols(block)] = jnp.where(mine, dhid * act, 0.0).astype(low)
            return carry

        lax.fori_loop(0, block // width, hidden_tile, 0)

    pd_v, po_v = px_v, ps_v

    def back(b):
        at = rows_at(b * pair, pair)

        def back_tile(n, carry):
            cols = pl.ds(pl.multiple_of(n * width, width), width)
            pd_v[pl.ds(0, pair), cols] = dot_nt(
                dgu_v[at, :], w_v[cols, pl.ds(0, 2 * block)]
            ).astype(low)
            po_v[pl.ds(0, pair), cols] = dot_nt(hid_v[at, :], w_v[cols, pl.ds(2 * block, block)]).astype(low)
            return carry

        lax.fori_loop(0, MODEL // width, back_tile, 0)

    class Chain:
        def __init__(self, own, own_start, landing, count, pieces, cols=slice(None)):
            self.cols = cols
            self.own, self.own_start, self.landing = own, own_start, landing
            self.count, self.pieces, self.size = count, pieces, count // pieces
            self.slots = {}
            for way in range(2):
                for k in range(1, zs):
                    for piece in range(pieces):
                        self.slots[way, k, piece] = wires.slot()

        def owner(self, way, k):
            return lax.min(z + k, zs - 1) if way == 0 else lax.max(z - k, 0)

        def exists(self, way, k):
            return z + k < zs if way == 0 else z >= k

        def feeds(self, way):
            return z > 0 if way == 0 else z < zs - 1

        def land(self, way, k, piece):
            return (way * (zs - 1) + k - 1) * self.count + piece * self.size

        def copy(self, way, k, piece):
            start = self.own_start(self.owner(way, k)) + piece * self.size
            return wires.copy(
                self.slots[way, k, piece],
                self.own.at[rows_at(start, self.size), self.cols],
                self.landing.at[pl.ds(self.land(way, k, piece), self.size), self.cols],
                here.device(z=self.owner(way, 1)),
            )

        def take(self, way, k, piece):
            land = self.land(way, k + 1, piece)
            view = self.landing.at[pl.ds(land, self.size), self.cols]
            wires.copy(
                self.slots[way, k + 1, piece], view, view, here.device(z=self.owner(1 - way, 1))
            ).wait_recv()
            owner = z if k == 0 else self.owner(way, k)
            start = self.own_start(owner) + piece * self.size
            add(self.own, start, [(self.landing, land)], self.size, self.cols)

        def first(self, way, k):
            @pl.when(jnp.logical_not(self.feeds(way)) & self.exists(way, k))
            def _():
                for piece in range(self.pieces):
                    self.copy(way, k, piece).start()

        def onward(self, way, k):
            if k == zs - 1:
                return

            @pl.when(self.feeds(way) & self.exists(way, k))
            def _():
                for piece in range(self.pieces):
                    self.take(way, k, piece)
                    self.copy(way, k, piece).start()

        def last(self):
            for way in range(2):

                @pl.when(self.feeds(way))
                def _(way=way):
                    for piece in range(self.pieces):
                        self.take(way, 0, piece)

        def drain(self):
            for way in range(2):
                for k in range(1, zs):

                    @pl.when(self.exists(way, k))
                    def _(way=way, k=k):
                        for piece in range(self.pieces):
                            self.copy(way, k, piece).wait_send()

    def line_rows(b):
        return b * toks

    kinds = ((pd_v, sd_v), (po_v, so_v))
    d_chain = Chain(sd_v, line_rows, z_land, toks, 4)
    o_chain = Chain(so_v, line_rows, z_land, toks, 1)
    shares = {}

    def share(turn, b):
        for kind, (buffer, landing) in enumerate(kinds):
            slot = wires.slot()
            done = wires.start(
                slot,
                buffer.at[rows_at((1 - c) * toks, toks)],
                landing.at[rows_at(b * toks, toks)],
                sibling,
            )
            shares[turn, kind] = (slot, done)

    def add_up(turn, b):
        for kind, (buffer, landing) in enumerate(kinds):
            slot, done = shares[turn, kind]
            wires.arrive(slot, landing.at[rows_at(b * toks, toks)], sibling)
            add(landing, b * toks, [(buffer, c * toks)], toks)
            done()
            if turn and kind == 0:
                d_chain.first(0, turn)
                d_chain.first(1, turn)

    relays = [
        (acts, step) for step in range(2, zs) for acts in (dys, s2s)
    ]
    s2s.crossed(0)
    dys.crossed(0)
    for turn in range(zs):
        if turn:
            while relays and relays[0][1] <= turn:
                acts, step = relays.pop(0)
                acts.step(step)
            s2s.crossed(turn)
            dys.crossed(turn)
        hidden(blocks[turn])
        if turn:
            add_up(turn - 1, blocks[turn - 1])
        back(blocks[turn])
        share(turn, blocks[turn])
        if relays:
            acts, step = relays.pop(0)
            acts.step(step)
    add_up(zs - 1, blocks[zs - 1])
    for done in w_sent:
        done()

    f_order = list(range(1, zs)) + [0]
    y_order = list(range(1, ys)) + [0]
    pair_rows = 2 * rows
    first_slots, second_slots, ffn_z = {}, {}, {}

    def y_first(step):
        return step == f_order[0]

    x_base, y_base = {}, {}
    x_used = y_used = 0
    for step in f_order:
        x_base[step], y_base[step] = x_used, y_used
        x_used += (xs - 1) * pair_rows * (1 if y_first(step) else ys)
        y_used += (ys - 1) * pair_rows * (xs if y_first(step) else 1)

    def f_rows(z_at, y_at, x_at):
        return index(z_at, y_at, x_at, 0) * rows

    def grad_ffn(step, hop_y):
        z_at, y_at = shifted(z, step, zs), shifted(y, hop_y, ys)

        def tile(n, carry):
            cols = pl.ds(pl.multiple_of((z_at * ys + y_at) * slab + n * LANES, LANES), LANES)
            w_v[cols, pl.ds(0, 2 * block)] = dot_tn(s2_v[:, cols], dgu_v[...]).astype(low)
            w_v[cols, pl.ds(2 * block, block)] = dot_tn(dy_v[:, cols], hid_v[...]).astype(low)
            return carry

        lax.fori_loop(0, slab // LANES, tile, 0)

    def f_send(step, hop_y):
        z_at, y_at = shifted(z, step, zs), shifted(y, hop_y, ys)
        if y_first(step):
            if hop_y:
                slot = first_slots[step, hop_y] = wires.slot()
                wires.start(
                    slot,
                    w_v.at[rows_at(f_rows(z_at, y_at, 0), slab)],
                    y_f.at[pl.ds(y_base[step] + (hop_y - 1) * slab, slab)],
                    here.device(y=y_at),
                )
            return
        for hop in range(1, xs):
            x_at = shifted(x, hop, xs)
            slot = first_slots[step, hop_y, hop] = wires.slot()
            wires.start(
                slot,
                w_v.at[rows_at(f_rows(z_at, y_at, x_at), pair_rows)],
                x_f.at[rows_at(x_base[step] + ((hop - 1) * ys + y_at) * pair_rows, pair_rows)],
                here.device(x=x_at),
            )

    def f_across(step):
        z_at = shifted(z, step, zs)
        if y_first(step):
            sources = []
            for hop in range(1, ys):
                start = y_base[step] + (hop - 1) * slab
                there = here.device(y=shifted(y, -hop, ys))
                wires.arrive(first_slots[step, hop], y_f.at[pl.ds(start, slab)], there)
                sources.append((y_f, start))
            add(w_v, f_rows(z_at, y, 0), sources, slab)
            for hop in range(1, xs):
                x_at = shifted(x, hop, xs)
                slot = second_slots[step, hop] = wires.slot()
                wires.start(
                    slot,
                    w_v.at[rows_at(f_rows(z_at, y, x_at), pair_rows)],
                    x_f.at[pl.ds(x_base[step] + (hop - 1) * pair_rows, pair_rows)],
                    here.device(x=x_at),
                )
            return
        for hop_y in y_order:
            y_at = shifted(y, hop_y, ys)
            sources = []
            for hop in range(1, xs):
                start = x_base[step] + ((hop - 1) * ys + y_at) * pair_rows
                there = here.device(x=shifted(x, -hop, xs))
                view = x_f.at[rows_at(start, pair_rows)]
                wires.arrive(first_slots[step, hop_y, hop], view, there)
                sources.append((x_f, start))
            add(w_v, f_rows(z_at, y_at, x), sources, pair_rows)
            if hop_y:
                slot = second_slots[step, hop_y] = wires.slot()
                wires.start(
                    slot,
                    w_v.at[rows_at(f_rows(z_at, y_at, x), pair_rows)],
                    y_f.at[pl.ds(y_base[step] + (hop_y - 1) * pair_rows, pair_rows)],
                    here.device(y=y_at),
                )

    def f_out(step):
        z_at = shifted(z, step, zs)
        sources = []
        if y_first(step):
            for hop in range(1, xs):
                start = x_base[step] + (hop - 1) * pair_rows
                there = here.device(x=shifted(x, -hop, xs))
                wires.arrive(second_slots[step, hop], x_f.at[pl.ds(start, pair_rows)], there)
                sources.append((x_f, start))
        else:
            for hop in range(1, ys):
                start = y_base[step] + (hop - 1) * pair_rows
                there = here.device(y=shifted(y, -hop, ys))
                wires.arrive(second_slots[step, hop], y_f.at[pl.ds(start, pair_rows)], there)
                sources.append((y_f, start))
        add(w_v, f_rows(z_at, y, x), sources, pair_rows)
        for core in range(2):
            to_c = lax.rem(c + core, 2)
            source = w_v.at[rows_at(f_rows(z_at, y, x) + to_c * rows, rows)]
            target = out_f.at[z * 2 + c]
            if step == 0 and core == 0:
                keep(source, target)
            else:
                slot = ffn_z[step, core] = wires.slot()
                wires.start(slot, source, target, here.device(z=z_at, c=to_c))

    early = 2 * ys
    all_blocks = [(step, hop_y) for step in f_order for hop_y in y_order]
    for turn, (step, hop_y) in enumerate(all_blocks):
        grad_ffn(step, hop_y)
        if turn < early:
            f_send(step, hop_y)
    for k in reversed(range(1, zs - 1)):
        d_chain.onward(0, k)
        d_chain.onward(1, k)

    d_chain.last()

    def dmiddle_rows(at, first):
        ds2 = sd_v[at16(z * toks + first), :].astype(f32)
        middle = mid_v[at, :]
        inverse = inv_v[at, :][:, :1]
        s2 = middle * inverse
        grad = dy_v[at16(my_s2 + first), :].astype(f32) + inverse * (
            ds2 - s2 * jnp.mean(ds2 * s2, axis=1, keepdims=True)
        )
        input_grad[at, :] = grad.astype(low)

    each_rows(toks, dmiddle_rows)

    dbr_v = pr_v

    def dbr_view(x_at, c_at):
        return dbr_v.at[part_rows(x_at, c_at)]

    own_copy = keep(input_grad, dbr_view(x, c))
    dbr_cross = [wires.slot() for step in range(xs)]
    dbr_core = [wires.slot() for step in range(xs)]
    dbr_sent = [wires.start(dbr_core[0], input_grad, dbr_view(x, c), sibling)]
    for step in range(1, xs):
        there = here.device(x=shifted(x, step, xs))
        dbr_sent.append(wires.start(dbr_cross[step], input_grad, dbr_view(x, c), there))
    for step, exists in ((1, z < zs - 1), (-1, z > 0)):

        @pl.when(exists)
        def _(step=step):
            there = here.device(z=lax.clamp(0, z + step, zs - 1))
            pl.semaphore_signal(
                credit.at[(1 - step) // 2], inc=1, device_id=there, device_id_type=MESH
            )

    for step, hop_y in all_blocks[early:]:
        f_send(step, hop_y)
    for way, exists in enumerate((z < zs - 1, z > 0)):

        @pl.when(exists)
        def _(way=way):
            pl.semaphore_wait(credit.at[1 - way], 1)

    for k in reversed(range(1, zs)):
        o_chain.first(0, k)
        o_chain.first(1, k)
    f_across(f_order[1])
    for step in range(1, xs):
        from_x = shifted(x, -step, xs)
        view = dbr_view(from_x, c)
        wires.arrive(dbr_cross[step], view, here.device(x=from_x))
        wires.start(dbr_core[step], view, view, sibling)
    own_copy.wait()
    o_chain.onward(0, zs - 2)
    o_chain.onward(1, zs - 2)
    for step in range(xs):
        wires.arrive(dbr_core[step], dbr_view(shifted(x, -step, xs), 1 - c), sibling)
    da_v, dpr_v = hid_v, dgu_v
    qkv_rows = pl.ds(0, seq)

    def dattended_tile(n, carry):
        at = rows_at(lax.rem(n, row_blocks) * width, width)
        start = n // row_blocks * width
        cols = pl.ds(pl.multiple_of(start, width), width)
        w_cols = pl.ds(pl.multiple_of(proj + start, width), width)
        da_v[at, cols] = dot_nn(dbr_v[at, :], wa[:, w_cols]).astype(low)
        return carry

    lax.fori_loop(0, row_blocks * (heads // width), dattended_tile, 0)

    def grad_out_tile(n, carry):
        cols = pl.ds(pl.multiple_of(n * width, width), width)
        wa[cols, out_cols] = dot_tn(dbr_v[:, cols], att_v[...]).astype(low)
        return carry

    for done in qkv.sent + outw.sent:
        done()
    lax.fori_loop(0, MODEL // width, grad_out_tile, 0)

    far_first = [blocks[zs - 1 - turn] for turn in range(zs)]
    attn_y = {}

    def y_slot(hop, z_at):
        return ((hop - 1) * zs + z_at) * slab

    def attn_send_y(part, cols):
        for turn, z_at in enumerate(far_first):
            for hop in range(1, ys):
                y_at = shifted(y, hop, ys)
                slot = attn_y[part, turn, hop] = wires.slot()
                wires.start(
                    slot,
                    wa.at[rows_at((z_at * ys + y_at) * slab, slab), cols],
                    y_a.at[rows_at(y_slot(hop, z_at), slab), cols],
                    here.device(y=y_at),
                )

    def a_across(part, cols, turn):
        z_at = far_first[turn]
        sources = []
        for hop in range(1, ys):
            start = y_slot(hop, z_at)
            there = here.device(y=shifted(y, -hop, ys))
            wires.arrive(attn_y[part, turn, hop], y_a.at[rows_at(start, slab), cols], there)
            sources.append((y_a, start))
        add(wa, (z_at * ys + y) * slab, sources, slab, cols)

    def slab_rows(b):
        return (b * ys + y) * slab

    attn_chains = [
        Chain(wa, slab_rows, z_a, slab, 2, out_cols),
        Chain(wa, slab_rows, z_a, slab, 2, qkv_cols),
    ]

    def a_first(part, cols):
        for turn in range(zs):
            a_across(part, cols, turn)
            if turn < zs - 1:
                attn_chains[part].first(0, zs - 1 - turn)
                attn_chains[part].first(1, zs - 1 - turn)

    def a_onward(part, k):
        attn_chains[part].onward(0, k)
        attn_chains[part].onward(1, k)

    attn_send_y(0, out_cols)

    dkv_v[...] = jnp.zeros_like(dkv_v)

    def attend_back(step, carry):
        at = rows_at(lax.rem(step, row_blocks) * width, width)
        cols = pl.ds(pl.multiple_of(step // row_blocks * HEAD_DIM, HEAD_DIM), HEAD_DIM)
        exponent, total = weights_of(at, cols, lax.rem(step, row_blocks) * width)
        prob = exponent / total
        dout = da_v[at, cols]
        delta = jnp.sum(dout.astype(f32) * att_v[at, cols].astype(f32), axis=1, keepdims=True)
        dprob = dot_nt(dout, kv_v[:, HEAD_DIM:])
        dscore = (prob * (dprob - delta)).astype(low)
        dquery = dot_nn(dscore, kv_v[:, :HEAD_DIM]) * scale
        dpr_v[at, cols] = turned(dquery, at, -1.0).astype(low)
        dkv_v[:, :HEAD_DIM] += dot_tn(dscore, q_v[at, cols]) * scale
        dkv_v[:, HEAD_DIM:] += dot_tn(prob.astype(low), dout)
        return carry

    lax.fori_loop(0, row_blocks * (heads // HEAD_DIM), attend_back, 0)
    mine = rows_at(here.fs * toks, toks)
    dkv_v[mine, :] += kv_grad[...].astype(f32)

    def dkv_rows(step, carry):
        at = rows_at(step * width, width)
        dpr_v[at, pl.ds(heads, HEAD_DIM)] = turned(dkv_v[at, :HEAD_DIM], at, -1.0).astype(low)
        dpr_v[at, pl.ds(heads + HEAD_DIM, HEAD_DIM)] = dkv_v[at, HEAD_DIM:].astype(low)
        return carry

    lax.fori_loop(0, row_blocks, dkv_rows, 0)
    dn1_v = s2_v

    def dn1_tile(n, carry):
        cols = pl.ds(pl.multiple_of(n * width, width), width)
        dn1_v[qkv_rows, cols] = dot_nt(dpr_v[qkv_rows, qkv_cols], wa[cols, qkv_cols]).astype(low)
        return carry

    for done in s2s.sent:
        done()
    lax.fori_loop(0, MODEL // width, dn1_tile, 0)

    def grad_qkv_tile(n, carry):
        cols = pl.ds(pl.multiple_of(n * width, width), width)
        wa[cols, qkv_cols] = dot_tn(tok_v[:, cols], dpr_v[qkv_rows, qkv_cols]).astype(low)
        return carry

    lax.fori_loop(0, MODEL // width, grad_qkv_tile, 0)
    attn_send_y(1, qkv_cols)
    across, across_sent = reduce_sequence(dn1_v)

    f_across(f_order[0])
    for k in reversed(range(1, zs - 2)):
        o_chain.onward(0, k)
        o_chain.onward(1, k)
    a_first(0, out_cols)
    for k in reversed(range(1, zs - 1)):
        a_onward(0, k)
    f_out(f_order[1])
    for step in f_order[2:]:
        f_across(step)
    a_first(1, qkv_cols)
    f_out(f_order[0])
    for k in reversed(range(1, zs - 1)):
        a_onward(1, k)
    attn_chains[0].last()
    attn_chains[1].last()
    attn_f = {}
    for step in range(fsdp):
        other = shifted(here.fs, step, fsdp)
        source = wa.at[rows_at((here.dp * fsdp + other) * rows, rows)]
        target = out_a.at[here.fs]
        if step:
            slot = attn_f[step] = wires.slot()
            wires.start(slot, source, target, (here.dp, other))
        else:
            keep(source, target)
    for step in f_order[2:]:
        f_out(step)
    o_chain.last()

    def mixed_rows(at, first):
        mixed[at, :] = (mid_v[at, :] + so_v[at16(z * toks + first), :].astype(f32)).astype(low)

    each_rows(toks, mixed_rows)
    sequence_arrive(across)

    def input_rows(at, first):
        ds1 = sequence_total(first)
        values = tokens[at, :].astype(f32)
        inverse = lax.rsqrt(jnp.mean(values * values, axis=1, keepdims=True) + EPSILON)
        s1 = values * inverse
        back = inverse * (ds1 - s1 * jnp.mean(ds1 * s1, axis=1, keepdims=True))
        input_grad[at, :] = (input_grad[at, :].astype(f32) + back).astype(low)

    for done in dbr_sent:
        done()
    each_rows(toks, input_rows)
    for step in range(1, fsdp):
        other = shifted(here.fs, -step, fsdp)
        wires.arrive(attn_f[step], out_a.at[other], (here.dp, other))
    for step in range(zs):
        from_z = shifted(z, -step, zs)
        for core in range(2):
            if step or core:
                from_c = lax.rem(c + core, 2)
                wires.arrive(
                    ffn_z[step, core],
                    out_f.at[from_z * 2 + from_c],
                    here.device(z=from_z, c=from_c),
                )
    for copy in locals_[first_local + 1 :]:
        copy.wait()
    for chain in [d_chain, o_chain] + attn_chains:
        chain.drain()
    wires.drain()


def whole_block(place, w_qkv, w_out, w_gateup, w_down, tokens, dy, kv_grad, rope, key_at):
    toks = tokens.shape[0]
    zs, ys, xs, fsdp, rows = place.zs, place.ys, place.xs, place.fsdp, place.rows
    heads = place.heads
    seq = toks * fsdp
    every = zs * 2 * toks
    slab = fsdp * rows
    low, f32 = jnp.bfloat16, jnp.float32
    count = place.copies
    vmem = pl.BlockSpec(memory_space=pltpu.VMEM)
    hbm = pl.BlockSpec(memory_space=ANY)
    return pl.pallas_call(
        functools.partial(block_kernel, place),
        out_shape=(
            jax.ShapeDtypeStruct((toks, MODEL), low),
            jax.ShapeDtypeStruct((toks, KV), low),
            jax.ShapeDtypeStruct((toks, MODEL), low),
            jax.ShapeDtypeStruct((2 * zs, rows, place.ffn_width), low),
            jax.ShapeDtypeStruct((fsdp, rows, place.attn_width), low),
        ),
        in_specs=[hbm] * 4 + [vmem, hbm] + [vmem] * 3,
        out_specs=(vmem, vmem, vmem, hbm, hbm),
        scratch_shapes=[
            pltpu.VMEM((MODEL, place.attn_width), low),
            pltpu.VMEM((MODEL, place.ffn_width), low),
            pltpu.VMEM((seq, MODEL), low),
            pltpu.VMEM((every, MODEL), low),
            pltpu.VMEM((every, MODEL), low),
            pltpu.VMEM((every, place.block), low),
            pltpu.VMEM((every, 2 * place.block), low),
            pltpu.VMEM((seq, MODEL), low),
            pltpu.VMEM((xs * toks, MODEL), low),
            pltpu.VMEM((xs * toks, MODEL), low),
            pltpu.VMEM((toks, MODEL), f32),
            pltpu.VMEM((toks, LANES), f32),
            pltpu.VMEM((zs * toks, MODEL), low),
            pltpu.VMEM((zs * toks, MODEL), low),
            pltpu.VMEM((2 * (zs - 1) * toks, MODEL), low),
            pltpu.VMEM((seq, heads), low),
            pltpu.VMEM((seq, KV), low),
            pltpu.VMEM((seq, heads), low),
            pltpu.VMEM((seq, KV), f32),
            pltpu.VMEM(((xs - 1) * ((zs - 1) * ys + 1) * 2 * rows, place.ffn_width), low),
            pltpu.VMEM(((ys - 1) * (zs - 1 + xs) * 2 * rows, place.ffn_width), low),
            pltpu.VMEM(((ys - 1) * zs * slab, place.attn_width), low),
            pltpu.VMEM((2 * (zs - 1) * slab, place.attn_width), low),
            pltpu.SemaphoreType.DMA((16,)),
            pltpu.SemaphoreType.DMA((count,)),
            pltpu.SemaphoreType.DMA((count,)),
            pltpu.SemaphoreType.REGULAR((2,)),
        ],
        compiler_params=pltpu.CompilerParams(
            collective_id=0, has_side_effects=True, vmem_limit_bytes=63 * 2**20 + 2**19
        ),
        name="whole_block",
    )(w_qkv, w_out, w_gateup, w_down, tokens, dy, kv_grad, rope, key_at)


def on_device(
    place, tokens, lengths, gain_attn, w_qkv, w_out, gain_ffn, w_gateup, w_down, out_grad, kv_grad
):
    toks = tokens.shape[0]
    fsdp = place.fsdp
    seq = toks * fsdp
    low = jnp.bfloat16
    f32 = jnp.float32
    group = lax.axis_index("dp")
    length = jnp.sum(
        jnp.where(jnp.arange(lengths.shape[0], dtype=jnp.int32) == group, lengths, 0)
    )
    slots = np.arange(seq)
    at = slots % toks * fsdp + slots // toks
    frequency = THETA ** (-np.arange(HEAD_DIM // 2, dtype=np.float64) * (2.0 / HEAD_DIM))
    angles = at[:, None] * frequency[None, :]
    rope = jnp.asarray(np.concatenate([np.cos(angles), np.sin(angles)], axis=1), f32)
    positions = jnp.asarray(at, jnp.int32)
    key_at = jnp.where(positions < length, positions, seq)
    key_at = jnp.broadcast_to(key_at[None, :], (8, seq))

    gain_a = gain_attn.astype(f32)[:, None]
    gain_f = gain_ffn.astype(f32)[:, None]
    folded_qkv = (w_qkv.astype(f32) * gain_a).astype(low)
    folded_gateup = (w_gateup.astype(f32) * gain_f).astype(low)
    mixed, shared_kv, input_grad, out_f, out_a = whole_block(
        place, folded_qkv, w_out, folded_gateup, w_down, tokens, out_grad, kv_grad,
        rope, key_at,
    )

    heads, block = place.heads, place.block
    duplicate = 2 * block - place.zone
    out_f = out_f.astype(f32)
    out_a = out_a.astype(f32)

    def columns(start):
        pieces = []
        for z_at in range(place.zs):
            pieces.append(out_f[2 * z_at, :, start : start + block])
            pieces.append(out_f[2 * z_at + 1, :, start + duplicate : start + block])
        return pieces

    plain_gateup = jnp.concatenate(columns(0) + columns(block), axis=1)
    grad_down = jnp.concatenate(columns(2 * block), axis=1)
    plain_qkv = jnp.concatenate(
        [out_a[at, :, :heads] for at in range(fsdp)]
        + [jnp.sum(out_a[:, :, heads : heads + KV], axis=0)],
        axis=1,
    )
    grad_out = jnp.concatenate([out_a[at, :, heads + KV :] for at in range(fsdp)], axis=1)
    grad_gain_attn = jnp.sum(w_qkv.astype(f32) * plain_qkv, axis=1)
    grad_gain_ffn = jnp.sum(w_gateup.astype(f32) * plain_gateup, axis=1)
    return (
        mixed,
        shared_kv,
        input_grad,
        grad_gain_attn,
        plain_qkv * gain_a,
        grad_out,
        grad_gain_ffn,
        plain_gateup * gain_f,
        grad_down,
    )


def solution(mesh):
    place = Place(mesh.shape["dp"], mesh.shape["fsdp"])
    row = P(("dp", "fsdp"), None)
    line = P(("dp", "fsdp"))
    return jax.shard_map(
        functools.partial(on_device, place),
        mesh=mesh,
        in_specs=(row, P(), line, row, row, line, row, row, row, row),
        out_specs=(row, row, row, line, row, row, line, row, row),
        check_vma=False,
    )
```

```python
import functools

import jax
import jax.numpy as jnp
import numpy as np
from jax import lax
from jax.experimental import pallas as pl
from jax.experimental.pallas import tpu as pltpu
from jax.sharding import PartitionSpec as P

HEADS = 16
HEAD_DIM = 128
FF = 5632
HQ = 2048
MODEL = 2048
KV = 2 * HEAD_DIM
LANES = 128

EPSILON = 1e-05
THETA = 10000.0
MASKED = -1e30
MESH = pl.DeviceIdType.MESH
ANY = pl.ANY


class Place:
    def __init__(self, dp_count, fsdp_count):
        self.fsdp = fsdp_count
        self.xs = fsdp_count // 2
        self.ys = self.xs
        self.zs = dp_count // self.ys
        self.rows = MODEL // (dp_count * fsdp_count)
        self.heads = HQ // fsdp_count
        self.attn_width = 2 * self.heads + KV
        self.zone = FF // self.zs
        self.block = LANES * -(-(self.zone // LANES) // 2)
        self.ffn_width = 3 * self.block
        zs, ys, xs, fsdp = self.zs, self.ys, self.xs, self.fsdp
        across = (ys - 1) + (xs - 1)
        line = 2 * (zs - 1)
        self.copies = (
            3 * (fsdp - 1) + 3 * (2 * zs - 1) + 2 * (line + (2 * zs - 1) * (ys - 1))
            + 2 * (line + 2 * zs - 1) + 2 * xs + 2 * (2 * xs - 1) + 2 * zs + 9 * line
            + 2 * zs * max(across + xs * (ys - 1), across + ys * (xs - 1))
            + 2 * zs * (ys - 1) + 2 * zs - 1 + fsdp - 1 + 2 * xs
        )


class Here:
    def __init__(self, place):
        self.place = place
        self.dp = lax.axis_index("dp")
        self.fs = lax.axis_index("fsdp")
        self.z = self.dp // place.ys
        self.y = lax.rem(self.dp, place.ys)
        self.x = self.fs // 2
        self.c = lax.rem(self.fs, 2)

    def device(self, z=None, y=None, x=None, c=None):
        z = self.z if z is None else z
        y = self.y if y is None else y
        x = self.x if x is None else x
        c = self.c if c is None else c
        return (z * self.place.ys + y, x * 2 + c)

    def sibling(self):
        return self.device(c=1 - self.c)


def shifted(value, step, count):
    return lax.rem(value + (step + count), count)


def rows_at(start, count):
    return pl.ds(pl.multiple_of(start, count), count)


def cols_at(start, count):
    return pl.ds(pl.multiple_of(start, LANES), count)


class Wires:
    def __init__(self, send, recv):
        self.send = send
        self.recv = recv
        self.used = 0
        self.finish = []

    def slot(self):
        self.used += 1
        return self.used - 1

    def copy(self, slot, source, target, device):
        return pltpu.make_async_remote_copy(
            src_ref=source,
            dst_ref=target,
            send_sem=self.send.at[slot],
            recv_sem=self.recv.at[slot],
            device_id=device,
            device_id_type=MESH,
        )

    def start(self, slot, source, target, device, when=None):
        copy = self.copy(slot, source, target, device)
        if when is None:
            copy.start()
            wait = copy.wait_send
        else:
            pl.when(when)(copy.start)

            def wait():
                pl.when(when)(copy.wait_send)

        self.finish.append(wait)

        def done():
            self.finish.remove(wait)
            wait()

        return done

    def arrive(self, slot, target, device, when=None):
        copy = self.copy(slot, target, target, device)
        if when is None:
            copy.wait_recv()
        else:
            pl.when(when)(copy.wait_recv)

    def drain(self):
        for wait in self.finish:
            wait()
        self.finish = []


def greet(devices):
    barrier = pltpu.get_barrier_semaphore()
    for device in devices:
        pl.semaphore_signal(barrier, inc=1, device_id=device, device_id_type=MESH)
    pl.semaphore_wait(barrier, len(devices))


def line_partners(here):
    place = here.place
    return [here.device(z=shifted(here.z, step, place.zs)) for step in range(1, place.zs)]


def plane_partners(here):
    place = here.place
    return [here.device(y=shifted(here.y, step, place.ys)) for step in range(1, place.ys)] + [
        here.device(x=shifted(here.x, step, place.xs)) for step in range(1, place.xs)
    ]


class Line:
    def __init__(self, wires, here, view):
        self.wires = wires
        self.here = here
        self.view = view
        count = here.place.zs
        self.count = count
        self.up = [wires.slot() for step in range(count - 1)]
        self.down = [wires.slot() for step in range(count - 1)]

    def send(self, step):
        here, count = self.here, self.count
        if step >= count - 1:
            return []
        z = here.z
        low = lax.max(z - step, 0)
        high = lax.min(z + step, count - 1)
        up = self.wires.start(
            self.up[step],
            self.view(low),
            self.view(low),
            here.device(z=lax.min(z + 1, count - 1)),
            when=(z >= step) & (z < count - 1),
        )
        down = self.wires.start(
            self.down[step],
            self.view(high),
            self.view(high),
            here.device(z=lax.max(z - 1, 0)),
            when=(z + step < count) & (z > 0),
        )
        return [up, down]

    def arrive(self, step):
        here, count = self.here, self.count
        z = here.z
        low = lax.max(z - step, 0)
        high = lax.min(z + step, count - 1)
        self.wires.arrive(
            self.up[step - 1], self.view(low), here.device(z=lax.max(z - 1, 0)), when=z >= step
        )
        self.wires.arrive(
            self.down[step - 1],
            self.view(high),
            here.device(z=lax.min(z + 1, count - 1)),
            when=z + step < count,
        )

    def valid(self, step):
        z = self.here.z
        if step == 0:
            return [(z, None)]
        return [
            (lax.max(z - step, 0), z >= step),
            (lax.min(z + step, self.count - 1), z + step < self.count),
        ]


def each_rows(count, body, size=16):
    def step(index, carry):
        body(pl.ds(pl.multiple_of(index * size, size), size), index * size)
        return carry

    lax.fori_loop(0, count // size, step, 0)


def dot_nn(left, right):
    return lax.dot_general(
        left, right, (((1,), (0,)), ((), ())), preferred_element_type=jnp.float32
    )


def dot_nt(left, right):
    return lax.dot_general(
        left, right, (((1,), (1,)), ((), ())), preferred_element_type=jnp.float32
    )


def dot_tn(left, right):
    return lax.dot_general(
        left, right, (((0,), (0,)), ((), ())), preferred_element_type=jnp.float32
    )


def visit_order(count):
    orders = []
    for z in range(count):
        far = sorted(range(count), key=lambda other: (abs(other - z), other))
        orders.append(far)
    return orders


def chosen(z, turn, orders):
    total = 0
    for z_at, order in enumerate(orders):
        here = jnp.where(z == z_at, 1, 0)
        for turn_at, value in enumerate(order):
            if isinstance(turn, int):
                if turn == turn_at:
                    total = total + here * value
            else:
                total = total + here * jnp.where(turn == turn_at, 1, 0) * value
    return total


def block_kernel(
    place, w_qkv, w_out, w_gateup, w_down, tokens, dy, kv_grad, rope, key_at,
    mixed, shared_kv, input_grad, out_f, out_a,
    wa, w_v, tok_v, dy_v, s2_v, hid_v, dgu_v, pr_v, ps_v, px_v, mid_v, inv_v,
    so_v, sd_v, z_land, q_v, kv_v, att_v, dkv_v,
    x_f, y_f, y_a, z_a, local, send, recv, credit,
):
    here = Here(place)
    wires = Wires(send, recv)
    z, y, x, c = here.z, here.y, here.x, here.c
    zs, ys, xs, fsdp, rows = place.zs, place.ys, place.xs, place.fsdp, place.rows
    heads, block, zone = place.heads, place.block, place.zone
    proj = heads + KV
    toks = tokens.shape[0]
    seq = toks * fsdp
    pair = 2 * toks
    slab = fsdp * rows
    width = 256
    low = jnp.bfloat16
    f32 = jnp.float32
    scale = HEAD_DIM ** (-0.5)
    sibling = here.sibling()
    partners = line_partners(here) + plane_partners(here)
    partners += [here.device(x=shifted(x, step, xs), c=1 - c) for step in range(xs)]
    partners += [here.device(z=shifted(z, step, zs), c=1 - c) for step in range(1, zs)]
    greet(partners)

    def index(z=z, y=y, x=x, c=c):
        return (z * ys + y) * fsdp + x * 2 + c

    locals_ = []

    def keep(source, target):
        copy = pltpu.make_async_copy(source, target, local.at[len(locals_)])
        copy.start()
        locals_.append(copy)
        return copy

    def at16(start):
        return pl.ds(pl.multiple_of(start, 16), 16)

    def add(target, start, sources, count, cols=slice(None)):
        def step(at, first):
            at = at16(start + first)
            total = target[at, cols].astype(f32)
            for source, source_start in sources:
                total = total + source[at16(source_start + first), cols].astype(f32)
            target[at, cols] = total.astype(low)

        each_rows(count, step)

    own_rows = rows_at(index() * rows, rows)
    qkv_cols, out_cols = pl.ds(0, proj), pl.ds(proj, heads)

    def qkv_pieces(owner):
        return [(w_qkv, owner * heads, heads, 0), (w_qkv, HQ, KV, heads)]

    def out_pieces(owner):
        return [(w_out, owner * heads, heads, proj)]

    def attn_spread(pieces):
        slots = []
        for step in range(1, fsdp):
            other = shifted(here.fs, step, fsdp)
            for ref, start, count, place_at in pieces(other):
                slot = wires.slot()
                slots.append((slot, step, count, place_at))
                wires.start(
                    slot,
                    ref.at[:, cols_at(start, count)],
                    wa.at[own_rows, pl.ds(place_at, count)],
                    (here.dp, other),
                )
        for ref, start, count, place_at in pieces(here.fs):
            keep(ref.at[:, cols_at(start, count)], wa.at[own_rows, pl.ds(place_at, count)])
        return slots

    def attn_collect(slots):
        for slot, step, count, place_at in slots:
            other = shifted(here.fs, -step, fsdp)
            at = rows_at((here.dp * fsdp + other) * rows, rows)
            wires.arrive(slot, wa.at[at, pl.ds(place_at, count)], (here.dp, other))

    def ffn_pieces(zone_z, core):
        start = zone_z * zone + core * (zone - block)
        return [(w_gateup, start, 0), (w_gateup, FF + start, block), (w_down, start, 2 * block)]

    ffn_slots = {}

    def ffn_spread(step):
        for core in range(2):
            to_z, to_c = shifted(z, step, zs), lax.rem(c + core, 2)
            for ref, start, place_at in ffn_pieces(to_z, to_c):
                source = ref.at[:, cols_at(start, block)]
                target = w_v.at[own_rows, pl.ds(place_at, block)]
                if step == 0 and core == 0:
                    keep(source, target)
                    continue
                slot = wires.slot()
                ffn_slots.setdefault(step, []).append((slot, core, place_at))
                wires.start(slot, source, target, here.device(z=to_z, c=to_c))

    def ffn_collect(step):
        from_z = shifted(z, -step, zs)
        for slot, core, place_at in ffn_slots[step]:
            from_c = lax.rem(c + core, 2)
            at = rows_at(index(z=from_z, c=from_c) * rows, rows)
            wires.arrive(slot, w_v.at[at, pl.ds(place_at, block)], here.device(z=from_z, c=from_c))

    def w_view(z_at, y_at, x_at):
        return w_v.at[rows_at(index(z_at, y_at, x_at, 0) * rows, 2 * rows)]

    near, far = {}, {}
    w_sent = []

    def axes(step):
        ways = [("y", y, ys), ("x", x, xs)]
        return ways if step else ways[::-1]

    def at_plane(name, value, other):
        return {"y_at": value, "x_at": other} if name == "y" else {"y_at": other, "x_at": value}

    def to_plane(name, value):
        return here.device(y=value) if name == "y" else here.device(x=value)

    def ffn_send(slots, key, name, me, count, view):
        for hop in range(1, count):
            slot = slots[key + (hop,)] = wires.slot()
            w_sent.append(wires.start(slot, view, view, to_plane(name, shifted(me, hop, count))))

    def ffn_near(step):
        z_at = shifted(z, -step, zs)
        first, me, count = axes(step)[0]
        ffn_send(near, (step,), first, me, count, w_view(z_at, y, x))

    def ffn_far(step):
        z_at = shifted(z, -step, zs)
        second, me, count = axes(step)[1]
        ffn_send(far, (step, 0), second, me, count, w_view(z_at, y, x))

    def ffn_forward(step):
        ffn_collect(step)
        ffn_near(step)
        ffn_far(step)

    def ffn_across(step):
        z_at = shifted(z, -step, zs)
        (first, me, count), (second, me2, count2) = axes(step)
        for hop in range(1, count):
            origin = shifted(me, -hop, count)
            view = w_view(z_at, **at_plane(first, origin, me2))
            wires.arrive(near[step, hop], view, to_plane(first, origin))
            ffn_send(far, (step, hop), second, me2, count2, view)

    def ffn_arrive(step):
        z_at = shifted(z, -step, zs)
        (first, me, count), (second, me2, count2) = axes(step)
        for hop in range(count):
            for hop2 in range(1, count2):
                origin, origin2 = shifted(me, -hop, count), shifted(me2, -hop2, count2)
                view = w_view(z_at, **at_plane(first, origin, origin2))
                wires.arrive(far[step, hop, hop2], view, to_plane(second, origin2))

    class Spread:
        def __init__(self, cols):
            self.cols = cols
            self.line = Line(wires, here, lambda z_at: self.view(z_at, y))
            self.plane = {}
            self.sent = []

        def view(self, z_at, y_at):
            return wa.at[rows_at((z_at * ys + y_at) * slab, slab), self.cols]

        def step(self, step):
            if step:
                self.line.arrive(step)
            self.sent += self.line.send(step)
            for side, (z_at, exists) in enumerate(self.line.valid(step)):
                for hop in range(1, ys):
                    slot = self.plane[step, side, hop] = wires.slot()
                    view = self.view(z_at, y)
                    there = here.device(y=shifted(y, hop, ys))
                    self.sent.append(wires.start(slot, view, view, there, when=exists))

        def crossed(self):
            for step in range(zs):
                for side, (z_at, exists) in enumerate(self.line.valid(step)):
                    for hop in range(1, ys):
                        from_y = shifted(y, -hop, ys)
                        wires.arrive(
                            self.plane[step, side, hop],
                            self.view(z_at, from_y),
                            here.device(y=from_y),
                            when=exists,
                        )

    class Acts:
        def __init__(self, ref):
            self.ref = ref
            self.line = Line(wires, here, lambda z_at: self.view(z_at, c))
            self.core = {}
            self.sent = []

        def view(self, z_at, c_at):
            return self.ref.at[rows_at((z_at * 2 + c_at) * toks, toks)]

        def step(self, step):
            if step:
                self.line.arrive(step)
            self.sent += self.line.send(step)
            for side, (z_at, exists) in enumerate(self.line.valid(step)):
                slot = self.core[step, side] = wires.slot()
                view = self.view(z_at, c)
                self.sent.append(wires.start(slot, view, view, sibling, when=exists))

        def crossed(self, step):
            for side, (z_at, exists) in enumerate(self.line.valid(step)):
                wires.arrive(self.core[step, side], self.view(z_at, 1 - c), sibling, when=exists)

    def tok_view(x_at, c_at):
        return tok_v.at[rows_at((x_at * 2 + c_at) * toks, toks)]

    qkv_slots = attn_spread(qkv_pieces)
    ffn_spread(0)
    ffn_spread(1)
    keep(tokens, tok_view(x, c))
    tok_cross = [wires.slot() for step in range(xs)]
    tok_core = [wires.slot() for step in range(xs)]
    wires.start(tok_core[0], tokens, tok_view(x, c), sibling)
    for step in range(1, xs):
        wires.start(
            tok_cross[step], tokens, tok_view(x, c), here.device(x=shifted(x, step, xs))
        )
    out_slots = attn_spread(out_pieces)
    dys = Acts(dy_v)
    keep(dy, dys.view(z, c))
    for copy in locals_:
        copy.wait()
    first_local = len(locals_)
    ffn_collect(0)
    ffn_near(0)
    attn_collect(qkv_slots)
    qkv = Spread(qkv_cols)
    qkv.step(0)
    attn_collect(out_slots)
    outw = Spread(out_cols)
    outw.step(0)
    ffn_collect(1)
    ffn_far(1)
    tok_sent = []
    for step in range(1, xs):
        from_x = shifted(x, -step, xs)
        view = tok_view(from_x, c)
        wires.arrive(tok_cross[step], view, here.device(x=from_x))
        tok_sent.append(wires.start(tok_core[step], view, view, sibling))
    qkv.step(1)
    outw.step(1)
    for step in range(xs):
        from_x = shifted(x, -step, xs)
        wires.arrive(tok_core[step], tok_view(from_x, 1 - c), sibling)
    for done in tok_sent:
        done()

    def norm_rows(at, first):
        values = tok_v[at, :].astype(f32)
        inverse = lax.rsqrt(jnp.mean(values * values, axis=1, keepdims=True) + EPSILON)
        tok_v[at, :] = (values * inverse).astype(low)

    each_rows(seq, norm_rows)
    qkv.step(2)
    outw.step(2)
    late = [zs - 1] + list(range(2, zs - 1))
    for step in late:
        ffn_spread(step)
    dys.step(0)
    for step in range(3, zs):
        qkv.step(step)
        outw.step(step)
    ffn_far(0)
    ffn_across(0)
    ffn_near(1)
    qkv.crossed()

    half = HEAD_DIM // 2

    def turned(values, at, sign):
        table = rope[at, :]
        across = pltpu.roll(table, half, 1)
        low_half = lax.broadcasted_iota(jnp.int32, table.shape, 1) < half
        cosine = jnp.where(low_half, table, across)
        sine_part = jnp.where(low_half, -across, table)
        return values * cosine + pltpu.roll(values, half, 1) * (sign * sine_part)

    row_blocks = seq // width

    def project(step, carry):
        at = rows_at(step * width, width)

        def query_tile(j, carry):
            cols = pl.ds(pl.multiple_of(j * HEAD_DIM, HEAD_DIM), HEAD_DIM)
            q_v[at, cols] = turned(dot_nn(tok_v[at, :], wa[:, cols]), at, 1.0).astype(low)
            return carry

        lax.fori_loop(0, heads // HEAD_DIM, query_tile, 0)
        both = dot_nn(tok_v[at, :], wa[:, pl.ds(heads, KV)])
        kv_v[at, :HEAD_DIM] = turned(both[:, :HEAD_DIM], at, 1.0).astype(low)
        kv_v[at, HEAD_DIM:] = both[:, HEAD_DIM:].astype(low)
        return carry

    lax.fori_loop(0, row_blocks, project, 0)
    shared_kv[...] = kv_v[rows_at(here.fs * toks, toks), :]

    def weights_of(at, cols, first):
        scores = dot_nt(q_v[at, cols], kv_v[:, :HEAD_DIM]) * scale
        row = lax.broadcasted_iota(jnp.int32, (width, LANES), 0) + first
        query_at = lax.rem(row, toks) * fsdp + row // toks
        allowed = key_at[0:1, :] <= query_at[:, :1]
        scores = jnp.where(allowed, scores, MASKED)
        exponent = jnp.exp(scores - jnp.max(scores, axis=1, keepdims=True))
        return exponent, jnp.sum(exponent, axis=1, keepdims=True)

    def attend(step, carry):
        at = rows_at(lax.rem(step, row_blocks) * width, width)
        cols = pl.ds(pl.multiple_of(step // row_blocks * HEAD_DIM, HEAD_DIM), HEAD_DIM)
        exponent, total = weights_of(at, cols, lax.rem(step, row_blocks) * width)
        att_v[at, cols] = (dot_nn(exponent.astype(low), kv_v[:, HEAD_DIM:]) / total).astype(low)
        return carry

    ffn_forward(late[0])
    lax.fori_loop(0, row_blocks * (heads // HEAD_DIM), attend, 0)
    outw.crossed()

    def branch_tile(n, carry):
        cols = pl.ds(pl.multiple_of(n * width, width), width)
        pr_v[:, cols] = dot_nt(att_v[...], wa[cols, out_cols]).astype(low)
        return carry

    lax.fori_loop(0, MODEL // width, branch_tile, 0)

    def part_rows(x_at, c_at):
        return rows_at((x_at * 2 + c_at) * toks, toks)

    def x_rows(x_at):
        return rows_at(x_at * toks, toks)

    x_order = list(range(1, xs)) + [0]

    def reduce_sequence(source):
        sib = [wires.slot() for step in range(xs)]
        across = {}
        sent = []
        for step in x_order:
            x_at = shifted(x, step, xs)
            sent.append(
                wires.start(
                    sib[step], source.at[part_rows(x_at, 1 - c)], ps_v.at[x_rows(x_at)], sibling
                )
            )
        for step in x_order:
            x_at = shifted(x, step, xs)
            wires.arrive(sib[step], ps_v.at[x_rows(x_at)], sibling)
            add(ps_v, x_at * toks, [(source, (x_at * 2 + c) * toks)], toks)
            if step == x_order[0]:
                for done in sent:
                    done()
            if step:
                across[step] = wires.slot()
                sent.append(
                    wires.start(
                        across[step], ps_v.at[x_rows(x_at)], px_v.at[x_rows(x)], here.device(x=x_at)
                    )
                )
        return across, sent[xs:]

    def sequence_arrive(across):
        for step in range(1, xs):
            from_x = shifted(x, -step, xs)
            wires.arrive(across[step], px_v.at[x_rows(from_x)], here.device(x=from_x))

    def sequence_total(first):
        total = ps_v[at16(x * toks + first), :].astype(f32)
        for step in range(1, xs):
            total = total + px_v[at16(shifted(x, -step, xs) * toks + first), :].astype(f32)
        return total

    across, across_sent = reduce_sequence(pr_v)
    sequence_arrive(across)
    s2s = Acts(s2_v)
    my_s2 = (z * 2 + c) * toks

    def middle_rows(at, first):
        middle = tokens[at, :].astype(f32) + sequence_total(first)
        inverse = lax.rsqrt(jnp.mean(middle * middle, axis=1, keepdims=True) + EPSILON)
        mid_v[at, :] = middle
        inv_v[at, :] = jnp.broadcast_to(inverse, (16, LANES))
        s2_v[at16(my_s2 + first), :] = (middle * inverse).astype(low)

    each_rows(toks, middle_rows)
    s2s.step(0)
    for step in late[1:]:
        ffn_forward(step)
    ffn_across(1)
    dys.step(1)
    ffn_across(late[0])
    s2s.step(1)
    for step in late[1:]:
        ffn_across(step)
    dys.step(2)
    s2s.step(2)
    for done in across_sent:
        done()
    for step in range(zs):
        ffn_arrive(step)
    orders = visit_order(zs)
    blocks = [chosen(z, turn, orders) for turn in range(zs)]
    duplicate = 2 * block - zone

    def hidden(b):
        at = rows_at(b * pair, pair)

        def hidden_tile(j, carry):
            def cols(base):
                return pl.ds(pl.multiple_of(base + j * width, width), width)

            gate = dot_nn(s2_v[at, :], w_v[:, cols(0)])
            up = dot_nn(s2_v[at, :], w_v[:, cols(block)])
            dhid = dot_nn(dy_v[at, :], w_v[:, cols(2 * block)])
            sg = 1.0 / (1.0 + jnp.exp(-gate))
            lane = lax.broadcasted_iota(jnp.int32, gate.shape, 1) + j * width
            mine = (lane >= duplicate) | (c == 0)
            act = gate * sg
            hid_v[at, cols(0)] = jnp.where(mine, act * up, 0.0).astype(low)
            dgate = dhid * up * sg * (1.0 + gate * (1.0 - sg))
            dgu_v[at, cols(0)] = jnp.where(mine, dgate, 0.0).astype(low)
            dgu_v[at, cols(block)] = jnp.where(mine, dhid * act, 0.0).astype(low)
            return carry

        lax.fori_loop(0, block // width, hidden_tile, 0)

    pd_v, po_v = px_v, ps_v

    def back(b):
        at = rows_at(b * pair, pair)

        def back_tile(n, carry):
            cols = pl.ds(pl.multiple_of(n * width, width), width)
            pd_v[pl.ds(0, pair), cols] = dot_nt(
                dgu_v[at, :], w_v[cols, pl.ds(0, 2 * block)]
            ).astype(low)
            po_v[pl.ds(0, pair), cols] = dot_nt(hid_v[at, :], w_v[cols, pl.ds(2 * block, block)]).astype(low)
            return carry

        lax.fori_loop(0, MODEL // width, back_tile, 0)

    class Chain:
        def __init__(self, own, own_start, landing, count, pieces, cols=slice(None)):
            self.cols = cols
            self.own, self.own_start, self.landing = own, own_start, landing
            self.count, self.pieces, self.size = count, pieces, count // pieces
            self.slots = {}
            for way in range(2):
                for k in range(1, zs):
                    for piece in range(pieces):
                        self.slots[way, k, piece] = wires.slot()

        def owner(self, way, k):
            return lax.min(z + k, zs - 1) if way == 0 else lax.max(z - k, 0)

        def exists(self, way, k):
            return z + k < zs if way == 0 else z >= k

        def feeds(self, way):
            return z > 0 if way == 0 else z < zs - 1

        def land(self, way, k, piece):
            return (way * (zs - 1) + k - 1) * self.count + piece * self.size

        def copy(self, way, k, piece):
            start = self.own_start(self.owner(way, k)) + piece * self.size
            return wires.copy(
                self.slots[way, k, piece],
                self.own.at[rows_at(start, self.size), self.cols],
                self.landing.at[pl.ds(self.land(way, k, piece), self.size), self.cols],
                here.device(z=self.owner(way, 1)),
            )

        def take(self, way, k, piece):
            land = self.land(way, k + 1, piece)
            view = self.landing.at[pl.ds(land, self.size), self.cols]
            wires.copy(
                self.slots[way, k + 1, piece], view, view, here.device(z=self.owner(1 - way, 1))
            ).wait_recv()
            owner = z if k == 0 else self.owner(way, k)
            start = self.own_start(owner) + piece * self.size
            add(self.own, start, [(self.landing, land)], self.size, self.cols)

        def first(self, way, k):
            @pl.when(jnp.logical_not(self.feeds(way)) & self.exists(way, k))
            def _():
                for piece in range(self.pieces):
                    self.copy(way, k, piece).start()

        def onward(self, way, k):
            if k == zs - 1:
                return

            @pl.when(self.feeds(way) & self.exists(way, k))
            def _():
                for piece in range(self.pieces):
                    self.take(way, k, piece)
                    self.copy(way, k, piece).start()

        def last(self):
            for way in range(2):

                @pl.when(self.feeds(way))
                def _(way=way):
                    for piece in range(self.pieces):
                        self.take(way, 0, piece)

        def drain(self):
            for way in range(2):
                for k in range(1, zs):

                    @pl.when(self.exists(way, k))
                    def _(way=way, k=k):
                        for piece in range(self.pieces):
                            self.copy(way, k, piece).wait_send()

    def line_rows(b):
        return b * toks

    kinds = ((pd_v, sd_v), (po_v, so_v))
    d_chain = Chain(sd_v, line_rows, z_land, toks, 4)
    o_chain = Chain(so_v, line_rows, z_land, toks, 1)
    shares = {}

    def share(turn, b):
        for kind, (buffer, landing) in enumerate(kinds):
            slot = wires.slot()
            done = wires.start(
                slot,
                buffer.at[rows_at((1 - c) * toks, toks)],
                landing.at[rows_at(b * toks, toks)],
                sibling,
            )
            shares[turn, kind] = (slot, done)

    def add_up(turn, b):
        for kind, (buffer, landing) in enumerate(kinds):
            slot, done = shares[turn, kind]
            wires.arrive(slot, landing.at[rows_at(b * toks, toks)], sibling)
            add(landing, b * toks, [(buffer, c * toks)], toks)
            done()
            if turn and kind == 0:
                d_chain.first(0, turn)
                d_chain.first(1, turn)

    relays = [
        (acts, step) for step in range(2, zs) for acts in (dys, s2s)
    ][2:]
    s2s.crossed(0)
    dys.crossed(0)
    for turn in range(zs):
        if turn:
            while relays and relays[0][1] <= turn:
                acts, step = relays.pop(0)
                acts.step(step)
            s2s.crossed(turn)
            dys.crossed(turn)
        hidden(blocks[turn])
        if turn:
            add_up(turn - 1, blocks[turn - 1])
        back(blocks[turn])
        share(turn, blocks[turn])
        if relays:
            acts, step = relays.pop(0)
            acts.step(step)
    add_up(zs - 1, blocks[zs - 1])
    for done in w_sent:
        done()

    f_order = list(range(1, zs)) + [0]
    y_order = list(range(1, ys)) + [0]
    pair_rows = 2 * rows
    first_slots, second_slots, ffn_z = {}, {}, {}

    def y_first(step):
        return step == f_order[0]

    x_base, y_base = {}, {}
    x_used = y_used = 0
    for step in f_order:
        x_base[step], y_base[step] = x_used, y_used
        x_used += (xs - 1) * pair_rows * (1 if y_first(step) else ys)
        y_used += (ys - 1) * pair_rows * (xs if y_first(step) else 1)

    def f_rows(z_at, y_at, x_at):
        return index(z_at, y_at, x_at, 0) * rows

    def grad_ffn(step, hop_y):
        z_at, y_at = shifted(z, step, zs), shifted(y, hop_y, ys)

        def tile(n, carry):
            cols = pl.ds(pl.multiple_of((z_at * ys + y_at) * slab + n * LANES, LANES), LANES)
            w_v[cols, pl.ds(0, 2 * block)] = dot_tn(s2_v[:, cols], dgu_v[...]).astype(low)
            w_v[cols, pl.ds(2 * block, block)] = dot_tn(dy_v[:, cols], hid_v[...]).astype(low)
            return carry

        lax.fori_loop(0, slab // LANES, tile, 0)

    def f_send(step, hop_y):
        z_at, y_at = shifted(z, step, zs), shifted(y, hop_y, ys)
        if y_first(step):
            if hop_y:
                slot = first_slots[step, hop_y] = wires.slot()
                wires.start(
                    slot,
                    w_v.at[rows_at(f_rows(z_at, y_at, 0), slab)],
                    y_f.at[pl.ds(y_base[step] + (hop_y - 1) * slab, slab)],
                    here.device(y=y_at),
                )
            return
        for hop in range(1, xs):
            x_at = shifted(x, hop, xs)
            slot = first_slots[step, hop_y, hop] = wires.slot()
            wires.start(
                slot,
                w_v.at[rows_at(f_rows(z_at, y_at, x_at), pair_rows)],
                x_f.at[rows_at(x_base[step] + ((hop - 1) * ys + y_at) * pair_rows, pair_rows)],
                here.device(x=x_at),
            )

    def f_across(step):
        z_at = shifted(z, step, zs)
        if y_first(step):
            sources = []
            for hop in range(1, ys):
                start = y_base[step] + (hop - 1) * slab
                there = here.device(y=shifted(y, -hop, ys))
                wires.arrive(first_slots[step, hop], y_f.at[pl.ds(start, slab)], there)
                sources.append((y_f, start))
            add(w_v, f_rows(z_at, y, 0), sources, slab)
            for hop in range(1, xs):
                x_at = shifted(x, hop, xs)
                slot = second_slots[step, hop] = wires.slot()
                wires.start(
                    slot,
                    w_v.at[rows_at(f_rows(z_at, y, x_at), pair_rows)],
                    x_f.at[pl.ds(x_base[step] + (hop - 1) * pair_rows, pair_rows)],
                    here.device(x=x_at),
                )
            return
        for hop_y in y_order:
            y_at = shifted(y, hop_y, ys)
            sources = []
            for hop in range(1, xs):
                start = x_base[step] + ((hop - 1) * ys + y_at) * pair_rows
                there = here.device(x=shifted(x, -hop, xs))
                view = x_f.at[rows_at(start, pair_rows)]
                wires.arrive(first_slots[step, hop_y, hop], view, there)
                sources.append((x_f, start))
            add(w_v, f_rows(z_at, y_at, x), sources, pair_rows)
            if hop_y:
                slot = second_slots[step, hop_y] = wires.slot()
                wires.start(
                    slot,
                    w_v.at[rows_at(f_rows(z_at, y_at, x), pair_rows)],
                    y_f.at[pl.ds(y_base[step] + (hop_y - 1) * pair_rows, pair_rows)],
                    here.device(y=y_at),
                )

    def f_out(step):
        z_at = shifted(z, step, zs)
        sources = []
        if y_first(step):
            for hop in range(1, xs):
                start = x_base[step] + (hop - 1) * pair_rows
                there = here.device(x=shifted(x, -hop, xs))
                wires.arrive(second_slots[step, hop], x_f.at[pl.ds(start, pair_rows)], there)
                sources.append((x_f, start))
        else:
            for hop in range(1, ys):
                start = y_base[step] + (hop - 1) * pair_rows
                there = here.device(y=shifted(y, -hop, ys))
                wires.arrive(second_slots[step, hop], y_f.at[pl.ds(start, pair_rows)], there)
                sources.append((y_f, start))
        add(w_v, f_rows(z_at, y, x), sources, pair_rows)
        for core in range(2):
            to_c = lax.rem(c + core, 2)
            source = w_v.at[rows_at(f_rows(z_at, y, x) + to_c * rows, rows)]
            target = out_f.at[z * 2 + c]
            if step == 0 and core == 0:
                keep(source, target)
            else:
                slot = ffn_z[step, core] = wires.slot()
                wires.start(slot, source, target, here.device(z=z_at, c=to_c))

    early = 2 * ys
    all_blocks = [(step, hop_y) for step in f_order for hop_y in y_order]
    for turn, (step, hop_y) in enumerate(all_blocks):
        grad_ffn(step, hop_y)
        if turn < early:
            f_send(step, hop_y)
    for k in reversed(range(1, zs - 1)):
        d_chain.onward(0, k)
        d_chain.onward(1, k)

    d_chain.last()

    def dmiddle_rows(at, first):
        ds2 = sd_v[at16(z * toks + first), :].astype(f32)
        middle = mid_v[at, :]
        inverse = inv_v[at, :][:, :1]
        s2 = middle * inverse
        grad = dy_v[at16(my_s2 + first), :].astype(f32) + inverse * (
            ds2 - s2 * jnp.mean(ds2 * s2, axis=1, keepdims=True)
        )
        input_grad[at, :] = grad.astype(low)

    each_rows(toks, dmiddle_rows)

    dbr_v = pr_v

    def dbr_view(x_at, c_at):
        return dbr_v.at[part_rows(x_at, c_at)]

    own_copy = keep(input_grad, dbr_view(x, c))
    dbr_cross = [wires.slot() for step in range(xs)]
    dbr_core = [wires.slot() for step in range(xs)]
    dbr_sent = [wires.start(dbr_core[0], input_grad, dbr_view(x, c), sibling)]
    for step in range(1, xs):
        there = here.device(x=shifted(x, step, xs))
        dbr_sent.append(wires.start(dbr_cross[step], input_grad, dbr_view(x, c), there))
    for step, exists in ((1, z < zs - 1), (-1, z > 0)):

        @pl.when(exists)
        def _(step=step):
            there = here.device(z=lax.clamp(0, z + step, zs - 1))
            pl.semaphore_signal(
                credit.at[(1 - step) // 2], inc=1, device_id=there, device_id_type=MESH
            )

    for step, hop_y in all_blocks[early:]:
        f_send(step, hop_y)
    for way, exists in enumerate((z < zs - 1, z > 0)):

        @pl.when(exists)
        def _(way=way):
            pl.semaphore_wait(credit.at[1 - way], 1)

    for k in reversed(range(1, zs)):
        o_chain.first(0, k)
        o_chain.first(1, k)
    f_across(f_order[1])
    for step in range(1, xs):
        from_x = shifted(x, -step, xs)
        view = dbr_view(from_x, c)
        wires.arrive(dbr_cross[step], view, here.device(x=from_x))
        wires.start(dbr_core[step], view, view, sibling)
    own_copy.wait()
    o_chain.onward(0, zs - 2)
    o_chain.onward(1, zs - 2)
    for step in range(xs):
        wires.arrive(dbr_core[step], dbr_view(shifted(x, -step, xs), 1 - c), sibling)
    da_v, dpr_v = hid_v, dgu_v
    qkv_rows = pl.ds(0, seq)

    def dattended_tile(n, carry):
        at = rows_at(lax.rem(n, row_blocks) * width, width)
        start = n // row_blocks * width
        cols = pl.ds(pl.multiple_of(start, width), width)
        w_cols = pl.ds(pl.multiple_of(proj + start, width), width)
        da_v[at, cols] = dot_nn(dbr_v[at, :], wa[:, w_cols]).astype(low)
        return carry

    lax.fori_loop(0, row_blocks * (heads // width), dattended_tile, 0)

    def grad_out_tile(n, carry):
        cols = pl.ds(pl.multiple_of(n * width, width), width)
        wa[cols, out_cols] = dot_tn(dbr_v[:, cols], att_v[...]).astype(low)
        return carry

    for done in qkv.sent + outw.sent:
        done()
    lax.fori_loop(0, MODEL // width, grad_out_tile, 0)

    far_first = [blocks[zs - 1 - turn] for turn in range(zs)]
    attn_y = {}

    def y_slot(hop, z_at):
        return ((hop - 1) * zs + z_at) * slab

    def attn_send_y(part, cols):
        for turn, z_at in enumerate(far_first):
            for hop in range(1, ys):
                y_at = shifted(y, hop, ys)
                slot = attn_y[part, turn, hop] = wires.slot()
                wires.start(
                    slot,
                    wa.at[rows_at((z_at * ys + y_at) * slab, slab), cols],
                    y_a.at[rows_at(y_slot(hop, z_at), slab), cols],
                    here.device(y=y_at),
                )

    def a_across(part, cols, turn):
        z_at = far_first[turn]
        sources = []
        for hop in range(1, ys):
            start = y_slot(hop, z_at)
            there = here.device(y=shifted(y, -hop, ys))
            wires.arrive(attn_y[part, turn, hop], y_a.at[rows_at(start, slab), cols], there)
            sources.append((y_a, start))
        add(wa, (z_at * ys + y) * slab, sources, slab, cols)

    def slab_rows(b):
        return (b * ys + y) * slab

    attn_chains = [
        Chain(wa, slab_rows, z_a, slab, 2, out_cols),
        Chain(wa, slab_rows, z_a, slab, 2, qkv_cols),
    ]

    def a_first(part, cols):
        for turn in range(zs):
            a_across(part, cols, turn)
            if turn < zs - 1:
                attn_chains[part].first(0, zs - 1 - turn)
                attn_chains[part].first(1, zs - 1 - turn)

    def a_onward(part, k):
        attn_chains[part].onward(0, k)
        attn_chains[part].onward(1, k)

    attn_send_y(0, out_cols)

    dkv_v[...] = jnp.zeros_like(dkv_v)

    def attend_back(step, carry):
        at = rows_at(lax.rem(step, row_blocks) * width, width)
        cols = pl.ds(pl.multiple_of(step // row_blocks * HEAD_DIM, HEAD_DIM), HEAD_DIM)
        exponent, total = weights_of(at, cols, lax.rem(step, row_blocks) * width)
        prob = exponent / total
        dout = da_v[at, cols]
        delta = jnp.sum(dout.astype(f32) * att_v[at, cols].astype(f32), axis=1, keepdims=True)
        dprob = dot_nt(dout, kv_v[:, HEAD_DIM:])
        dscore = (prob * (dprob - delta)).astype(low)
        dquery = dot_nn(dscore, kv_v[:, :HEAD_DIM]) * scale
        dpr_v[at, cols] = turned(dquery, at, -1.0).astype(low)
        dkv_v[:, :HEAD_DIM] += dot_tn(dscore, q_v[at, cols]) * scale
        dkv_v[:, HEAD_DIM:] += dot_tn(prob.astype(low), dout)
        return carry

    lax.fori_loop(0, row_blocks * (heads // HEAD_DIM), attend_back, 0)
    mine = rows_at(here.fs * toks, toks)
    dkv_v[mine, :] += kv_grad[...].astype(f32)

    def dkv_rows(step, carry):
        at = rows_at(step * width, width)
        dpr_v[at, pl.ds(heads, HEAD_DIM)] = turned(dkv_v[at, :HEAD_DIM], at, -1.0).astype(low)
        dpr_v[at, pl.ds(heads + HEAD_DIM, HEAD_DIM)] = dkv_v[at, HEAD_DIM:].astype(low)
        return carry

    lax.fori_loop(0, row_blocks, dkv_rows, 0)
    dn1_v = s2_v

    def dn1_tile(n, carry):
        cols = pl.ds(pl.multiple_of(n * width, width), width)
        dn1_v[qkv_rows, cols] = dot_nt(dpr_v[qkv_rows, qkv_cols], wa[cols, qkv_cols]).astype(low)
        return carry

    for done in s2s.sent:
        done()
    lax.fori_loop(0, MODEL // width, dn1_tile, 0)

    def grad_qkv_tile(n, carry):
        cols = pl.ds(pl.multiple_of(n * width, width), width)
        wa[cols, qkv_cols] = dot_tn(tok_v[:, cols], dpr_v[qkv_rows, qkv_cols]).astype(low)
        return carry

    lax.fori_loop(0, MODEL // width, grad_qkv_tile, 0)
    attn_send_y(1, qkv_cols)
    across, across_sent = reduce_sequence(dn1_v)

    f_across(f_order[0])
    for k in reversed(range(1, zs - 2)):
        o_chain.onward(0, k)
        o_chain.onward(1, k)
    a_first(0, out_cols)
    for k in reversed(range(1, zs - 1)):
        a_onward(0, k)
    f_out(f_order[1])
    for step in f_order[2:]:
        f_across(step)
    a_first(1, qkv_cols)
    f_out(f_order[0])
    for k in reversed(range(1, zs - 1)):
        a_onward(1, k)
    attn_chains[0].last()
    attn_chains[1].last()
    attn_f = {}
    for step in range(fsdp):
        other = shifted(here.fs, step, fsdp)
        source = wa.at[rows_at((here.dp * fsdp + other) * rows, rows)]
        target = out_a.at[here.fs]
        if step:
            slot = attn_f[step] = wires.slot()
            wires.start(slot, source, target, (here.dp, other))
        else:
            keep(source, target)
    for step in f_order[2:]:
        f_out(step)
    o_chain.last()

    def mixed_rows(at, first):
        mixed[at, :] = (mid_v[at, :] + so_v[at16(z * toks + first), :].astype(f32)).astype(low)

    each_rows(toks, mixed_rows)
    sequence_arrive(across)

    def input_rows(at, first):
        ds1 = sequence_total(first)
        values = tokens[at, :].astype(f32)
        inverse = lax.rsqrt(jnp.mean(values * values, axis=1, keepdims=True) + EPSILON)
        s1 = values * inverse
        back = inverse * (ds1 - s1 * jnp.mean(ds1 * s1, axis=1, keepdims=True))
        input_grad[at, :] = (input_grad[at, :].astype(f32) + back).astype(low)

    for done in dbr_sent:
        done()
    each_rows(toks, input_rows)
    for step in range(1, fsdp):
        other = shifted(here.fs, -step, fsdp)
        wires.arrive(attn_f[step], out_a.at[other], (here.dp, other))
    for step in range(zs):
        from_z = shifted(z, -step, zs)
        for core in range(2):
            if step or core:
                from_c = lax.rem(c + core, 2)
                wires.arrive(
                    ffn_z[step, core],
                    out_f.at[from_z * 2 + from_c],
                    here.device(z=from_z, c=from_c),
                )
    for copy in locals_[first_local + 1 :]:
        copy.wait()
    for chain in [d_chain, o_chain] + attn_chains:
        chain.drain()
    wires.drain()


def whole_block(place, w_qkv, w_out, w_gateup, w_down, tokens, dy, kv_grad, rope, key_at):
    toks = tokens.shape[0]
    zs, ys, xs, fsdp, rows = place.zs, place.ys, place.xs, place.fsdp, place.rows
    heads = place.heads
    seq = toks * fsdp
    every = zs * 2 * toks
    slab = fsdp * rows
    low, f32 = jnp.bfloat16, jnp.float32
    count = place.copies
    vmem = pl.BlockSpec(memory_space=pltpu.VMEM)
    hbm = pl.BlockSpec(memory_space=ANY)
    return pl.pallas_call(
        functools.partial(block_kernel, place),
        out_shape=(
            jax.ShapeDtypeStruct((toks, MODEL), low),
            jax.ShapeDtypeStruct((toks, KV), low),
            jax.ShapeDtypeStruct((toks, MODEL), low),
            jax.ShapeDtypeStruct((2 * zs, rows, place.ffn_width), low),
            jax.ShapeDtypeStruct((fsdp, rows, place.attn_width), low),
        ),
        in_specs=[hbm] * 4 + [vmem, hbm] + [vmem] * 3,
        out_specs=(vmem, vmem, vmem, hbm, hbm),
        scratch_shapes=[
            pltpu.VMEM((MODEL, place.attn_width), low),
            pltpu.VMEM((MODEL, place.ffn_width), low),
            pltpu.VMEM((seq, MODEL), low),
            pltpu.VMEM((every, MODEL), low),
            pltpu.VMEM((every, MODEL), low),
            pltpu.VMEM((every, place.block), low),
            pltpu.VMEM((every, 2 * place.block), low),
            pltpu.VMEM((seq, MODEL), low),
            pltpu.VMEM((xs * toks, MODEL), low),
            pltpu.VMEM((xs * toks, MODEL), low),
            pltpu.VMEM((toks, MODEL), f32),
            pltpu.VMEM((toks, LANES), f32),
            pltpu.VMEM((zs * toks, MODEL), low),
            pltpu.VMEM((zs * toks, MODEL), low),
            pltpu.VMEM((2 * (zs - 1) * toks, MODEL), low),
            pltpu.VMEM((seq, heads), low),
            pltpu.VMEM((seq, KV), low),
            pltpu.VMEM((seq, heads), low),
            pltpu.VMEM((seq, KV), f32),
            pltpu.VMEM(((xs - 1) * ((zs - 1) * ys + 1) * 2 * rows, place.ffn_width), low),
            pltpu.VMEM(((ys - 1) * (zs - 1 + xs) * 2 * rows, place.ffn_width), low),
            pltpu.VMEM(((ys - 1) * zs * slab, place.attn_width), low),
            pltpu.VMEM((2 * (zs - 1) * slab, place.attn_width), low),
            pltpu.SemaphoreType.DMA((16,)),
            pltpu.SemaphoreType.DMA((count,)),
            pltpu.SemaphoreType.DMA((count,)),
            pltpu.SemaphoreType.REGULAR((2,)),
        ],
        compiler_params=pltpu.CompilerParams(
            collective_id=0, has_side_effects=True, vmem_limit_bytes=63 * 2**20 + 2**19
        ),
        name="whole_block",
    )(w_qkv, w_out, w_gateup, w_down, tokens, dy, kv_grad, rope, key_at)


def on_device(
    place, tokens, lengths, gain_attn, w_qkv, w_out, gain_ffn, w_gateup, w_down, out_grad, kv_grad
):
    toks = tokens.shape[0]
    fsdp = place.fsdp
    seq = toks * fsdp
    low = jnp.bfloat16
    f32 = jnp.float32
    group = lax.axis_index("dp")
    length = jnp.sum(
        jnp.where(jnp.arange(lengths.shape[0], dtype=jnp.int32) == group, lengths, 0)
    )
    slots = np.arange(seq)
    at = slots % toks * fsdp + slots // toks
    frequency = THETA ** (-np.arange(HEAD_DIM // 2, dtype=np.float64) * (2.0 / HEAD_DIM))
    angles = at[:, None] * frequency[None, :]
    rope = jnp.asarray(np.concatenate([np.cos(angles), np.sin(angles)], axis=1), f32)
    positions = jnp.asarray(np.broadcast_to(at, (8, seq)), jnp.int32)
    key_at = jnp.where(positions < length, positions, seq)

    gain_a = gain_attn.astype(f32)[:, None]
    gain_f = gain_ffn.astype(f32)[:, None]
    folded_qkv = (w_qkv.astype(f32) * gain_a).astype(low)
    folded_gateup = (w_gateup.astype(f32) * gain_f).astype(low)
    mixed, shared_kv, input_grad, out_f, out_a = whole_block(
        place, folded_qkv, w_out, folded_gateup, w_down, tokens, out_grad, kv_grad,
        rope, key_at,
    )

    heads, block = place.heads, place.block
    duplicate = 2 * block - place.zone
    out_f = out_f.astype(f32)
    out_a = out_a.astype(f32)

    def columns(start):
        pieces = []
        for z_at in range(place.zs):
            pieces.append(out_f[2 * z_at, :, start : start + block])
            pieces.append(out_f[2 * z_at + 1, :, start + duplicate : start + block])
        return pieces

    plain_gateup = jnp.concatenate(columns(0) + columns(block), axis=1)
    grad_down = jnp.concatenate(columns(2 * block), axis=1)
    plain_qkv = jnp.concatenate(
        [out_a[at, :, :heads] for at in range(fsdp)]
        + [jnp.sum(out_a[:, :, heads : heads + KV], axis=0)],
        axis=1,
    )
    grad_out = jnp.concatenate([out_a[at, :, heads + KV :] for at in range(fsdp)], axis=1)
    grad_gain_attn = jnp.sum(w_qkv.astype(f32) * plain_qkv, axis=1)
    grad_gain_ffn = jnp.sum(w_gateup.astype(f32) * plain_gateup, axis=1)
    return (
        mixed,
        shared_kv,
        input_grad,
        grad_gain_attn,
        plain_qkv * gain_a,
        grad_out,
        grad_gain_ffn,
        plain_gateup * gain_f,
        grad_down,
    )


def solution(mesh):
    place = Place(mesh.shape["dp"], mesh.shape["fsdp"])
    row = P(("dp", "fsdp"), None)
    line = P(("dp", "fsdp"))
    return jax.shard_map(
        functools.partial(on_device, place),
        mesh=mesh,
        in_specs=(row, P(), line, row, row, line, row, row, row, row),
        out_specs=(row, row, row, line, row, row, line, row, row),
        check_vma=False,
    )
```

```python
import functools

import jax
import jax.numpy as jnp
import numpy as np
from jax import lax
from jax.experimental import pallas as pl
from jax.experimental.pallas import tpu as pltpu
from jax.sharding import PartitionSpec as P

HEADS = 16
HEAD_DIM = 128
FF = 5632
HQ = 2048
MODEL = 2048
KV = 2 * HEAD_DIM
LANES = 128

EPSILON = 1e-05
THETA = 10000.0
MASKED = -1e30
MESH = pl.DeviceIdType.MESH
ANY = pl.ANY


class Place:
    def __init__(self, dp_count, fsdp_count):
        self.fsdp = fsdp_count
        self.xs = fsdp_count // 2
        self.ys = self.xs
        self.zs = dp_count // self.ys
        self.rows = MODEL // (dp_count * fsdp_count)
        self.heads = HQ // fsdp_count
        self.attn_width = 2 * self.heads + KV
        self.zone = FF // self.zs
        self.block = LANES * -(-(self.zone // LANES) // 2)
        self.ffn_width = 3 * self.block
        zs, ys, xs, fsdp = self.zs, self.ys, self.xs, self.fsdp
        across = (ys - 1) + (xs - 1)
        line = 2 * (zs - 1)
        self.copies = (
            3 * (fsdp - 1) + 3 * (2 * zs - 1) + 2 * (line + (2 * zs - 1) * (ys - 1))
            + 2 * (line + 2 * zs - 1) + 2 * xs + 2 * (2 * xs - 1) + 2 * zs + 13 * line
            + 2 * zs * max(across + xs * (ys - 1), across + ys * (xs - 1))
            + 2 * zs * (ys - 1) + 2 * zs - 1 + fsdp - 1 + 2 * xs
        )


class Here:
    def __init__(self, place):
        self.place = place
        self.dp = lax.axis_index("dp")
        self.fs = lax.axis_index("fsdp")
        self.z = self.dp // place.ys
        self.y = lax.rem(self.dp, place.ys)
        self.x = self.fs // 2
        self.c = lax.rem(self.fs, 2)

    def device(self, z=None, y=None, x=None, c=None):
        z = self.z if z is None else z
        y = self.y if y is None else y
        x = self.x if x is None else x
        c = self.c if c is None else c
        return (z * self.place.ys + y, x * 2 + c)

    def sibling(self):
        return self.device(c=1 - self.c)


def shifted(value, step, count):
    return lax.rem(value + (step + count), count)


def rows_at(start, count):
    return pl.ds(pl.multiple_of(start, count), count)


def cols_at(start, count):
    return pl.ds(pl.multiple_of(start, LANES), count)


class Wires:
    def __init__(self, send, recv):
        self.send = send
        self.recv = recv
        self.used = 0
        self.finish = []

    def slot(self):
        self.used += 1
        return self.used - 1

    def copy(self, slot, source, target, device):
        return pltpu.make_async_remote_copy(
            src_ref=source,
            dst_ref=target,
            send_sem=self.send.at[slot],
            recv_sem=self.recv.at[slot],
            device_id=device,
            device_id_type=MESH,
        )

    def start(self, slot, source, target, device, when=None):
        copy = self.copy(slot, source, target, device)
        if when is None:
            copy.start()
            wait = copy.wait_send
        else:
            pl.when(when)(copy.start)

            def wait():
                pl.when(when)(copy.wait_send)

        self.finish.append(wait)

        def done():
            self.finish.remove(wait)
            wait()

        return done

    def arrive(self, slot, target, device, when=None):
        copy = self.copy(slot, target, target, device)
        if when is None:
            copy.wait_recv()
        else:
            pl.when(when)(copy.wait_recv)

    def drain(self):
        for wait in self.finish:
            wait()
        self.finish = []


def greet(devices):
    barrier = pltpu.get_barrier_semaphore()
    for device in devices:
        pl.semaphore_signal(barrier, inc=1, device_id=device, device_id_type=MESH)
    pl.semaphore_wait(barrier, len(devices))


def line_partners(here):
    place = here.place
    return [here.device(z=shifted(here.z, step, place.zs)) for step in range(1, place.zs)]


def plane_partners(here):
    place = here.place
    return [here.device(y=shifted(here.y, step, place.ys)) for step in range(1, place.ys)] + [
        here.device(x=shifted(here.x, step, place.xs)) for step in range(1, place.xs)
    ]


class Line:
    def __init__(self, wires, here, view):
        self.wires = wires
        self.here = here
        self.view = view
        count = here.place.zs
        self.count = count
        self.up = [wires.slot() for step in range(count - 1)]
        self.down = [wires.slot() for step in range(count - 1)]

    def send(self, step):
        here, count = self.here, self.count
        if step >= count - 1:
            return []
        z = here.z
        low = lax.max(z - step, 0)
        high = lax.min(z + step, count - 1)
        up = self.wires.start(
            self.up[step],
            self.view(low),
            self.view(low),
            here.device(z=lax.min(z + 1, count - 1)),
            when=(z >= step) & (z < count - 1),
        )
        down = self.wires.start(
            self.down[step],
            self.view(high),
            self.view(high),
            here.device(z=lax.max(z - 1, 0)),
            when=(z + step < count) & (z > 0),
        )
        return [up, down]

    def arrive(self, step):
        here, count = self.here, self.count
        z = here.z
        low = lax.max(z - step, 0)
        high = lax.min(z + step, count - 1)
        self.wires.arrive(
            self.up[step - 1], self.view(low), here.device(z=lax.max(z - 1, 0)), when=z >= step
        )
        self.wires.arrive(
            self.down[step - 1],
            self.view(high),
            here.device(z=lax.min(z + 1, count - 1)),
            when=z + step < count,
        )

    def valid(self, step):
        z = self.here.z
        if step == 0:
            return [(z, None)]
        return [
            (lax.max(z - step, 0), z >= step),
            (lax.min(z + step, self.count - 1), z + step < self.count),
        ]


def each_rows(count, body, size=16):
    def step(index, carry):
        body(pl.ds(pl.multiple_of(index * size, size), size), index * size)
        return carry

    lax.fori_loop(0, count // size, step, 0)


def dot_nn(left, right):
    return lax.dot_general(
        left, right, (((1,), (0,)), ((), ())), preferred_element_type=jnp.float32
    )


def dot_nt(left, right):
    return lax.dot_general(
        left, right, (((1,), (1,)), ((), ())), preferred_element_type=jnp.float32
    )


def dot_tn(left, right):
    return lax.dot_general(
        left, right, (((0,), (0,)), ((), ())), preferred_element_type=jnp.float32
    )


def visit_order(count):
    orders = []
    for z in range(count):
        far = sorted(range(count), key=lambda other: (abs(other - z), other))
        orders.append(far)
    return orders


def chosen(z, turn, orders):
    total = 0
    for z_at, order in enumerate(orders):
        here = jnp.where(z == z_at, 1, 0)
        for turn_at, value in enumerate(order):
            if isinstance(turn, int):
                if turn == turn_at:
                    total = total + here * value
            else:
                total = total + here * jnp.where(turn == turn_at, 1, 0) * value
    return total


def block_kernel(
    place, w_qkv, w_out, w_gateup, w_down, tokens, dy, kv_grad, rope, key_at,
    mixed, shared_kv, input_grad, out_f, out_a,
    wa, w_v, tok_v, dy_v, s2_v, hid_v, dgu_v, pr_v, ps_v, px_v, mid_v, inv_v,
    so_v, sd_v, z_land, q_v, kv_v, att_v, dkv_v,
    x_f, y_f, y_a, z_a, local, send, recv, credit,
):
    here = Here(place)
    wires = Wires(send, recv)
    z, y, x, c = here.z, here.y, here.x, here.c
    zs, ys, xs, fsdp, rows = place.zs, place.ys, place.xs, place.fsdp, place.rows
    heads, block, zone = place.heads, place.block, place.zone
    proj = heads + KV
    toks = tokens.shape[0]
    seq = toks * fsdp
    pair = 2 * toks
    slab = fsdp * rows
    width = 256
    low = jnp.bfloat16
    f32 = jnp.float32
    scale = HEAD_DIM ** (-0.5)
    sibling = here.sibling()
    partners = line_partners(here) + plane_partners(here)
    partners += [here.device(x=shifted(x, step, xs), c=1 - c) for step in range(xs)]
    partners += [here.device(z=shifted(z, step, zs), c=1 - c) for step in range(1, zs)]
    greet(partners)

    def index(z=z, y=y, x=x, c=c):
        return (z * ys + y) * fsdp + x * 2 + c

    locals_ = []

    def keep(source, target):
        copy = pltpu.make_async_copy(source, target, local.at[len(locals_)])
        copy.start()
        locals_.append(copy)
        return copy

    def at16(start):
        return pl.ds(pl.multiple_of(start, 16), 16)

    def add(target, start, sources, count, cols=slice(None)):
        def step(at, first):
            at = at16(start + first)
            total = target[at, cols].astype(f32)
            for source, source_start in sources:
                total = total + source[at16(source_start + first), cols].astype(f32)
            target[at, cols] = total.astype(low)

        each_rows(count, step)

    own_rows = rows_at(index() * rows, rows)
    qkv_cols, out_cols = pl.ds(0, proj), pl.ds(proj, heads)

    def qkv_pieces(owner):
        return [(w_qkv, owner * heads, heads, 0), (w_qkv, HQ, KV, heads)]

    def out_pieces(owner):
        return [(w_out, owner * heads, heads, proj)]

    def attn_spread(pieces):
        slots = []
        for step in range(1, fsdp):
            other = shifted(here.fs, step, fsdp)
            for ref, start, count, place_at in pieces(other):
                slot = wires.slot()
                slots.append((slot, step, count, place_at))
                wires.start(
                    slot,
                    ref.at[:, cols_at(start, count)],
                    wa.at[own_rows, pl.ds(place_at, count)],
                    (here.dp, other),
                )
        for ref, start, count, place_at in pieces(here.fs):
            keep(ref.at[:, cols_at(start, count)], wa.at[own_rows, pl.ds(place_at, count)])
        return slots

    def attn_collect(slots):
        for slot, step, count, place_at in slots:
            other = shifted(here.fs, -step, fsdp)
            at = rows_at((here.dp * fsdp + other) * rows, rows)
            wires.arrive(slot, wa.at[at, pl.ds(place_at, count)], (here.dp, other))

    def ffn_pieces(zone_z, core):
        start = zone_z * zone + core * (zone - block)
        return [(w_gateup, start, 0), (w_gateup, FF + start, block), (w_down, start, 2 * block)]

    ffn_slots = {}

    def ffn_spread(step):
        for core in range(2):
            to_z, to_c = shifted(z, step, zs), lax.rem(c + core, 2)
            for ref, start, place_at in ffn_pieces(to_z, to_c):
                source = ref.at[:, cols_at(start, block)]
                target = w_v.at[own_rows, pl.ds(place_at, block)]
                if step == 0 and core == 0:
                    keep(source, target)
                    continue
                slot = wires.slot()
                ffn_slots.setdefault(step, []).append((slot, core, place_at))
                wires.start(slot, source, target, here.device(z=to_z, c=to_c))

    def ffn_collect(step):
        from_z = shifted(z, -step, zs)
        for slot, core, place_at in ffn_slots[step]:
            from_c = lax.rem(c + core, 2)
            at = rows_at(index(z=from_z, c=from_c) * rows, rows)
            wires.arrive(slot, w_v.at[at, pl.ds(place_at, block)], here.device(z=from_z, c=from_c))

    def w_view(z_at, y_at, x_at):
        return w_v.at[rows_at(index(z_at, y_at, x_at, 0) * rows, 2 * rows)]

    near, far = {}, {}
    w_sent = []

    def axes(step):
        ways = [("y", y, ys), ("x", x, xs)]
        return ways if step else ways[::-1]

    def at_plane(name, value, other):
        return {"y_at": value, "x_at": other} if name == "y" else {"y_at": other, "x_at": value}

    def to_plane(name, value):
        return here.device(y=value) if name == "y" else here.device(x=value)

    def ffn_send(slots, key, name, me, count, view):
        for hop in range(1, count):
            slot = slots[key + (hop,)] = wires.slot()
            w_sent.append(wires.start(slot, view, view, to_plane(name, shifted(me, hop, count))))

    def ffn_near(step):
        z_at = shifted(z, -step, zs)
        first, me, count = axes(step)[0]
        ffn_send(near, (step,), first, me, count, w_view(z_at, y, x))

    def ffn_far(step):
        z_at = shifted(z, -step, zs)
        second, me, count = axes(step)[1]
        ffn_send(far, (step, 0), second, me, count, w_view(z_at, y, x))

    def ffn_forward(step):
        ffn_collect(step)
        ffn_near(step)
        ffn_far(step)

    def ffn_across(step):
        z_at = shifted(z, -step, zs)
        (first, me, count), (second, me2, count2) = axes(step)
        for hop in range(1, count):
            origin = shifted(me, -hop, count)
            view = w_view(z_at, **at_plane(first, origin, me2))
            wires.arrive(near[step, hop], view, to_plane(first, origin))
            ffn_send(far, (step, hop), second, me2, count2, view)

    def ffn_arrive(step):
        z_at = shifted(z, -step, zs)
        (first, me, count), (second, me2, count2) = axes(step)
        for hop in range(count):
            for hop2 in range(1, count2):
                origin, origin2 = shifted(me, -hop, count), shifted(me2, -hop2, count2)
                view = w_view(z_at, **at_plane(first, origin, origin2))
                wires.arrive(far[step, hop, hop2], view, to_plane(second, origin2))

    class Spread:
        def __init__(self, cols):
            self.cols = cols
            self.line = Line(wires, here, lambda z_at: self.view(z_at, y))
            self.plane = {}
            self.sent = []

        def view(self, z_at, y_at):
            return wa.at[rows_at((z_at * ys + y_at) * slab, slab), self.cols]

        def step(self, step):
            if step:
                self.line.arrive(step)
            self.sent += self.line.send(step)
            for side, (z_at, exists) in enumerate(self.line.valid(step)):
                for hop in range(1, ys):
                    slot = self.plane[step, side, hop] = wires.slot()
                    view = self.view(z_at, y)
                    there = here.device(y=shifted(y, hop, ys))
                    self.sent.append(wires.start(slot, view, view, there, when=exists))

        def crossed(self):
            for step in range(zs):
                for side, (z_at, exists) in enumerate(self.line.valid(step)):
                    for hop in range(1, ys):
                        from_y = shifted(y, -hop, ys)
                        wires.arrive(
                            self.plane[step, side, hop],
                            self.view(z_at, from_y),
                            here.device(y=from_y),
                            when=exists,
                        )

    class Acts:
        def __init__(self, ref):
            self.ref = ref
            self.line = Line(wires, here, lambda z_at: self.view(z_at, c))
            self.core = {}
            self.sent = []

        def view(self, z_at, c_at):
            return self.ref.at[rows_at((z_at * 2 + c_at) * toks, toks)]

        def step(self, step):
            if step:
                self.line.arrive(step)
            self.sent += self.line.send(step)
            for side, (z_at, exists) in enumerate(self.line.valid(step)):
                slot = self.core[step, side] = wires.slot()
                view = self.view(z_at, c)
                self.sent.append(wires.start(slot, view, view, sibling, when=exists))

        def crossed(self, step):
            for side, (z_at, exists) in enumerate(self.line.valid(step)):
                wires.arrive(self.core[step, side], self.view(z_at, 1 - c), sibling, when=exists)

    def tok_view(x_at, c_at):
        return tok_v.at[rows_at((x_at * 2 + c_at) * toks, toks)]

    qkv_slots = attn_spread(qkv_pieces)
    ffn_spread(0)
    ffn_spread(1)
    keep(tokens, tok_view(x, c))
    tok_cross = [wires.slot() for step in range(xs)]
    tok_core = [wires.slot() for step in range(xs)]
    wires.start(tok_core[0], tokens, tok_view(x, c), sibling)
    for step in range(1, xs):
        wires.start(
            tok_cross[step], tokens, tok_view(x, c), here.device(x=shifted(x, step, xs))
        )
    out_slots = attn_spread(out_pieces)
    dys = Acts(dy_v)
    keep(dy, dys.view(z, c))
    for copy in locals_:
        copy.wait()
    first_local = len(locals_)
    ffn_collect(0)
    ffn_near(0)
    attn_collect(qkv_slots)
    qkv = Spread(qkv_cols)
    qkv.step(0)
    attn_collect(out_slots)
    outw = Spread(out_cols)
    outw.step(0)
    ffn_collect(1)
    ffn_far(1)
    tok_sent = []
    for step in range(1, xs):
        from_x = shifted(x, -step, xs)
        view = tok_view(from_x, c)
        wires.arrive(tok_cross[step], view, here.device(x=from_x))
        tok_sent.append(wires.start(tok_core[step], view, view, sibling))
    qkv.step(1)
    outw.step(1)
    for step in range(xs):
        from_x = shifted(x, -step, xs)
        wires.arrive(tok_core[step], tok_view(from_x, 1 - c), sibling)
    for done in tok_sent:
        done()

    def norm_rows(at, first):
        values = tok_v[at, :].astype(f32)
        inverse = lax.rsqrt(jnp.mean(values * values, axis=1, keepdims=True) + EPSILON)
        tok_v[at, :] = (values * inverse).astype(low)

    each_rows(seq, norm_rows)
    qkv.step(2)
    outw.step(2)
    late = [zs - 1] + list(range(2, zs - 1))
    for step in late:
        ffn_spread(step)
    dys.step(0)
    for step in range(3, zs):
        qkv.step(step)
        outw.step(step)
    ffn_far(0)
    ffn_across(0)
    ffn_near(1)
    qkv.crossed()

    half = HEAD_DIM // 2

    def turned(values, at, sign):
        table = rope[at, :]
        across = pltpu.roll(table, half, 1)
        low_half = lax.broadcasted_iota(jnp.int32, table.shape, 1) < half
        cosine = jnp.where(low_half, table, across)
        sine_part = jnp.where(low_half, -across, table)
        return values * cosine + pltpu.roll(values, half, 1) * (sign * sine_part)

    row_blocks = seq // width

    def project(step, carry):
        at = rows_at(step * width, width)

        def query_tile(j, carry):
            cols = pl.ds(pl.multiple_of(j * HEAD_DIM, HEAD_DIM), HEAD_DIM)
            q_v[at, cols] = turned(dot_nn(tok_v[at, :], wa[:, cols]), at, 1.0).astype(low)
            return carry

        lax.fori_loop(0, heads // HEAD_DIM, query_tile, 0)
        both = dot_nn(tok_v[at, :], wa[:, pl.ds(heads, KV)])
        kv_v[at, :HEAD_DIM] = turned(both[:, :HEAD_DIM], at, 1.0).astype(low)
        kv_v[at, HEAD_DIM:] = both[:, HEAD_DIM:].astype(low)
        return carry

    lax.fori_loop(0, row_blocks, project, 0)
    shared_kv[...] = kv_v[rows_at(here.fs * toks, toks), :]

    def weights_of(at, cols, first):
        scores = dot_nt(q_v[at, cols], kv_v[:, :HEAD_DIM]) * scale
        row = lax.broadcasted_iota(jnp.int32, (width, LANES), 0) + first
        query_at = lax.rem(row, toks) * fsdp + row // toks
        allowed = key_at[0:1, :] <= query_at[:, :1]
        scores = jnp.where(allowed, scores, MASKED)
        exponent = jnp.exp(scores - jnp.max(scores, axis=1, keepdims=True))
        return exponent, jnp.sum(exponent, axis=1, keepdims=True)

    def attend(step, carry):
        at = rows_at(lax.rem(step, row_blocks) * width, width)
        cols = pl.ds(pl.multiple_of(step // row_blocks * HEAD_DIM, HEAD_DIM), HEAD_DIM)
        exponent, total = weights_of(at, cols, lax.rem(step, row_blocks) * width)
        att_v[at, cols] = (dot_nn(exponent.astype(low), kv_v[:, HEAD_DIM:]) / total).astype(low)
        return carry

    ffn_forward(late[0])
    lax.fori_loop(0, row_blocks * (heads // HEAD_DIM), attend, 0)
    outw.crossed()

    def branch_tile(n, carry):
        cols = pl.ds(pl.multiple_of(n * width, width), width)
        pr_v[:, cols] = dot_nt(att_v[...], wa[cols, out_cols]).astype(low)
        return carry

    lax.fori_loop(0, MODEL // width, branch_tile, 0)

    def part_rows(x_at, c_at):
        return rows_at((x_at * 2 + c_at) * toks, toks)

    def x_rows(x_at):
        return rows_at(x_at * toks, toks)

    x_order = list(range(1, xs)) + [0]

    def reduce_sequence(source):
        sib = [wires.slot() for step in range(xs)]
        across = {}
        sent = []
        for step in x_order:
            x_at = shifted(x, step, xs)
            sent.append(
                wires.start(
                    sib[step], source.at[part_rows(x_at, 1 - c)], ps_v.at[x_rows(x_at)], sibling
                )
            )
        for step in x_order:
            x_at = shifted(x, step, xs)
            wires.arrive(sib[step], ps_v.at[x_rows(x_at)], sibling)
            add(ps_v, x_at * toks, [(source, (x_at * 2 + c) * toks)], toks)
            if step == x_order[0]:
                for done in sent:
                    done()
            if step:
                across[step] = wires.slot()
                sent.append(
                    wires.start(
                        across[step], ps_v.at[x_rows(x_at)], px_v.at[x_rows(x)], here.device(x=x_at)
                    )
                )
        return across, sent[xs:]

    def sequence_arrive(across):
        for step in range(1, xs):
            from_x = shifted(x, -step, xs)
            wires.arrive(across[step], px_v.at[x_rows(from_x)], here.device(x=from_x))

    def sequence_total(first):
        total = ps_v[at16(x * toks + first), :].astype(f32)
        for step in range(1, xs):
            total = total + px_v[at16(shifted(x, -step, xs) * toks + first), :].astype(f32)
        return total

    across, across_sent = reduce_sequence(pr_v)
    sequence_arrive(across)
    s2s = Acts(s2_v)
    my_s2 = (z * 2 + c) * toks

    def middle_rows(at, first):
        middle = tokens[at, :].astype(f32) + sequence_total(first)
        inverse = lax.rsqrt(jnp.mean(middle * middle, axis=1, keepdims=True) + EPSILON)
        mid_v[at, :] = middle
        inv_v[at, :] = jnp.broadcast_to(inverse, (16, LANES))
        s2_v[at16(my_s2 + first), :] = (middle * inverse).astype(low)

    each_rows(toks, middle_rows)
    s2s.step(0)
    for step in late[1:]:
        ffn_forward(step)
    ffn_across(1)
    dys.step(1)
    ffn_across(late[0])
    s2s.step(1)
    for step in late[1:]:
        ffn_across(step)
    dys.step(2)
    s2s.step(2)
    for done in across_sent:
        done()
    for step in range(zs):
        ffn_arrive(step)
    orders = visit_order(zs)
    blocks = [chosen(z, turn, orders) for turn in range(zs)]
    duplicate = 2 * block - zone

    def hidden(b):
        at = rows_at(b * pair, pair)

        def hidden_tile(j, carry):
            def cols(base):
                return pl.ds(pl.multiple_of(base + j * width, width), width)

            gate = dot_nn(s2_v[at, :], w_v[:, cols(0)])
            up = dot_nn(s2_v[at, :], w_v[:, cols(block)])
            dhid = dot_nn(dy_v[at, :], w_v[:, cols(2 * block)])
            sg = 1.0 / (1.0 + jnp.exp(-gate))
            lane = lax.broadcasted_iota(jnp.int32, gate.shape, 1) + j * width
            mine = (lane >= duplicate) | (c == 0)
            act = gate * sg
            hid_v[at, cols(0)] = jnp.where(mine, act * up, 0.0).astype(low)
            dgate = dhid * up * sg * (1.0 + gate * (1.0 - sg))
            dgu_v[at, cols(0)] = jnp.where(mine, dgate, 0.0).astype(low)
            dgu_v[at, cols(block)] = jnp.where(mine, dhid * act, 0.0).astype(low)
            return carry

        lax.fori_loop(0, block // width, hidden_tile, 0)

    pd_v, po_v = px_v, ps_v

    def back(b):
        at = rows_at(b * pair, pair)

        def back_tile(n, carry):
            cols = pl.ds(pl.multiple_of(n * width, width), width)
            pd_v[pl.ds(0, pair), cols] = dot_nt(
                dgu_v[at, :], w_v[cols, pl.ds(0, 2 * block)]
            ).astype(low)
            po_v[pl.ds(0, pair), cols] = dot_nt(hid_v[at, :], w_v[cols, pl.ds(2 * block, block)]).astype(low)
            return carry

        lax.fori_loop(0, MODEL // width, back_tile, 0)

    class Chain:
        def __init__(self, own, own_start, landing, count, pieces, cols=slice(None)):
            self.cols = cols
            self.own, self.own_start, self.landing = own, own_start, landing
            self.count, self.pieces, self.size = count, pieces, count // pieces
            self.slots = {}
            for way in range(2):
                for k in range(1, zs):
                    for piece in range(pieces):
                        self.slots[way, k, piece] = wires.slot()

        def owner(self, way, k):
            return lax.min(z + k, zs - 1) if way == 0 else lax.max(z - k, 0)

        def exists(self, way, k):
            return z + k < zs if way == 0 else z >= k

        def feeds(self, way):
            return z > 0 if way == 0 else z < zs - 1

        def land(self, way, k, piece):
            return (way * (zs - 1) + k - 1) * self.count + piece * self.size

        def copy(self, way, k, piece):
            start = self.own_start(self.owner(way, k)) + piece * self.size
            return wires.copy(
                self.slots[way, k, piece],
                self.own.at[rows_at(start, self.size), self.cols],
                self.landing.at[pl.ds(self.land(way, k, piece), self.size), self.cols],
                here.device(z=self.owner(way, 1)),
            )

        def take(self, way, k, piece):
            land = self.land(way, k + 1, piece)
            view = self.landing.at[pl.ds(land, self.size), self.cols]
            wires.copy(
                self.slots[way, k + 1, piece], view, view, here.device(z=self.owner(1 - way, 1))
            ).wait_recv()
            owner = z if k == 0 else self.owner(way, k)
            start = self.own_start(owner) + piece * self.size
            add(self.own, start, [(self.landing, land)], self.size, self.cols)

        def first(self, way, k):
            @pl.when(jnp.logical_not(self.feeds(way)) & self.exists(way, k))
            def _():
                for piece in range(self.pieces):
                    self.copy(way, k, piece).start()

        def onward(self, way, k):
            if k == zs - 1:
                return

            @pl.when(self.feeds(way) & self.exists(way, k))
            def _():
                for piece in range(self.pieces):
                    self.take(way, k, piece)
                    self.copy(way, k, piece).start()

        def last(self):
            for way in range(2):

                @pl.when(self.feeds(way))
                def _(way=way):
                    for piece in range(self.pieces):
                        self.take(way, 0, piece)

        def drain(self):
            for way in range(2):
                for k in range(1, zs):

                    @pl.when(self.exists(way, k))
                    def _(way=way, k=k):
                        for piece in range(self.pieces):
                            self.copy(way, k, piece).wait_send()

    def line_rows(b):
        return b * toks

    kinds = ((pd_v, sd_v), (po_v, so_v))
    d_chain = Chain(sd_v, line_rows, z_land, toks, 8)
    o_chain = Chain(so_v, line_rows, z_land, toks, 1)
    shares = {}

    def share(turn, b):
        for kind, (buffer, landing) in enumerate(kinds):
            slot = wires.slot()
            done = wires.start(
                slot,
                buffer.at[rows_at((1 - c) * toks, toks)],
                landing.at[rows_at(b * toks, toks)],
                sibling,
            )
            shares[turn, kind] = (slot, done)

    def add_up(turn, b):
        for kind, (buffer, landing) in enumerate(kinds):
            slot, done = shares[turn, kind]
            wires.arrive(slot, landing.at[rows_at(b * toks, toks)], sibling)
            add(landing, b * toks, [(buffer, c * toks)], toks)
            done()
            if turn and kind == 0:
                d_chain.first(0, turn)
                d_chain.first(1, turn)

    relays = [
        (acts, step) for step in range(2, zs) for acts in (dys, s2s)
    ][2:]
    s2s.crossed(0)
    dys.crossed(0)
    for turn in range(zs):
        if turn:
            while relays and relays[0][1] <= turn:
                acts, step = relays.pop(0)
                acts.step(step)
            s2s.crossed(turn)
            dys.crossed(turn)
        hidden(blocks[turn])
        if turn:
            add_up(turn - 1, blocks[turn - 1])
        back(blocks[turn])
        share(turn, blocks[turn])
        if relays:
            acts, step = relays.pop(0)
            acts.step(step)
    add_up(zs - 1, blocks[zs - 1])
    for done in w_sent:
        done()

    f_order = list(range(1, zs)) + [0]
    y_order = list(range(1, ys)) + [0]
    pair_rows = 2 * rows
    first_slots, second_slots, ffn_z = {}, {}, {}

    def y_first(step):
        return step == f_order[0]

    x_base, y_base = {}, {}
    x_used = y_used = 0
    for step in f_order:
        x_base[step], y_base[step] = x_used, y_used
        x_used += (xs - 1) * pair_rows * (1 if y_first(step) else ys)
        y_used += (ys - 1) * pair_rows * (xs if y_first(step) else 1)

    def f_rows(z_at, y_at, x_at):
        return index(z_at, y_at, x_at, 0) * rows

    def grad_ffn(step, hop_y):
        z_at, y_at = shifted(z, step, zs), shifted(y, hop_y, ys)

        def tile(n, carry):
            cols = pl.ds(pl.multiple_of((z_at * ys + y_at) * slab + n * LANES, LANES), LANES)
            w_v[cols, pl.ds(0, 2 * block)] = dot_tn(s2_v[:, cols], dgu_v[...]).astype(low)
            w_v[cols, pl.ds(2 * block, block)] = dot_tn(dy_v[:, cols], hid_v[...]).astype(low)
            return carry

        lax.fori_loop(0, slab // LANES, tile, 0)

    def f_send(step, hop_y):
        z_at, y_at = shifted(z, step, zs), shifted(y, hop_y, ys)
        if y_first(step):
            if hop_y:
                slot = first_slots[step, hop_y] = wires.slot()
                wires.start(
                    slot,
                    w_v.at[rows_at(f_rows(z_at, y_at, 0), slab)],
                    y_f.at[pl.ds(y_base[step] + (hop_y - 1) * slab, slab)],
                    here.device(y=y_at),
                )
            return
        for hop in range(1, xs):
            x_at = shifted(x, hop, xs)
            slot = first_slots[step, hop_y, hop] = wires.slot()
            wires.start(
                slot,
                w_v.at[rows_at(f_rows(z_at, y_at, x_at), pair_rows)],
                x_f.at[rows_at(x_base[step] + ((hop - 1) * ys + y_at) * pair_rows, pair_rows)],
                here.device(x=x_at),
            )

    def f_across(step):
        z_at = shifted(z, step, zs)
        if y_first(step):
            sources = []
            for hop in range(1, ys):
                start = y_base[step] + (hop - 1) * slab
                there = here.device(y=shifted(y, -hop, ys))
                wires.arrive(first_slots[step, hop], y_f.at[pl.ds(start, slab)], there)
                sources.append((y_f, start))
            add(w_v, f_rows(z_at, y, 0), sources, slab)
            for hop in range(1, xs):
                x_at = shifted(x, hop, xs)
                slot = second_slots[step, hop] = wires.slot()
                wires.start(
                    slot,
                    w_v.at[rows_at(f_rows(z_at, y, x_at), pair_rows)],
                    x_f.at[pl.ds(x_base[step] + (hop - 1) * pair_rows, pair_rows)],
                    here.device(x=x_at),
                )
            return
        for hop_y in y_order:
            y_at = shifted(y, hop_y, ys)
            sources = []
            for hop in range(1, xs):
                start = x_base[step] + ((hop - 1) * ys + y_at) * pair_rows
                there = here.device(x=shifted(x, -hop, xs))
                view = x_f.at[rows_at(start, pair_rows)]
                wires.arrive(first_slots[step, hop_y, hop], view, there)
                sources.append((x_f, start))
            add(w_v, f_rows(z_at, y_at, x), sources, pair_rows)
            if hop_y:
                slot = second_slots[step, hop_y] = wires.slot()
                wires.start(
                    slot,
                    w_v.at[rows_at(f_rows(z_at, y_at, x), pair_rows)],
                    y_f.at[pl.ds(y_base[step] + (hop_y - 1) * pair_rows, pair_rows)],
                    here.device(y=y_at),
                )

    def f_out(step):
        z_at = shifted(z, step, zs)
        sources = []
        if y_first(step):
            for hop in range(1, xs):
                start = x_base[step] + (hop - 1) * pair_rows
                there = here.device(x=shifted(x, -hop, xs))
                wires.arrive(second_slots[step, hop], x_f.at[pl.ds(start, pair_rows)], there)
                sources.append((x_f, start))
        else:
            for hop in range(1, ys):
                start = y_base[step] + (hop - 1) * pair_rows
                there = here.device(y=shifted(y, -hop, ys))
                wires.arrive(second_slots[step, hop], y_f.at[pl.ds(start, pair_rows)], there)
                sources.append((y_f, start))
        add(w_v, f_rows(z_at, y, x), sources, pair_rows)
        for core in range(2):
            to_c = lax.rem(c + core, 2)
            source = w_v.at[rows_at(f_rows(z_at, y, x) + to_c * rows, rows)]
            target = out_f.at[z * 2 + c]
            if step == 0 and core == 0:
                keep(source, target)
            else:
                slot = ffn_z[step, core] = wires.slot()
                wires.start(slot, source, target, here.device(z=z_at, c=to_c))

    early = 2 * ys
    all_blocks = [(step, hop_y) for step in f_order for hop_y in y_order]
    for turn, (step, hop_y) in enumerate(all_blocks):
        grad_ffn(step, hop_y)
        if turn < early:
            f_send(step, hop_y)
    for k in reversed(range(1, zs - 1)):
        d_chain.onward(0, k)
        d_chain.onward(1, k)

    d_chain.last()

    def dmiddle_rows(at, first):
        ds2 = sd_v[at16(z * toks + first), :].astype(f32)
        middle = mid_v[at, :]
        inverse = inv_v[at, :][:, :1]
        s2 = middle * inverse
        grad = dy_v[at16(my_s2 + first), :].astype(f32) + inverse * (
            ds2 - s2 * jnp.mean(ds2 * s2, axis=1, keepdims=True)
        )
        input_grad[at, :] = grad.astype(low)

    each_rows(toks, dmiddle_rows)

    dbr_v = pr_v

    def dbr_view(x_at, c_at):
        return dbr_v.at[part_rows(x_at, c_at)]

    own_copy = keep(input_grad, dbr_view(x, c))
    dbr_cross = [wires.slot() for step in range(xs)]
    dbr_core = [wires.slot() for step in range(xs)]
    dbr_sent = [wires.start(dbr_core[0], input_grad, dbr_view(x, c), sibling)]
    for step in range(1, xs):
        there = here.device(x=shifted(x, step, xs))
        dbr_sent.append(wires.start(dbr_cross[step], input_grad, dbr_view(x, c), there))
    for step, exists in ((1, z < zs - 1), (-1, z > 0)):

        @pl.when(exists)
        def _(step=step):
            there = here.device(z=lax.clamp(0, z + step, zs - 1))
            pl.semaphore_signal(
                credit.at[(1 - step) // 2], inc=1, device_id=there, device_id_type=MESH
            )

    for step, hop_y in all_blocks[early:]:
        f_send(step, hop_y)
    for way, exists in enumerate((z < zs - 1, z > 0)):

        @pl.when(exists)
        def _(way=way):
            pl.semaphore_wait(credit.at[1 - way], 1)

    for k in reversed(range(1, zs)):
        o_chain.first(0, k)
        o_chain.first(1, k)
    f_across(f_order[1])
    for step in range(1, xs):
        from_x = shifted(x, -step, xs)
        view = dbr_view(from_x, c)
        wires.arrive(dbr_cross[step], view, here.device(x=from_x))
        wires.start(dbr_core[step], view, view, sibling)
    own_copy.wait()
    o_chain.onward(0, zs - 2)
    o_chain.onward(1, zs - 2)
    for step in range(xs):
        wires.arrive(dbr_core[step], dbr_view(shifted(x, -step, xs), 1 - c), sibling)
    da_v, dpr_v = hid_v, dgu_v
    qkv_rows = pl.ds(0, seq)

    def dattended_tile(n, carry):
        at = rows_at(lax.rem(n, row_blocks) * width, width)
        start = n // row_blocks * width
        cols = pl.ds(pl.multiple_of(start, width), width)
        w_cols = pl.ds(pl.multiple_of(proj + start, width), width)
        da_v[at, cols] = dot_nn(dbr_v[at, :], wa[:, w_cols]).astype(low)
        return carry

    lax.fori_loop(0, row_blocks * (heads // width), dattended_tile, 0)

    def grad_out_tile(n, carry):
        cols = pl.ds(pl.multiple_of(n * width, width), width)
        wa[cols, out_cols] = dot_tn(dbr_v[:, cols], att_v[...]).astype(low)
        return carry

    for done in qkv.sent + outw.sent:
        done()
    lax.fori_loop(0, MODEL // width, grad_out_tile, 0)

    far_first = [blocks[zs - 1 - turn] for turn in range(zs)]
    attn_y = {}

    def y_slot(hop, z_at):
        return ((hop - 1) * zs + z_at) * slab

    def attn_send_y(part, cols):
        for turn, z_at in enumerate(far_first):
            for hop in range(1, ys):
                y_at = shifted(y, hop, ys)
                slot = attn_y[part, turn, hop] = wires.slot()
                wires.start(
                    slot,
                    wa.at[rows_at((z_at * ys + y_at) * slab, slab), cols],
                    y_a.at[rows_at(y_slot(hop, z_at), slab), cols],
                    here.device(y=y_at),
                )

    def a_across(part, cols, turn):
        z_at = far_first[turn]
        sources = []
        for hop in range(1, ys):
            start = y_slot(hop, z_at)
            there = here.device(y=shifted(y, -hop, ys))
            wires.arrive(attn_y[part, turn, hop], y_a.at[rows_at(start, slab), cols], there)
            sources.append((y_a, start))
        add(wa, (z_at * ys + y) * slab, sources, slab, cols)

    def slab_rows(b):
        return (b * ys + y) * slab

    attn_chains = [
        Chain(wa, slab_rows, z_a, slab, 2, out_cols),
        Chain(wa, slab_rows, z_a, slab, 2, qkv_cols),
    ]

    def a_first(part, cols):
        for turn in range(zs):
            a_across(part, cols, turn)
            if turn < zs - 1:
                attn_chains[part].first(0, zs - 1 - turn)
                attn_chains[part].first(1, zs - 1 - turn)

    def a_onward(part, k):
        attn_chains[part].onward(0, k)
        attn_chains[part].onward(1, k)

    attn_send_y(0, out_cols)

    dkv_v[...] = jnp.zeros_like(dkv_v)

    def attend_back(step, carry):
        at = rows_at(lax.rem(step, row_blocks) * width, width)
        cols = pl.ds(pl.multiple_of(step // row_blocks * HEAD_DIM, HEAD_DIM), HEAD_DIM)
        exponent, total = weights_of(at, cols, lax.rem(step, row_blocks) * width)
        prob = exponent / total
        dout = da_v[at, cols]
        delta = jnp.sum(dout.astype(f32) * att_v[at, cols].astype(f32), axis=1, keepdims=True)
        dprob = dot_nt(dout, kv_v[:, HEAD_DIM:])
        dscore = (prob * (dprob - delta)).astype(low)
        dquery = dot_nn(dscore, kv_v[:, :HEAD_DIM]) * scale
        dpr_v[at, cols] = turned(dquery, at, -1.0).astype(low)
        dkv_v[:, :HEAD_DIM] += dot_tn(dscore, q_v[at, cols]) * scale
        dkv_v[:, HEAD_DIM:] += dot_tn(prob.astype(low), dout)
        return carry

    lax.fori_loop(0, row_blocks * (heads // HEAD_DIM), attend_back, 0)
    mine = rows_at(here.fs * toks, toks)
    dkv_v[mine, :] += kv_grad[...].astype(f32)

    def dkv_rows(step, carry):
        at = rows_at(step * width, width)
        dpr_v[at, pl.ds(heads, HEAD_DIM)] = turned(dkv_v[at, :HEAD_DIM], at, -1.0).astype(low)
        dpr_v[at, pl.ds(heads + HEAD_DIM, HEAD_DIM)] = dkv_v[at, HEAD_DIM:].astype(low)
        return carry

    lax.fori_loop(0, row_blocks, dkv_rows, 0)
    dn1_v = s2_v

    def dn1_tile(n, carry):
        cols = pl.ds(pl.multiple_of(n * width, width), width)
        dn1_v[qkv_rows, cols] = dot_nt(dpr_v[qkv_rows, qkv_cols], wa[cols, qkv_cols]).astype(low)
        return carry

    for done in s2s.sent:
        done()
    lax.fori_loop(0, MODEL // width, dn1_tile, 0)

    def grad_qkv_tile(n, carry):
        cols = pl.ds(pl.multiple_of(n * width, width), width)
        wa[cols, qkv_cols] = dot_tn(tok_v[:, cols], dpr_v[qkv_rows, qkv_cols]).astype(low)
        return carry

    lax.fori_loop(0, MODEL // width, grad_qkv_tile, 0)
    attn_send_y(1, qkv_cols)
    across, across_sent = reduce_sequence(dn1_v)

    f_across(f_order[0])
    for k in reversed(range(1, zs - 2)):
        o_chain.onward(0, k)
        o_chain.onward(1, k)
    a_first(0, out_cols)
    for k in reversed(range(1, zs - 1)):
        a_onward(0, k)
    f_out(f_order[1])
    f_across(f_order[2])
    a_first(1, qkv_cols)
    for k in reversed(range(1, zs - 1)):
        a_onward(1, k)
    f_out(f_order[0])
    for step in f_order[3:]:
        f_across(step)
    f_out(f_order[2])
    attn_chains[0].last()
    attn_chains[1].last()
    attn_f = {}
    for step in range(fsdp):
        other = shifted(here.fs, step, fsdp)
        source = wa.at[rows_at((here.dp * fsdp + other) * rows, rows)]
        target = out_a.at[here.fs]
        if step:
            slot = attn_f[step] = wires.slot()
            wires.start(slot, source, target, (here.dp, other))
        else:
            keep(source, target)
    for step in f_order[3:]:
        f_out(step)
    o_chain.last()

    def mixed_rows(at, first):
        mixed[at, :] = (mid_v[at, :] + so_v[at16(z * toks + first), :].astype(f32)).astype(low)

    each_rows(toks, mixed_rows)
    sequence_arrive(across)

    def input_rows(at, first):
        ds1 = sequence_total(first)
        values = tokens[at, :].astype(f32)
        inverse = lax.rsqrt(jnp.mean(values * values, axis=1, keepdims=True) + EPSILON)
        s1 = values * inverse
        back = inverse * (ds1 - s1 * jnp.mean(ds1 * s1, axis=1, keepdims=True))
        input_grad[at, :] = (input_grad[at, :].astype(f32) + back).astype(low)

    for done in dbr_sent:
        done()
    each_rows(toks, input_rows)
    for step in range(1, fsdp):
        other = shifted(here.fs, -step, fsdp)
        wires.arrive(attn_f[step], out_a.at[other], (here.dp, other))
    for step in range(zs):
        from_z = shifted(z, -step, zs)
        for core in range(2):
            if step or core:
                from_c = lax.rem(c + core, 2)
                wires.arrive(
                    ffn_z[step, core],
                    out_f.at[from_z * 2 + from_c],
                    here.device(z=from_z, c=from_c),
                )
    for copy in locals_[first_local + 1 :]:
        copy.wait()
    for chain in [d_chain, o_chain] + attn_chains:
        chain.drain()
    wires.drain()


def whole_block(place, w_qkv, w_out, w_gateup, w_down, tokens, dy, kv_grad, rope, key_at):
    toks = tokens.shape[0]
    zs, ys, xs, fsdp, rows = place.zs, place.ys, place.xs, place.fsdp, place.rows
    heads = place.heads
    seq = toks * fsdp
    every = zs * 2 * toks
    slab = fsdp * rows
    low, f32 = jnp.bfloat16, jnp.float32
    count = place.copies
    vmem = pl.BlockSpec(memory_space=pltpu.VMEM)
    hbm = pl.BlockSpec(memory_space=ANY)
    return pl.pallas_call(
        functools.partial(block_kernel, place),
        out_shape=(
            jax.ShapeDtypeStruct((toks, MODEL), low),
            jax.ShapeDtypeStruct((toks, KV), low),
            jax.ShapeDtypeStruct((toks, MODEL), low),
            jax.ShapeDtypeStruct((2 * zs, rows, place.ffn_width), low),
            jax.ShapeDtypeStruct((fsdp, rows, place.attn_width), low),
        ),
        in_specs=[hbm] * 4 + [vmem, hbm] + [vmem] * 3,
        out_specs=(vmem, vmem, vmem, hbm, hbm),
        scratch_shapes=[
            pltpu.VMEM((MODEL, place.attn_width), low),
            pltpu.VMEM((MODEL, place.ffn_width), low),
            pltpu.VMEM((seq, MODEL), low),
            pltpu.VMEM((every, MODEL), low),
            pltpu.VMEM((every, MODEL), low),
            pltpu.VMEM((every, place.block), low),
            pltpu.VMEM((every, 2 * place.block), low),
            pltpu.VMEM((seq, MODEL), low),
            pltpu.VMEM((xs * toks, MODEL), low),
            pltpu.VMEM((xs * toks, MODEL), low),
            pltpu.VMEM((toks, MODEL), f32),
            pltpu.VMEM((toks, LANES), f32),
            pltpu.VMEM((zs * toks, MODEL), low),
            pltpu.VMEM((zs * toks, MODEL), low),
            pltpu.VMEM((2 * (zs - 1) * toks, MODEL), low),
            pltpu.VMEM((seq, heads), low),
            pltpu.VMEM((seq, KV), low),
            pltpu.VMEM((seq, heads), low),
            pltpu.VMEM((seq, KV), f32),
            pltpu.VMEM(((xs - 1) * ((zs - 1) * ys + 1) * 2 * rows, place.ffn_width), low),
            pltpu.VMEM(((ys - 1) * (zs - 1 + xs) * 2 * rows, place.ffn_width), low),
            pltpu.VMEM(((ys - 1) * zs * slab, place.attn_width), low),
            pltpu.VMEM((2 * (zs - 1) * slab, place.attn_width), low),
            pltpu.SemaphoreType.DMA((16,)),
            pltpu.SemaphoreType.DMA((count,)),
            pltpu.SemaphoreType.DMA((count,)),
            pltpu.SemaphoreType.REGULAR((2,)),
        ],
        compiler_params=pltpu.CompilerParams(
            collective_id=0, has_side_effects=True, vmem_limit_bytes=63 * 2**20 + 2**19
        ),
        name="whole_block",
    )(w_qkv, w_out, w_gateup, w_down, tokens, dy, kv_grad, rope, key_at)


def on_device(
    place, tokens, lengths, gain_attn, w_qkv, w_out, gain_ffn, w_gateup, w_down, out_grad, kv_grad
):
    toks = tokens.shape[0]
    fsdp = place.fsdp
    seq = toks * fsdp
    low = jnp.bfloat16
    f32 = jnp.float32
    group = lax.axis_index("dp")
    length = jnp.sum(
        jnp.where(jnp.arange(lengths.shape[0], dtype=jnp.int32) == group, lengths, 0)
    )
    slots = np.arange(seq)
    at = slots % toks * fsdp + slots // toks
    frequency = THETA ** (-np.arange(HEAD_DIM // 2, dtype=np.float64) * (2.0 / HEAD_DIM))
    angles = at[:, None] * frequency[None, :]
    rope = jnp.asarray(np.concatenate([np.cos(angles), np.sin(angles)], axis=1), f32)
    positions = jnp.asarray(np.broadcast_to(at, (8, seq)), jnp.int32)
    key_at = jnp.where(positions < length, positions, seq)

    gain_a = gain_attn.astype(f32)[:, None]
    gain_f = gain_ffn.astype(f32)[:, None]
    folded_qkv = (w_qkv.astype(f32) * gain_a).astype(low)
    folded_gateup = (w_gateup.astype(f32) * gain_f).astype(low)
    mixed, shared_kv, input_grad, out_f, out_a = whole_block(
        place, folded_qkv, w_out, folded_gateup, w_down, tokens, out_grad, kv_grad,
        rope, key_at,
    )

    heads, block = place.heads, place.block
    duplicate = 2 * block - place.zone
    out_f = out_f.astype(f32)
    out_a = out_a.astype(f32)

    def columns(start):
        pieces = []
        for z_at in range(place.zs):
            pieces.append(out_f[2 * z_at, :, start : start + block])
            pieces.append(out_f[2 * z_at + 1, :, start + duplicate : start + block])
        return pieces

    plain_gateup = jnp.concatenate(columns(0) + columns(block), axis=1)
    grad_down = jnp.concatenate(columns(2 * block), axis=1)
    plain_qkv = jnp.concatenate(
        [out_a[at, :, :heads] for at in range(fsdp)]
        + [jnp.sum(out_a[:, :, heads : heads + KV], axis=0)],
        axis=1,
    )
    grad_out = jnp.concatenate([out_a[at, :, heads + KV :] for at in range(fsdp)], axis=1)
    grad_gain_attn = jnp.sum(w_qkv.astype(f32) * plain_qkv, axis=1)
    grad_gain_ffn = jnp.sum(w_gateup.astype(f32) * plain_gateup, axis=1)
    return (
        mixed,
        shared_kv,
        input_grad,
        grad_gain_attn,
        plain_qkv * gain_a,
        grad_out,
        grad_gain_ffn,
        plain_gateup * gain_f,
        grad_down,
    )


def solution(mesh):
    place = Place(mesh.shape["dp"], mesh.shape["fsdp"])
    row = P(("dp", "fsdp"), None)
    line = P(("dp", "fsdp"))
    return jax.shard_map(
        functools.partial(on_device, place),
        mesh=mesh,
        in_specs=(row, P(), line, row, row, line, row, row, row, row),
        out_specs=(row, row, row, line, row, row, line, row, row),
        check_vma=False,
    )
```
